32 devices in a mesh: dp: 8 (over z, y), head: 4 (over x, core).
Axes of the slice: x: 2, y: 2, z: 4, core: 2. Of those that a mesh axis runs over, the one named last changes fastest.
Arguments:
- hidden_in: bfloat16 [8192, 768], P(('dp', 'head')), may hold values from -6 to 6
- w_query: bfloat16 [2, 768, 768], P(None, None, 'head'), may hold values from -0.21875 to 0.21875
- w_key: bfloat16 [2, 768, 768], P(None, None, 'head'), may hold values from -0.21875 to 0.21875
- w_value: bfloat16 [2, 768, 768], P(None, None, 'head'), may hold values from -0.21875 to 0.21875
- b_query: float32 [2, 768], P(None, 'head'), may hold values from -3 to 3
- b_value: float32 [2, 768], P(None, 'head'), may hold values from -3 to 3
- w_out: bfloat16 [2, 768, 768], P(None, 'head'), may hold values from -1.75 to 1.75
- b_out: float32 [2, 768], replicated, may hold values from -2 to 2
- ln1_gain: float32 [2, 768], replicated, may hold values from 0.5 to 1.5
- ln1_bias: float32 [2, 768], replicated, may hold values from -2 to 2
- w_up: bfloat16 [2, 768, 3072], P(None, None, 'head'), may hold values from -0.21875 to 0.21875
- b_up: float32 [2, 3072], P(None, 'head'), may hold values from -3 to 3
- w_down: bfloat16 [2, 3072, 768], P(None, 'head'), may hold values from -0.109375 to 0.109375
- b_down: float32 [2, 768], replicated, may hold values from -2 to 2
- ln2_gain: float32 [2, 768], replicated, may hold values from 0.5 to 1.5
- ln2_bias: float32 [2, 768], replicated, may hold values from -2 to 2
- token_mask: int32 [8192], P('dp'), may hold values from 0 to 1, as said below
- query_order: int32 [2, 12, 8192], P(None, 'head', 'dp'), may hold values from 0 to 1023, as said below
- key_order: int32 [2, 12, 8192], P(None, 'head', 'dp'), may hold values from 0 to 1023, as said below
- out_cotangent: float32 [8192, 768], P(('dp', 'head')), may hold values from -6 to 6
Outputs:
- hidden_out: float32 [8192, 768], P(('dp', 'head'))
- hidden_in_grad: float32 [8192, 768], P(('dp', 'head'))
- w_query_grad: float32 [2, 768, 768], P(None, 'dp', 'head')
- w_key_grad: float32 [2, 768, 768], P(None, 'dp', 'head')
- w_value_grad: float32 [2, 768, 768], P(None, 'dp', 'head')
- b_query_grad: float32 [2, 768], replicated
- b_value_grad: float32 [2, 768], replicated
- w_out_grad: float32 [2, 768, 768], P(None, 'head', 'dp')
- b_out_grad: float32 [2, 768], replicated
- ln1_gain_grad: float32 [2, 768], replicated
- ln1_bias_grad: float32 [2, 768], replicated
- w_up_grad: float32 [2, 768, 3072], P(None, 'dp', 'head')
- b_up_grad: float32 [2, 3072], replicated
- w_down_grad: float32 [2, 3072, 768], P(None, 'head', 'dp')
- b_down_grad: float32 [2, 768], replicated
- ln2_gain_grad: float32 [2, 768], replicated
- ln2_bias_grad: float32 [2, 768], replicated
The draws below stay inside these ranges and needn't reach their ends.
Inputs may be any that keep to these rules, and one draw needn't show every extreme that they name: `token_mask`: 1s then 0s within each aligned block of 128 tokens; zeros stand only in a document's last block, at most 127 of them. Documents are runs of whole blocks inside one pack of 1024 tokens (8 blocks), at most 8 blocks each; in every draw at least one document fills a whole pack. `query_order`: for each layer and head, each aligned run of 1024 entries is a permutation of 0 to 1024 - 1 (positions in that pack) that maps each document's positions onto themselves; the documents are those of token_mask. `key_order`: as query_order, drawn independently, with the same documents.
All inputs are finite; a program needn't handle non-finite values.
Results may differ from the reference program's by a relative error of at most 0.038.
Values may be sent and summed in bfloat16 or wider, within the bound.
No kernel may reach another device: no remote copies, remote signals or barrier semaphores. Data moves between devices by JAX's collectives and lax.ppermute only.
A program may use at most 128 MiB of HBM per device.

```python
import math
import jax
import jax.numpy as jnp
from jax import lax

D = 768
HEADS = 12
FF = 3072
HEAD_DIM = 64
CLUSTER = 128
LONG_BLOCKS = 16
LAYERS = 2
TOK_DEV = 1024
TOKENS = 8192
N_HEAD = 4


def doc_layout(key):
    blocks = TOKENS // CLUSTER
    per_pack = TOK_DEV // CLUSTER
    longest = min(LONG_BLOCKS, per_pack)
    place = jnp.arange(blocks, dtype=jnp.int32)
    local = place % per_pack
    coin = jax.random.randint(jax.random.fold_in(key, 101), (blocks,), 0, 3) == 0
    forced = local % LONG_BLOCKS == 0
    starts = jnp.where(place < longest, forced, coin | forced).astype(jnp.int32)
    doc_id = jnp.cumsum(starts) - 1
    last = jnp.concatenate([starts[1:], jnp.ones((1,), jnp.int32)]) == 1
    return (doc_id, last)


def order_draw(key, doc_id):
    packs = TOKENS // TOK_DEV
    token_doc = jnp.repeat(doc_id, CLUSTER).reshape(packs, TOK_DEV)
    local_doc = token_doc - token_doc[:, :1]
    keys = jax.random.split(key, LAYERS * HEADS * packs)
    ties = jax.vmap(lambda single: jax.random.permutation(single, TOK_DEV))(keys)
    ties = ties.reshape(LAYERS, HEADS, packs, TOK_DEV).astype(jnp.int32)
    score = local_doc[None, None, :, :] * TOK_DEV + ties
    order = jnp.argsort(score, axis=-1, stable=True).astype(jnp.int32)
    return order.reshape(LAYERS, HEADS, TOKENS)


def draw_token_mask(key, part):
    doc_id, last = doc_layout(key)
    key = jax.random.fold_in(key, 1)
    blocks = TOKENS // CLUSTER
    pad = jax.random.randint(key, (blocks,), 0, CLUSTER)
    offset = jnp.arange(CLUSTER, dtype=jnp.int32)
    keep = jnp.logical_or(jnp.logical_not(last)[:, None], offset[None, :] < (CLUSTER - pad)[:, None])
    return keep.astype(jnp.int32).reshape(TOKENS)


def draw_query_order(key, part):
    doc_id, last = doc_layout(key)
    key = jax.random.fold_in(key, 2)
    return order_draw(key, doc_id)


def draw_key_order(key, part):
    doc_id, last = doc_layout(key)
    key = jax.random.fold_in(key, 3)
    return order_draw(key, doc_id)


def block_scale(own_key, shape, cuts, low, high):
    loudness, own = 1.0, jax.random.fold_in(own_key, 6)
    for axis_at, blocks in cuts:
        steps = jnp.exp(jax.random.uniform(jax.random.fold_in(own, axis_at), (blocks,), jnp.float32, low / len(cuts), high / len(cuts)))
        loudness = loudness * jnp.repeat(steps, shape[axis_at] // blocks).reshape([-1 if axis == axis_at else 1 for axis in range(len(shape))])
    return loudness


def scatter_about(stream_key, extent, scale, bound, pieces=(), kind=jnp.bfloat16):
    entries = scale * jax.random.normal(stream_key, extent, jnp.float32)
    if pieces:
        entries = entries * block_scale(stream_key, extent, pieces, -0.22, 0.18)
    return jnp.clip(entries, -bound, bound).astype(kind)


def setup_inputs(seed: int = 0) -> dict:
    key_of = jax.random.split(jax.random.key(seed), 21)
    return {
        "hidden_in": scatter_about(key_of[0], (TOKENS, D), 1.0, 6.0, ((0, 32),)),
        "w_query": scatter_about(key_of[1], (LAYERS, D, D), D ** -0.5, 0.21875, ((2, 4),)),
        "w_key": scatter_about(key_of[2], (LAYERS, D, D), D ** -0.5, 0.21875, ((2, 4),)),
        "w_value": scatter_about(key_of[3], (LAYERS, D, D), D ** -0.5, 0.21875, ((2, 4),)),
        "b_query": scatter_about(key_of[4], (LAYERS, D), 0.5, 3.0, ((1, 4),), jnp.float32),
        "b_value": scatter_about(key_of[5], (LAYERS, D), 0.5, 3.0, ((1, 4),), jnp.float32),
        "w_out": scatter_about(key_of[6], (LAYERS, D, D), (D // 64) ** -0.5, 1.75, ((1, 4),)),
        "b_out": scatter_about(key_of[7], (LAYERS, D), 0.3, 2.0, (), jnp.float32),
        "ln1_gain": jnp.clip(1.0 + 0.1 * jax.random.normal(key_of[8], (LAYERS, D), jnp.float32), 0.5, 1.5),
        "ln1_bias": scatter_about(key_of[9], (LAYERS, D), 0.3, 2.0, (), jnp.float32),
        "w_up": scatter_about(key_of[10], (LAYERS, D, FF), D ** -0.5, 0.21875, ((2, 4),)),
        "b_up": scatter_about(key_of[11], (LAYERS, FF), 0.5, 3.0, ((1, 4),), jnp.float32),
        "w_down": scatter_about(key_of[12], (LAYERS, FF, D), FF ** -0.5, 0.109375, ((1, 4),)),
        "b_down": scatter_about(key_of[13], (LAYERS, D), 0.3, 2.0, (), jnp.float32),
        "ln2_gain": jnp.clip(1.0 + 0.1 * jax.random.normal(key_of[14], (LAYERS, D), jnp.float32), 0.5, 1.5),
        "ln2_bias": scatter_about(key_of[15], (LAYERS, D), 0.3, 2.0, (), jnp.float32),
        "token_mask": draw_token_mask(jax.random.fold_in(key_of[20], 71), 0),
        "query_order": draw_query_order(jax.random.fold_in(key_of[20], 71), 0),
        "key_order": draw_key_order(jax.random.fold_in(key_of[20], 71), 0),
        "out_cotangent": scatter_about(key_of[19], (TOKENS, D), 1.0, 6.0, ((0, 32),), jnp.float32),
    }


EPS = 1e-12
NEG = -1e+30

@jax.custom_vjp
def low(v):
    return lax.optimization_barrier(v.astype(jnp.bfloat16)).astype(jnp.float32)

@jax.custom_vjp
def low_back(v):
    return v

def low_keep(v):
    return (low(v), None)

def low_pass(kept, grad):
    return (grad,)

def back_keep(v):
    return (v, None)

def back_low(kept, grad):
    return (low(grad),)
low.defvjp(low_keep, low_pass)
low_back.defvjp(back_keep, back_low)

def dense(left, right):
    return jnp.dot(left, right, precision=lax.Precision.HIGHEST)

def layer_norm(rows, gain, shift):
    centre = rows - lax.optimization_barrier(jnp.mean(rows, axis=-1, keepdims=True))
    spread = lax.optimization_barrier(jnp.mean(centre * centre, axis=-1, keepdims=True))
    return centre * lax.rsqrt(spread + EPS) * gain + shift

def gelu_exact(values):
    return jax.nn.gelu(values, approximate=False)

def inverse_order(order):
    places = jnp.broadcast_to(jnp.arange(order.shape[1], dtype=jnp.int32), order.shape)
    lines = jnp.broadcast_to(jnp.arange(order.shape[0], dtype=jnp.int32)[:, None], order.shape)
    return jnp.zeros_like(order).at[lines, order].set(places)

def cluster_mix(query, key, value, q_order, k_order, mask):
    length, width = query.shape
    heads = q_order.shape[0]
    hdim = width // heads

    def arrange(matrix, order):
        split = matrix.reshape(length, heads, hdim).transpose(1, 0, 2)
        picked = jnp.take_along_axis(split, order[:, :, None], axis=1)
        return picked.reshape(heads, length // CLUSTER, CLUSTER, hdim)
    q_perm = arrange(query, q_order)
    k_perm = arrange(key, k_order)
    v_perm = arrange(value, k_order)
    live = (jnp.take(mask, k_order, axis=0) > 0).reshape(heads, length // CLUSTER, 1, CLUSTER)
    scores = jnp.einsum('hcqd,hckd->hcqk', q_perm, k_perm, precision=lax.Precision.HIGHEST) * (1.0 / math.sqrt(hdim))
    scores = low_back(jnp.where(live, scores, NEG))
    top = lax.optimization_barrier(jnp.max(scores, axis=-1, keepdims=True))
    raised = jnp.exp(scores - top)
    probs = low(raised / lax.optimization_barrier(jnp.sum(raised, axis=-1, keepdims=True)))
    mixed = jnp.einsum('hcqk,hckd->hcqd', probs, v_perm, precision=lax.Precision.HIGHEST)
    mixed = mixed.reshape(heads, length, hdim)
    placed = jnp.take_along_axis(mixed, inverse_order(q_order)[:, :, None], axis=1)
    return placed.transpose(1, 0, 2).reshape(length, width)

def one_layer(rows, weights, mask, q_order, k_order):
    w_q, w_k, w_v, b_q, b_v, w_o, b_o, g_one, n_one, w_u, b_u, w_d, b_d, g_two, n_two = weights
    per_group = HEADS // N_HEAD
    width = per_group * HEAD_DIM
    units = FF // N_HEAD
    rows_low = low(rows)
    attended = jnp.zeros_like(rows)
    for group in range(N_HEAD):
        cols = slice(group * width, (group + 1) * width)
        chosen = slice(group * per_group, (group + 1) * per_group)
        copied = low_back(rows_low)
        query = low(low_back(dense(copied, w_q[:, cols]) + b_q[cols]))
        key = low(low_back(dense(copied, w_k[:, cols])))
        value = low(low_back(dense(copied, w_v[:, cols]) + b_v[cols]))
        mixed = low(low_back(cluster_mix(query, key, value, q_order[chosen], k_order[chosen], mask)))
        attended = attended + low(dense(mixed, w_o[cols, :]))
    attended = low_back(attended)
    normed = layer_norm(rows + attended + b_o, g_one, n_one)
    normed_low = low(normed)
    fed = jnp.zeros_like(rows)
    for group in range(N_HEAD):
        cols = slice(group * units, (group + 1) * units)
        copied = low_back(normed_low)
        hidden_pre = low_back(dense(copied, w_u[:, cols]) + b_u[cols])
        active = low(gelu_exact(hidden_pre))
        fed = fed + low(dense(active, w_d[cols, :]))
    fed = low_back(fed)
    return layer_norm(normed + fed + b_d, g_two, n_two)

def pack_forward(rows, params, mask, q_orders, k_orders):
    for layer in range(LAYERS):
        weights = tuple((item[layer] for item in params))
        rows = one_layer(rows, weights, mask, q_orders[layer], k_orders[layer])
    return rows

def reference(hidden_in, w_query, w_key, w_value, b_query, b_value, w_out, b_out, ln1_gain, ln1_bias, w_up, b_up, w_down, b_down, ln2_gain, ln2_bias, token_mask, query_order, key_order, out_cotangent):
    params = tuple((item.astype(jnp.float32) for item in (w_query, w_key, w_value, b_query, b_value, w_out, b_out, ln1_gain, ln1_bias, w_up, b_up, w_down, b_down, ln2_gain, ln2_bias)))
    packs = TOKENS // TOK_DEV
    inputs = hidden_in.astype(jnp.float32).reshape(packs, TOK_DEV, D)
    masks = token_mask.reshape(packs, TOK_DEV)
    q_orders = query_order.reshape(LAYERS, HEADS, packs, TOK_DEV).transpose(2, 0, 1, 3)
    k_orders = key_order.reshape(LAYERS, HEADS, packs, TOK_DEV).transpose(2, 0, 1, 3)
    cotangents = out_cotangent.astype(jnp.float32).reshape(packs, TOK_DEV, D)
    zeros = tuple((jnp.zeros_like(item) for item in params))

    def step(totals, item):
        rows, mask, q_ord, k_ord, cotangent = item

        def forward(values, weights):
            return pack_forward(values, weights, mask, q_ord, k_ord)
        result, pull = jax.vjp(forward, rows, params)
        d_rows, d_params = pull(cotangent)
        return (tuple((total + grad for total, grad in zip(totals, d_params))), (result, d_rows))
    totals, (results, d_inputs) = lax.scan(step, zeros, (inputs, masks, q_orders, k_orders, cotangents))
    return (results.reshape(TOKENS, D), d_inputs.reshape(TOKENS, D), totals[0], totals[1], totals[2], totals[3], totals[4], totals[5], totals[6], totals[7], totals[8], totals[9], totals[10], totals[11], totals[12], totals[13], totals[14])
```

```python
import functools
import math

import jax
import jax.numpy as jnp
from jax import lax
from jax.experimental import pallas as pl
from jax.experimental.pallas import tpu as pltpu
from jax.sharding import PartitionSpec as P

CLUSTER = 128
HEAD_DIM = 64
EPS = 1e-12
NEG = -1e30
MIB = 1024 * 1024
GIGA = {"attend_back_near": 3}

f32 = jnp.float32
bf16 = jnp.bfloat16


def swap(array, axis, bit):
    size = lax.axis_size(axis)
    return lax.ppermute(array, axis, [(item, item ^ bit) for item in range(size)])


def tie(value, *earlier):
    return lax.optimization_barrier((value, earlier))[0]


class Transfer:
    def __init__(self, send, bit):
        self.got = swap(send, "dp", 1 << bit)


class Halving:
    def __init__(self, keeps, sends, orders):
        self.keeps, self.orders = list(keeps), [list(order) for order in orders]
        self.slots = [(Transfer(send, order.pop(0)), 0) for send, order in zip(sends, self.orders)]

    def more(self):
        return bool(self.orders[0])


def transfers_of(items):
    found = []
    for item in items:
        for transfer, _ in item.slots:
            if transfer not in found:
                found.append(transfer)
    return found


def spots_of(items):
    found = transfers_of(items)
    return [
        (found.index(transfer), start, keep.shape[2])
        for item in items
        for keep, (transfer, start) in zip(item.keeps, item.slots)
    ]


def join(value, items, *earlier):
    return land(value, transfers_of(items), *earlier)


def land(value, found, *earlier):
    value, gots, _ = lax.optimization_barrier((value, [item.got for item in found], earlier))
    for item, got in zip(found, gots):
        item.got = got
    return value


def advance(items, pair, *earlier, apart=False):
    items = [item for item in items if item.more()]
    found = transfers_of(items)
    keeps = [keep for item in items for keep in item.keeps]
    keeps, gots, pair = tie((keeps, [item.got for item in found], pair), *earlier)
    outs = [((keep.shape[0] // 2,) + keep.shape[1:], bf16) for keep in keeps]
    groups = {}
    bits = [order.pop(0) for item in items for order in item.orders]
    for spot, (bit, out) in enumerate(zip(bits, outs)):
        groups.setdefault((bit, out[0][0], spot if apart else 0), []).append(spot)
    sends = []
    for group in groups.values():
        cols = sum(outs[spot][0][2] for spot in group)
        sends.append((outs[group[0]][0][:2] + (cols,), bf16))
    parts = call(
        functools.partial(halve_kernel, spots_of(items), list(groups.values()), len(gots)), "halve",
        [*keeps, *gots, *pair], outs + sends + [(part.shape, f32) for part in pair[:1]], vmem=8,
    )
    slots = [None] * len(keeps)
    for (bit, *_), group, send in zip(groups, groups.values(), parts[len(keeps) :]):
        transfer, start = Transfer(send, bit), 0
        for spot in group:
            slots[spot] = (transfer, start)
            start += outs[spot][0][2]
    start = 0
    for item in items:
        stop = start + len(item.keeps)
        item.keeps, item.slots = parts[start:stop], slots[start:stop]
        start = stop
    return parts


def dot(left, right):
    return jnp.dot(left, right, preferred_element_type=f32)


def dot_nt(left, right):
    return lax.dot_general(left, right, (((1,), (1,)), ((), ())), preferred_element_type=f32)


def dot_tn(left, right):
    return lax.dot_general(left, right, (((0,), (0,)), ((), ())), preferred_element_type=f32)


def row(ref, layer):
    return ref[layer : layer + 1, :]


def normalise(rows):
    centre = rows - jnp.mean(rows, axis=-1, keepdims=True)
    spread = jnp.mean(centre * centre, axis=-1, keepdims=True)
    scale = lax.rsqrt(spread + EPS)
    return centre * scale, scale


def normalise_back(grad, gain, normed, scale):
    part = grad * gain
    mean_one = jnp.mean(part, axis=-1, keepdims=True)
    mean_two = jnp.mean(part * normed, axis=-1, keepdims=True)
    return (part - mean_one - normed * mean_two) * scale


def store_sums(ref, *arrays):
    rows = [jnp.sum(item, axis=0, keepdims=True) for item in arrays]
    rows.append(jnp.zeros((ref.shape[0] - len(rows), ref.shape[1]), f32))
    ref[...] = jnp.concatenate(rows, axis=0)


def gelu_pair(values):
    bell = jnp.exp(values * values * -0.5)
    t = 1.0 / (1.0 + (0.3275911 * math.sqrt(0.5)) * jnp.abs(values))
    poly = 0.5 * 1.061405429
    for factor in (-1.453152027, 1.421413741, -0.284496736, 0.254829592):
        poly = poly * t + 0.5 * factor
    tail = poly * t * bell
    cdf = jnp.where(values >= 0.0, 1.0 - tail, tail)
    return values * cdf, cdf + values * bell * (1.0 / math.sqrt(2.0 * math.pi))


def stack_rows(refs):
    return jnp.concatenate([ref[...] for ref in refs], axis=0)


def head_cols(array, head):
    return array[:, head * HEAD_DIM : (head + 1) * HEAD_DIM]


def lanes_of(rows):
    return lax.broadcasted_iota(jnp.int32, (rows, 2 * HEAD_DIM), 1)


class Viewed:
    def __init__(self, source, pieces):
        self.source, self.shape, self.size = source, source.shape, source.shape[0] // pieces

    def piece(self, item):
        return self.source[item * self.size : (item + 1) * self.size]

    def __getitem__(self, index):
        return self.source[index]


def cluster_kernel(layer, spot, q_order, k_order, live, wq, wk, wv, q_marks, k_marks, weights, held, sems):
    heads, length, width = q_marks.shape
    copies = [
        pltpu.make_async_copy(source.at[layer], held.at[item], sems.at[item])
        for item, source in enumerate((wq, wk, wv))
    ]
    for copy in copies:
        copy.start()
    count = length // CLUSTER
    lines = lax.broadcasted_iota(jnp.int32, (length, length), 0)
    spread_line = lax.broadcasted_iota(jnp.int32, (length, width), 0) // CLUSTER + HEAD_DIM
    lanes = lanes_of(length)
    spread = jnp.where(spread_line == lanes, 1.0, 0.0).astype(bf16)
    in_use = jnp.logical_and(lanes >= HEAD_DIM, lanes < HEAD_DIM + count)
    for head in range(heads):
        order = q_order[head, layer : layer + 1, :] ^ spot[0]
        hot = jnp.where(order == lines, 1.0, 0.0).astype(bf16)
        q_marks[head] = dot(hot, spread).astype(bf16)
        order = k_order[head, layer : layer + 1, :] ^ spot[0]
        hot = jnp.where(order == lines, 1.0, 0.0).astype(bf16)
        inside = dot(hot, spread) * live[...]
        outside = jnp.where(in_use, jnp.where(inside > 0.5, 0.0, NEG), 0.0)
        k_marks[head] = outside.astype(bf16)
    for copy in copies:
        copy.wait()
    blank = jnp.zeros((HEAD_DIM, held.shape[2]), bf16)
    for head in range(heads):
        part = slice(head * HEAD_DIM, (head + 1) * HEAD_DIM)
        weights[head] = jnp.concatenate([held[0, part], blank, held[1, part], held[2, part]], axis=0)


def attend_rows(first, rows, q_ref, kv_ref, k_marks, raised_kept, out_kept):
    heads, length, width = kv_ref.shape
    chunk = rows
    left = lanes_of(length) < HEAD_DIM
    mixed = []
    for head in range(heads):
        keys = kv_ref[head].astype(f32)
        marked = jnp.where(left, keys, k_marks[head].astype(f32)).astype(bf16)
        values = jnp.where(left, 1.0, keys).astype(bf16)
        outs = []
        for start in range(0, rows, chunk):
            scores = dot_nt(q_ref[head, first + start : first + start + chunk], marked)
            raised = jnp.exp(scores - jnp.max(scores, axis=1, keepdims=True)).astype(bf16)
            raised_kept[head, pl.ds(start, chunk)] = raised
            total = dot(raised, values)
            share = 1.0 / total
            outs.append(jnp.where(left[:chunk], share, total * pltpu.roll(share, HEAD_DIM, 1)))
        outs = jnp.concatenate(outs, axis=0)
        out_kept[head] = outs
        mixed.append(outs[:, HEAD_DIM:])
    return jnp.concatenate(mixed, axis=1).astype(bf16)


def attend_kernel(
    layer, x0, x1, x2, x3, weights, bq, bv, q_marks, k_marks,
    q_out, kv_out, ob2, ob3, raised_kept, out_kept, ob_kept, x_kept,
):
    size = ob2.shape[0]
    for item, ref in enumerate((x0, x1, x2, x3)):
        x_kept[pl.ds(item * size, size)] = ref[...]
    x = stack_rows((x0, x1, x2, x3))
    heads = q_out.shape[0]
    blank_b = jnp.zeros((1, HEAD_DIM), f32)
    bias_q, bias_v = row(bq, layer), row(bv, layer)
    for head in range(heads):
        part = slice(head * HEAD_DIM, (head + 1) * HEAD_DIM)
        bias = jnp.concatenate([bias_q[:, part], blank_b, blank_b, bias_v[:, part]], axis=1)
        qkv = (dot_nt(x, weights[head]) + bias).astype(bf16)
        query = qkv[:, : 2 * HEAD_DIM].astype(f32) * (1.0 / math.sqrt(HEAD_DIM))
        q_out[head] = (query + q_marks[head].astype(f32)).astype(bf16)
        kv_out[head] = qkv[:, 2 * HEAD_DIM :]
    mixed = attend_rows(2 * size, 2 * size, q_out, kv_out, k_marks, raised_kept, out_kept)
    ob_kept[...] = mixed
    ob2[...] = mixed[:size]
    ob3[...] = mixed[size:]


def attend_near_kernel(
    q_in, kv_in, k_marks, ob0, ob1, raised_kept, out_kept, ob_kept, q_near, q_far, kv_kept
):
    size = ob0.shape[0]
    q_near[...] = q_in[:, : 2 * size]
    q_far[...] = q_in[:, 2 * size :]
    kv_kept[...] = kv_in[...]
    mixed = attend_rows(0, 2 * size, q_in, kv_in, k_marks, raised_kept, out_kept)
    ob_kept[...] = mixed
    ob0[...] = mixed[:size]
    ob1[...] = mixed[size:]


def entry_rows(layer, x, gain, shift):
    rows = x[...].astype(f32)
    if layer:
        rows = rows * row(gain, layer - 1) + row(shift, layer - 1)
    return rows


def with_scale(unit, scale):
    return jnp.concatenate([unit, jnp.broadcast_to(scale, (unit.shape[0], CLUSTER))], axis=1)


def mix_kernel(
    layer, ob0, ob1, ob2, ob3, w0, w1, w2, w3, x, b_out, gain1, shift1, gain2, shift2,
    normed, low, normed_kept, w_kept,
):
    total = entry_rows(layer, x, gain2, shift2) + row(b_out, layer)
    for item, (left, right) in enumerate(((ob0, w0), (ob1, w1), (ob2, w2), (ob3, w3))):
        w_kept[item] = right[...]
        total = total + dot(left[...], right[...])
    unit, root = normalise(total)
    normed[...] = unit
    normed_kept[...] = with_scale(unit, root)
    low[...] = (unit * row(gain1, layer) + row(shift1, layer)).astype(bf16)


def store_rows(value, refs):
    start = 0
    for ref in refs:
        ref[...] = value[start : start + ref.shape[0]].astype(ref.dtype)
        start += ref.shape[0]


def feed_kernel(layer, x, ups, biases, downs, x_kept, acts, slope, out):
    rows = x[...]
    x_kept[...] = rows
    total = 0.0
    units = acts[0].shape[1]
    for item in range(2):
        act, der = gelu_pair(dot(rows, ups[item][layer]) + row(biases[item], layer))
        act = act.astype(bf16)
        acts[item][...] = act
        slope[:, item * units : (item + 1) * units] = der.astype(bf16)
        total = total + dot(act, downs[item][layer])
    out[...] = total.astype(out.dtype)


def turn_weights_kernel(layer, ups, biases, downs, ups_t, biases_t, downs_t):
    for item in range(2):
        ups_t[item][...] = ups[item][layer].T
        downs_t[item][...] = downs[item][layer].T
        bias = row(biases[item], layer)
        biases_t[item][...] = jnp.broadcast_to(bias, (CLUSTER, bias.shape[1])).T


def feed_turned_kernel(x, ups_t, biases_t, downs_t, x_kept, acts, slope, out):
    rows = x[...]
    x_kept[...] = rows
    total = 0.0
    units, count = acts[0].shape
    for item in range(2):
        bias = jnp.concatenate([biases_t[item][...]] * (count // CLUSTER), axis=1)
        act, der = gelu_pair(dot_nt(ups_t[item][...], rows) + bias)
        act = act.astype(bf16)
        acts[item][...] = act
        slope[item * units : (item + 1) * units, :] = der.astype(bf16)
        total = total + dot(downs_t[item][...], act)
    out[...] = total.T.astype(out.dtype)


def second_rows(layer, normed1, gain1, shift1, own, far, b_down):
    rows = normed1[...] * row(gain1, layer) + row(shift1, layer)
    return rows + own[...] + far[...].astype(f32) + row(b_down, layer)


def close_kernel(
    layer, normed1, gain1, shift1, own, far, b_down, gain2, shift2, normed, low, normed_kept
):
    unit, root = normalise(
        second_rows(layer, normed1, gain1, shift1, own, far, b_down)
    )
    normed[...] = unit
    normed_kept[...] = with_scale(unit, root)
    low[...] = (unit * row(gain2, layer) + row(shift2, layer)).astype(bf16)


def turn_kernel(
    layer, normed1, gain1, shift1, own, far, b_down, gain2, shift2, grad,
    result, low, sums, d_second,
):
    unit, root = normalise(
        second_rows(layer, normed1, gain1, shift1, own, far, b_down)
    )
    gain = row(gain2, layer)
    result[...] = unit * gain + row(shift2, layer)
    back = normalise_back(grad[...], gain, unit, root)
    d_second[...] = back
    low[...] = back.astype(bf16)
    store_sums(sums, back, grad[...] * unit, grad[...])


def unit_and_scale(kept, width):
    both = kept[...]
    return both[:, :width], both[:, width : width + 1]


def open_back_kernel(layer, normed2, base, own, core, far, gain2, low, sums, d_second):
    rest = own[...] + core[...].astype(f32) + far[...].astype(f32)
    grad = base[...] + rest
    unit, root = unit_and_scale(normed2, grad.shape[1])
    back = normalise_back(grad, row(gain2, layer), unit, root)
    d_second[...] = back
    low[...] = back.astype(bf16)
    store_sums(sums, back, grad * unit, grad)


def feed_back_kernel(layer, grad, ups, downs, slope, pres, out):
    rows = grad[...]
    total = 0.0
    units = pres[0].shape[1]
    for item in range(2):
        der = slope[:, item * units : (item + 1) * units].astype(f32)
        pre = (dot_nt(rows, downs[item][layer]) * der).astype(bf16)
        pres[item][...] = pre
        total = total + dot_nt(pre, ups[item][layer])
    out[...] = total.astype(out.dtype)


def feed_back_turned_kernel(layer, grad, ups, downs, slope, pres, out):
    rows = grad[...]
    total = 0.0
    units = pres[0].shape[0]
    for item in range(2):
        der = slope[item * units : (item + 1) * units, :].astype(f32)
        pre = (dot_nt(downs[item][layer], rows) * der).astype(bf16)
        pres[item][...] = pre
        total = total + dot(ups[item][layer], pre)
    out[...] = total.T.astype(out.dtype)


def mix_back_kernel(
    layer, base, normed1, weights, own, far, gain1, low, d0, d1, d2, d3, sums, d_first
):
    grad = base[...] + own[...] + far[...].astype(f32)
    unit, root = unit_and_scale(normed1, grad.shape[1])
    back = normalise_back(grad, row(gain1, layer), unit, root)
    d_first[...] = back
    small = back.astype(bf16)
    low[...] = small
    for item, out in enumerate((d0, d1, d2, d3)):
        out[...] = dot_nt(small, weights.piece(item)[0]).astype(bf16)
    store_sums(sums, back, grad * unit, grad)


def attend_back_rows(refs, q_kept, kv_kept, out_kept, raised_kept):
    d_mixed = stack_rows(refs)
    rows = d_mixed.shape[0]
    heads, length, width = kv_kept.shape
    chunk = rows
    steps = rows // chunk
    key_lanes, lanes = lanes_of(length), lanes_of(rows)[:, :HEAD_DIM]
    d_q, d_k, d_v = [], [], []
    for head in range(heads):
        part = slice(head * HEAD_DIM, (head + 1) * HEAD_DIM)
        keys = kv_kept.piece(head)[0]
        both = out_kept.piece(head)[0]
        share, out = both[:, :HEAD_DIM], both[:, HEAD_DIM:]
        grad = (d_mixed[:, part].astype(f32) * share).astype(bf16).astype(f32)
        inner = jnp.sum(grad * out, axis=1, keepdims=True)
        high = inner.astype(bf16).astype(f32)
        middle = (inner - high).astype(bf16).astype(f32)
        low = inner - high - middle
        terms = jnp.where(
            lanes == 0, -high, jnp.where(lanes == 1, -middle, jnp.where(lanes == 2, -low, 0.0))
        )
        grad = jnp.concatenate([terms, grad], axis=1).astype(bf16)
        values = jnp.where(
            key_lanes < 3, 1.0, jnp.where(key_lanes < HEAD_DIM, 0.0, keys.astype(f32))
        ).astype(bf16)
        d_score, raised = [], []
        for item in range(steps):
            d_prob = dot_nt(grad[item * chunk : (item + 1) * chunk], values)
            raised.append(raised_kept.piece(head * steps + item))
            d_score.append((raised[-1].astype(f32) * d_prob).astype(bf16))
        d_score = jnp.concatenate(d_score, axis=0)
        raised = jnp.concatenate(raised, axis=0)
        query = q_kept.piece(head)[0]
        d_q.append(dot(d_score, keys)[:, :HEAD_DIM] * (1.0 / math.sqrt(HEAD_DIM)))
        d_k.append(dot(query.T[:HEAD_DIM], d_score))
        d_v.append(dot(grad.T[HEAD_DIM:], raised))
    return (
        jnp.concatenate(d_q, axis=1).astype(bf16),
        jnp.concatenate(d_k, axis=0),
        jnp.concatenate(d_v, axis=0),
    )


def attend_back_near_kernel(kv_kept, out_kept, raised_kept, q_kept, d0, d1, d_query, d_k, d_v):
    d_query[...], d_k[...], d_v[...] = attend_back_rows((d0, d1), q_kept, kv_kept, out_kept, raised_kept)


def attend_back_kernel(
    layer, kv_kept, out_kept, raised_kept, q_kept, d2, d3, near_q, near_k, near_v, wq, wk, wv,
    d_query, d_key, d_value, own, core, chip, cross, sums,
):
    d_q, d_k, d_v = attend_back_rows((d2, d3), q_kept, kv_kept, out_kept, raised_kept)
    d_q = jnp.concatenate([near_q[...], d_q], axis=0)
    d_k, d_v = ((item + near[...]).T.astype(bf16) for item, near in ((d_k, near_k), (d_v, near_v)))
    d_query[...] = d_q
    d_key[...] = d_k
    d_value[...] = d_v
    store_sums(sums, jnp.concatenate([d_q.astype(f32), d_v.astype(f32)], axis=1))
    store_rows(dot(d_q, wq[layer]) + dot(d_k, wk[layer]) + dot(d_v, wv[layer]), (own, core, chip, cross))


def store_pieces(place, grad, outs, order):
    if len(outs) == 1:
        outs[0][...] = grad.astype(bf16)
        return
    keep, send = outs
    bits = len(order)
    pieces = 1 << bits
    size = grad.shape[0] // pieces
    for piece in range(pieces):
        rel = place ^ piece
        index = 0
        for step, bit in enumerate(order[1:]):
            index = index + (((rel >> bit) & 1) << (bits - 2 - step))
        value = grad[piece * size : (piece + 1) * size].astype(bf16)
        leaves = (rel >> order[0]) & 1

        @pl.when(leaves == 0)
        def _(value=value, index=index, keep=keep):
            keep[index] = value

        @pl.when(leaves == 1)
        def _(value=value, index=index, send=send):
            send[index] = value


def split_refs(refs, *counts):
    parts = []
    for count in counts:
        parts.append(refs[:count])
        refs = refs[count:]
    return parts


def dot_tt(left, right):
    return lax.dot_general(left, right, (((0,), (1,)), ((), ())), preferred_element_type=f32)


def stack_cols(refs):
    return jnp.concatenate([ref[...] for ref in refs], axis=1)


def feed_grad_kernel(orders, spot, *refs):
    size = (len(refs) - 17) // 2
    pre, x, grad, act, one, two, (sums,) = split_refs(refs, 4, 4, 4, 4, size, size, 1)
    pre_near, pre_far = stack_rows(pre[:2]), stack_cols(pre[2:])
    up = dot_tn(stack_rows(x[:2]), pre_near) + dot_tt(stack_rows(x[2:]), pre_far)
    store_pieces(spot[1], up, one, orders[0])
    down = dot_tn(stack_rows(grad[:2]), stack_rows(act[:2])) + dot_tt(stack_rows(grad[2:]), stack_cols(act[2:]))
    store_pieces(spot[1], down, two, orders[1])
    ones = jnp.ones((sums.shape[0], pre_near.shape[0]), bf16)
    sums[...] = dot(ones, pre_near) + dot_nt(ones, pre_far)


def attend_grad_kernel(orders, spot, *refs):
    size = (len(refs) - 10) // 2
    x, (dq, dk, dv), grad, mixed, one, two = split_refs(refs, 1, 3, 4, 2, size, size)
    x = x[0][...]
    right = jnp.concatenate([dq[...], dk[...]], axis=1)
    store_pieces(spot[1], dot_tn(x, right), one, orders[0])
    out = dot_tn(stack_rows(grad), stack_rows(mixed))
    store_pieces(spot[1], jnp.concatenate([dot_tn(x, dv[...]), out], axis=1), two, orders[1])


def whole_grads(spots, keeps, gots):
    return [
        keep[...].astype(f32) + gots[spot][:, :, start : start + cols].astype(f32)
        for keep, (spot, start, cols) in zip(keeps, spots)
    ]


def halve_kernel(spots, groups, count, *refs):
    keeps, gots, rest = split_refs(refs, len(spots), count, len(refs) - len(spots) - count)
    held = [item.astype(bf16) for item in whole_grads(spots, keeps, gots)]
    if len(rest) > len(spots) + len(groups):
        rest[-1][...] = rest[0][...] + rest[1][...]
        rest = rest[2:]
    for item, ref in zip(held, rest):
        ref[...] = item[: ref.shape[0]]
    for group, ref in zip(groups, rest[len(spots) :]):
        ref[...] = jnp.concatenate([held[spot][ref.shape[0] :] for spot in group], axis=2)


def place_rows(head, piece, groups=4):
    return jnp.concatenate([jnp.where(head == item, piece, 0.0) for item in range(groups)], axis=1)


def collect_kernel(spot, *refs):
    rows = []
    for layer in range(len(refs) // 4):
        mix, feed, up, qv = refs[4 * layer : 4 * layer + 4]
        cols = qv.shape[1] // 2
        rows += [place_rows(spot[2], qv[:1, :cols]), place_rows(spot[2], qv[:1, cols:])]
        rows += [mix[:3, :], feed[:3, :]]
        rows += [jnp.where(spot[2] == item, up[:1, :], 0.0) for item in range(4)]
    refs[-1][...] = jnp.concatenate(rows, axis=0)


def assemble_kernel(spots, count, *refs):
    depth = len(spots) // 4
    keeps, gots, refs = split_refs(refs, len(spots), count, len(refs) - len(spots) - count)
    grads = whole_grads(spots, keeps, gots)
    small, refs = refs[0][...] + refs[1][...], refs[2:]
    g_q, g_k, g_v, g_o, g_up, g_down, *vectors, s_bu = refs
    cols = g_q.shape[2]
    for layer in range(depth):
        up, down, one, two = grads[4 * layer : 4 * layer + 4]
        g_up[layer] = up[0]
        g_down[layer] = down[0]
        g_q[layer] = one[0, :, :cols]
        g_k[layer] = one[0, :, cols:]
        g_v[layer] = two[0, :, :cols]
        g_o[layer] = two[0, :, cols:]
        rows = small[12 * layer : 12 * layer + 12]
        for item, ref in enumerate(vectors):
            ref[layer : layer + 1, :] = rows[item : item + 1, :]
        model = rows.shape[1]
        for item in range(4):
            s_bu[layer : layer + 1, item * model : (item + 1) * model] = rows[8 + item : 9 + item, :]


class Scalar:
    def __init__(self, array):
        self.array = array


class Far:
    def __init__(self, array):
        self.array = array


class Stay:
    def __init__(self, shape, kind):
        self.shape, self.kind = shape, kind


class View:
    def __init__(self, array, pieces=1):
        self.array, self.pieces = array, pieces


def call(kernel, name, ins, outs, vmem, scratch=()):
    arrays, specs, pieces = [], [], {}
    for spot, item in enumerate(ins):
        space = pltpu.VMEM
        if isinstance(item, Scalar):
            space = pltpu.SMEM
            arrays.append(item.array)
        elif isinstance(item, Far):
            space = pltpu.HBM
            arrays.append(pltpu.with_memory_space_constraint(item.array, pltpu.HBM))
        elif isinstance(item, View):
            arrays.append(pltpu.with_memory_space_constraint(item.array, pltpu.VMEM))
            pieces[spot] = item.pieces
        else:
            arrays.append(item)
        specs.append(pl.BlockSpec(memory_space=space))
    shapes = []
    for item in outs:
        if isinstance(item, Stay):
            shapes.append(pltpu.VMEM(item.shape, item.kind))
        else:
            shapes.append(jax.ShapeDtypeStruct(*item))

    def wrapped(*refs):
        kernel(*(Viewed(ref, pieces[spot]) if spot in pieces else ref for spot, ref in enumerate(refs)))

    return pl.pallas_call(
        wrapped,
        name=name,
        grid=(1,),
        out_shape=shapes,
        in_specs=specs,
        out_specs=[pl.BlockSpec(memory_space=pltpu.VMEM)] * len(shapes),
        scratch_shapes=scratch,
        compiler_params=pltpu.CompilerParams(vmem_limit_bytes=int(vmem * MIB)),
        cost_estimate=pl.CostEstimate(flops=int(GIGA.get(name, 0) * 1e9) + 1, bytes_accessed=1, transcendentals=0),
    )(*arrays)


def grad_outs(rows, cols, order):
    pieces = 1 << len(order)
    if (rows // pieces) % 16:
        return [((rows, cols), bf16)]
    return [((pieces // 2, rows // pieces, cols), bf16)] * 2


def start_halving(parts, place, orders):
    half = len(parts) // 2
    if half == 1:
        pairs = []
        for part, order in zip(parts, orders):
            pieces = 1 << len(order)
            whole = part.reshape(pieces, -1, part.shape[1])
            ranks = []
            for spot in range(pieces):
                ranks.append(
                    sum(((spot >> (len(order) - 1 - step)) & 1) << bit for step, bit in enumerate(order))
                )
            whole = jnp.take(whole, jnp.array(ranks, jnp.int32) ^ place, axis=0)
            pairs.append((whole[: pieces // 2], whole[pieces // 2 :]))
    else:
        pairs = (parts[:2], parts[2:])
    return Halving(*zip(*pairs), orders)


def body(
    hidden_in, w_query, w_key, w_value, b_query, b_value, w_out, b_out, ln1_gain, ln1_bias,
    w_up, b_up, w_down, b_down, ln2_gain, ln2_bias, token_mask, query_order, key_order,
    out_cotangent,
):
    depth, model, cols = w_query.shape
    rows = hidden_in.shape[0]
    units = w_up.shape[2]
    pack = token_mask.shape[0]
    heads = query_order.shape[1]
    head = lax.axis_index("head").astype(jnp.int32)
    groups = lax.axis_size("head")
    place = lax.axis_index("dp").astype(jnp.int32)
    spot = Scalar(jnp.stack([head * rows, place, head]))
    bits = lax.axis_size("dp").bit_length() - 1
    order_one = tuple(range(bits))
    order_two = order_one[:2][::-1] + order_one[2:]
    orders = (order_one, order_two)
    w_query, w_key, w_value = (item.transpose(0, 2, 1) for item in (w_query, w_key, w_value))
    q_order, k_order = query_order.transpose(1, 0, 2), key_order.transpose(1, 0, 2)

    wide = (rows, model)
    dense = 2 * rows * model
    wide_low, wide_full = (wide, bf16), (wide, f32)

    low = hidden_in
    chip, core = swap(low, "head", 2), swap(low, "head", 1)
    around = token_mask.reshape(groups, rows)
    live = jnp.concatenate(
        [lax.dynamic_index_in_dim(around, head ^ item, 0, keepdims=False) for item in range(groups)]
    )
    live = live.astype(f32).reshape(pack, 1)

    entry = hidden_in
    kept = []
    pair = 2 * rows
    two = 2 * HEAD_DIM
    kept_rows = [Stay((heads, pair, pack), bf16), Stay((heads, pair, two), f32), Stay((pair, cols), bf16)]
    other_units = [swap(item, "head", 1) for item in (w_up, b_up, w_down)]
    for layer in range(depth):
        *marks, weights = call(
            functools.partial(cluster_kernel, layer), "clusters",
            [spot, q_order, k_order, live, Far(w_query), Far(w_key), Far(w_value)],
            [((heads, pack, two), bf16)] * 2 + [((heads, 2 * two, model), bf16)], vmem=7,
            scratch=[pltpu.VMEM((3, cols, model), bf16), pltpu.SemaphoreType.DMA((3,))],
        )
        chip = tie(chip, weights)
        cross = swap(chip, "head", 1)
        if not layer:
            cross, other_units = tie((cross, other_units))
            ups, biases, downs = zip((w_up, b_up, w_down), other_units)
        w_mine = tie(w_out[layer], cross)
        w_core, w_chip = swap(w_mine, "head", 1), swap(w_mine, "head", 2)
        q_all, kv_all, ob2, ob3, raised_far, out_far, ob_far, x_kept = call(
            functools.partial(attend_kernel, layer), "attend",
            [low, core, chip, cross, weights, b_query, b_value, *marks],
            [((heads, pack, two), bf16)] * 2 + [((rows, cols), bf16)] * 2 + kept_rows
            + [Stay((pack, model), bf16)], vmem=6,
        )
        got2, got3 = swap(ob2, "head", 2), swap(ob3, "head", 3)
        ob0, ob1, raised_near, out_near, ob_near, *q_kept, kv_kept = call(
            attend_near_kernel, "attend_near", [q_all, kv_all, marks[1]],
            [((rows, cols), bf16)] * 2 + kept_rows + [Stay((heads, pair, two), bf16)] * 2
            + [Stay((heads, pack, two), bf16)], vmem=4,
        )
        got1 = swap(ob1, "head", 1)
        got1, got2, got3, w_core, w_chip = tie((got1, got2, got3, w_core, w_chip))
        w_cross = swap(w_chip, "head", 1)
        outs = (w_mine, w_core, w_chip, w_cross)
        got = [ob0, got1, got2, got3]
        normed1, low1, normed1_kept, w_kept = call(
            functools.partial(mix_kernel, layer), "mix",
            [*got, *outs, entry, b_out, ln1_gain, ln1_bias, ln2_gain, ln2_bias],
            [wide_full, wide_low, Stay((rows, model + CLUSTER), f32), Stay((4, cols, model), bf16)], vmem=4,
        )

        def feed(block, kind):
            def kernel(x, up, up2, bias, bias2, down, down2, x_kept, act, act2, slope, out):
                feed_kernel(layer, x, (up, up2), (bias, bias2), (down, down2), x_kept, (act, act2), slope, out)

            return call(
                kernel, "feed", [block, *ups, *biases, *downs],
                [Stay(wide, bf16), Stay((rows, units), bf16), ((rows, units), bf16),
                 Stay((rows, 2 * units), bf16), (wide, kind)], vmem=5.5,
            )

        def turn_weights(up, up2, bias, bias2, down, down2, *outs):
            turn_weights_kernel(layer, (up, up2), (bias, bias2), (down, down2), outs[:2], outs[2:4], outs[4:])

        def feed_turned(x, up, up2, bias, bias2, down, down2, x_kept, act, act2, slope, out):
            feed_turned_kernel(x, (up, up2), (bias, bias2), (down, down2), x_kept, (act, act2), slope, out)

        chip = swap(low1, "head", 2)
        turned = call(
            turn_weights, "turn_weights", [*tie([*ups, *biases, *downs], low1)],
            [((units, model), bf16)] * 2 + [((units, CLUSTER), f32)] * 2 + [((model, units), bf16)] * 2, vmem=4,
        )
        h_own, act_own, act_core, slope_own, own_term = feed(low1, f32)
        chip = tie(chip, own_term, turned)
        h_chip, act_chip, act_cross, slope_chip, far_term = call(
            feed_turned, "feed_turned", [chip, *turned],
            [Stay(wide, bf16), Stay((units, rows), bf16), ((units, rows), bf16), Stay((2 * units, rows), bf16),
             wide_low], vmem=5.5,
        )
        far = swap(far_term, "head", 2)
        away = [swap(item, "head", 1) for item in tie((h_own, act_core, h_chip, act_cross), far_term)]
        ends = [normed1, ln1_gain, ln1_bias, own_term, far, b_down, ln2_gain, ln2_bias]
        kept.append(
            (x_kept, (kv_kept, q_kept), ((out_near, raised_near), (out_far, raised_far)), (ob_near, ob_far),
             normed1_kept, w_kept, (slope_own, slope_chip))
        )
        if layer + 1 < depth:
            entry, low, normed2_kept = call(
                functools.partial(close_kernel, layer), "close", ends,
                [wide_full, wide_low, Stay((rows, model + CLUSTER), f32)], vmem=4,
            )
            kept[-1] += (normed2_kept,)
            low, away = tie((low, away))
            chip, core = swap(low, "head", 2), swap(low, "head", 1)
        else:
            result, low, sums2, d_second = call(
                functools.partial(turn_kernel, layer), "turn", ends + [out_cotangent],
                [wide_full, wide_low, ((8, model), f32), Stay(*wide_full)], vmem=4,
            )
            low, away = tie((low, away))
        h_core, act_core, h_cross, act_cross = away
        kept[-1] += ((h_own, h_core, h_chip, h_cross), (act_own, act_core, act_chip, act_cross))

    feed_sums = attend_sums = None
    grads, small = [None] * depth, [None] * depth
    pieces = heads
    for layer in reversed(range(depth)):
        x_kept, (kv_kept, q_kept), (near, far_rows), obs, normed1, w_kept, slopes, *_, h_kept, acts = kept[layer]
        above = feed_sums is not None

        def feed_back(grad, up, up2, down, down2, slope, pre, pre2, out):
            feed_back_kernel(layer, grad, (up, up2), (down, down2), slope, (pre, pre2), out)

        def feed_back_turned(grad, up, up2, down, down2, slope, pre, pre2, out):
            feed_back_turned_kernel(layer, grad, (up, up2), (down, down2), slope, (pre, pre2), out)

        chip, g_core = swap(low, "head", 2), swap(low, "head", 1)
        pre_own, pre_core, own_term = call(
            feed_back, "feed_back", [low, *ups, *downs, View(slopes[0])],
            [((rows, units), bf16)] * 2 + [wide_full], vmem=4,
        )
        pre_core = swap(pre_core, "head", 1)
        chip, g_core, pre_core = join((chip, g_core, pre_core), [feed_sums, attend_sums] if above else [], own_term)
        g_cross = swap(chip, "head", 1)
        pre_chip, pre_cross, far_term = call(
            feed_back_turned, "feed_back_turned", [chip, *ups, *downs, View(slopes[1])],
            [((units, rows), bf16)] * 2 + [wide_low], vmem=5,
        )
        far_term, g_cross = tie((far_term, g_cross))
        far = swap(far_term, "head", 2)
        pre_cross = swap(tie(pre_cross, far_term), "head", 1)
        g_blocks = (low, g_core, chip, g_cross)
        added = ()
        if above and attend_sums.more():
            added = advance([attend_sums], (), far_term)
        *parts, up_sums = call(
            functools.partial(feed_grad_kernel, orders), "feed_grad",
            [spot, *tie((pre_own, pre_core, pre_chip, pre_cross), added), *map(View, h_kept), *g_blocks,
             *map(View, acts)],
            grad_outs(model, units, order_one) + grad_outs(model, units, order_two) + [((8, units), f32)],
            vmem=9,
        )
        far = tie(far, parts)
        if above:
            parts = join(parts, [attend_sums])
        waiting = attend_sums
        feed_sums = start_halving(parts, place, orders)
        low, *d_obs, sums1, d_first = call(
            functools.partial(mix_back_kernel, layer), "mix_back",
            [View(d_second), View(normed1), View(w_kept, 4), own_term, far, ln1_gain],
            [wide_low] + [((rows, cols), bf16)] * 4 + [((8, model), f32), Stay(*wide_full)], vmem=4,
        )
        got = [d_obs[0]] + [swap(d_obs[item], "head", item) for item in (1, 2, 3)]

        def kept_part(part, start):
            out, raised = part
            raised = View(raised.reshape(heads * pair, pack), pieces)
            return [
                View(kv_kept, heads), View(out, heads), raised,
                View(q_kept[start // pair], heads),
            ]

        near_q, near_k, near_v = call(
            attend_back_near_kernel, "attend_back_near",
            kept_part(near, 0) + got[:2],
            [((pair, cols), bf16)] + [((cols, pack), f32)] * 2, vmem=4.5,
        )
        got = tie(got, near_q)
        others = [item for item in (feed_sums, waiting) if item]
        got = join(got, others)
        if any(item.more() for item in others):
            got = tie(got, advance(others, ()))
        low = tie(low, got)
        chip, core = swap(low, "head", 2), swap(low, "head", 1)
        d_q, d_k, d_v, own_term, core_term, chip_term, cross_term, sums_qv = call(
            functools.partial(attend_back_kernel, layer), "attend_back",
            kept_part(far_rows, pair)
            + [got[2], got[3], near_q, near_k, near_v, w_query, w_key, w_value],
            [((pack, cols), bf16)] * 3 + [wide_full, wide_low, wide_full, wide_low]
            + [((8, 2 * cols), f32)], vmem=7.5,
        )
        others = [item for item in (feed_sums, waiting) if item]
        chip, core, core_term, cross_term = join((chip, core, core_term, cross_term), others)
        got_chip, got_core = swap(cross_term, "head", 1), swap(core_term, "head", 1)
        cross = swap(chip, "head", 1)
        small[layer] = [sums1, sums2, up_sums, sums_qv]
        last = ()
        if not layer:
            mine = call(
                collect_kernel, "collect", [spot] + [item for part in small for item in part],
                [((12 * depth, model), f32)], vmem=3,
            )[0]
            last = (mine, swap(mine, "head", 1))
        got_chip, got_core, last = tie((got_chip, got_core, last))
        merged = (chip_term + got_chip.astype(f32)).astype(bf16)
        far = swap(merged, "head", 2)
        a_blocks = (low, core, chip, cross)
        added = ()
        if any(item.more() for item in others):
            added = advance(others, last, merged, apart=bool(layer))
        parts = call(
            functools.partial(attend_grad_kernel, orders), "attend_grad",
            [spot, View(x_kept), *tie((d_q, d_k, d_v), merged, added), *a_blocks, *map(View, obs)],
            grad_outs(model, 2 * cols, order_one) + grad_outs(model, 2 * cols, order_two), vmem=5,
        )
        if layer:
            far = land(far, [feed_sums.slots[0][0]], parts)
        if not layer:
            last = (added[-1], swap(added[-1], "dp", 1))
            parts, last = tie((parts, last))
        attend_sums = start_halving(parts, place, orders)
        grads[layer] = (feed_sums, attend_sums)
        if layer:
            low, sums2, d_second = call(
                functools.partial(open_back_kernel, layer - 1), "open_back",
                [View(kept[layer - 1][-3]), View(d_first), own_term, got_core, far, ln2_gain],
                [wide_low, ((8, model), f32), Stay(*wide_full)], vmem=4,
            )

    total = last[0] + last[1]
    for axis, bit in [("head", 1)] + [("dp", bit) for bit in reversed(range(1, bits))]:
        last = (total, swap(total, axis, 1 << bit))
        if attend_sums.more():
            far, last = join((far, last), [feed_sums, attend_sums])
            total = advance([attend_sums], last)[-1]
        elif (axis, bit) != ("dp", 1):
            total = last[0] + last[1]
    d_rows = d_first + own_term + got_core.astype(f32) + far.astype(f32)
    items = [item for layer in grads for item in layer]
    while any(item.more() for item in items):
        advance(items, ())
    ends = [keep for item in items for keep in item.keeps] + [item.got for item in transfers_of(items)]
    own = ends[0].shape[1]
    g_q, g_k, g_v, g_o, g_up, g_down, s_bq, s_bv, s_bo, s_g1, s_n1, s_bd, s_g2, s_n2, s_bu = call(
        functools.partial(assemble_kernel, spots_of(items), len(transfers_of(items))), "assemble", ends + list(last),
        [((depth, own, cols), f32)] * 4 + [((depth, own, units), f32)] * 2
        + [((depth, model), f32)] * 8 + [((depth, groups * units), f32)], vmem=8,
    )
    return (
        result, d_rows, g_q, g_k, g_v, s_bq, s_bv, g_o.transpose(0, 2, 1), s_bo, s_g1, s_n1, g_up,
        s_bu, g_down.transpose(0, 2, 1), s_bd, s_g2, s_n2,
    )


def solution(mesh):
    split = P(("dp", "head"), None)
    column, line = P(None, None, "head"), P(None, "head", None)
    placed = (
        split, column, column, column, P(None, "head"), P(None, "head"), line, P(), P(), P(),
        column, P(None, "head"), line, P(), P(), P(),
        P("dp"), P(None, "head", "dp"), P(None, "head", "dp"), split,
    )
    by_rows, by_cols = P(None, "dp", "head"), P(None, "head", "dp")
    results = (
        split, split, by_rows, by_rows, by_rows, P(), P(), by_cols, P(), P(), P(), by_rows, P(),
        by_cols, P(), P(), P(),
    )
    return jax.shard_map(body, mesh=mesh, in_specs=placed, out_specs=results, check_vma=False)
```

```python
import functools
import math

import jax
import jax.numpy as jnp
from jax import lax
from jax.experimental import pallas as pl
from jax.experimental.pallas import tpu as pltpu
from jax.sharding import PartitionSpec as P

CLUSTER = 128
HEAD_DIM = 64
EPS = 1e-12
NEG = -1e30
MIB = 1024 * 1024
GIGA = {"attend_back_near": 3}

f32 = jnp.float32
bf16 = jnp.bfloat16


def swap(array, axis, bit):
    size = lax.axis_size(axis)
    return lax.ppermute(array, axis, [(item, item ^ bit) for item in range(size)])


def tie(value, *earlier):
    return lax.optimization_barrier((value, earlier))[0]


class Transfer:
    def __init__(self, send, bit):
        self.got = swap(send, "dp", 1 << bit)


class Halving:
    def __init__(self, keeps, sends, orders):
        self.keeps, self.orders = list(keeps), [list(order) for order in orders]
        self.slots = [(Transfer(send, order.pop(0)), 0) for send, order in zip(sends, self.orders)]

    def more(self):
        return bool(self.orders[0])


def transfers_of(items):
    found = []
    for item in items:
        for transfer, _ in item.slots:
            if transfer not in found:
                found.append(transfer)
    return found


def spots_of(items):
    found = transfers_of(items)
    return [
        (found.index(transfer), start, keep.shape[2])
        for item in items
        for keep, (transfer, start) in zip(item.keeps, item.slots)
    ]


def join(value, items, *earlier):
    return land(value, transfers_of(items), *earlier)


def land(value, found, *earlier):
    value, gots, _ = lax.optimization_barrier((value, [item.got for item in found], earlier))
    for item, got in zip(found, gots):
        item.got = got
    return value


def advance(items, pair, *earlier, apart=False):
    items = [item for item in items if item.more()]
    found = transfers_of(items)
    keeps = [keep for item in items for keep in item.keeps]
    keeps, gots, pair = tie((keeps, [item.got for item in found], pair), *earlier)
    outs = [((keep.shape[0] // 2,) + keep.shape[1:], bf16) for keep in keeps]
    groups = {}
    bits = [order.pop(0) for item in items for order in item.orders]
    for spot, (bit, out) in enumerate(zip(bits, outs)):
        groups.setdefault((bit, out[0][0], spot if apart else 0), []).append(spot)
    sends = []
    for group in groups.values():
        cols = sum(outs[spot][0][2] for spot in group)
        sends.append((outs[group[0]][0][:2] + (cols,), bf16))
    parts = call(
        functools.partial(halve_kernel, spots_of(items), list(groups.values()), len(gots)), "halve",
        [*keeps, *gots, *pair], outs + sends + [(part.shape, f32) for part in pair[:1]], vmem=8,
    )
    slots = [None] * len(keeps)
    for (bit, *_), group, send in zip(groups, groups.values(), parts[len(keeps) :]):
        transfer, start = Transfer(send, bit), 0
        for spot in group:
            slots[spot] = (transfer, start)
            start += outs[spot][0][2]
    start = 0
    for item in items:
        stop = start + len(item.keeps)
        item.keeps, item.slots = parts[start:stop], slots[start:stop]
        start = stop
    return parts


def dot(left, right):
    return jnp.dot(left, right, preferred_element_type=f32)


def dot_nt(left, right):
    return lax.dot_general(left, right, (((1,), (1,)), ((), ())), preferred_element_type=f32)


def dot_tn(left, right):
    return lax.dot_general(left, right, (((0,), (0,)), ((), ())), preferred_element_type=f32)


def row(ref, layer):
    return ref[layer : layer + 1, :]


def normalise(rows):
    centre = rows - jnp.mean(rows, axis=-1, keepdims=True)
    spread = jnp.mean(centre * centre, axis=-1, keepdims=True)
    scale = lax.rsqrt(spread + EPS)
    return centre * scale, scale


def normalise_back(grad, gain, normed, scale):
    part = grad * gain
    mean_one = jnp.mean(part, axis=-1, keepdims=True)
    mean_two = jnp.mean(part * normed, axis=-1, keepdims=True)
    return (part - mean_one - normed * mean_two) * scale


def store_sums(ref, *arrays):
    rows = [jnp.sum(item, axis=0, keepdims=True) for item in arrays]
    rows.append(jnp.zeros((ref.shape[0] - len(rows), ref.shape[1]), f32))
    ref[...] = jnp.concatenate(rows, axis=0)


def gelu_pair(values):
    bell = jnp.exp(values * values * -0.5)
    t = 1.0 / (1.0 + (0.3275911 * math.sqrt(0.5)) * jnp.abs(values))
    poly = 0.5 * 1.061405429
    for factor in (-1.453152027, 1.421413741, -0.284496736, 0.254829592):
        poly = poly * t + 0.5 * factor
    tail = poly * t * bell
    cdf = jnp.where(values >= 0.0, 1.0 - tail, tail)
    return values * cdf, cdf + values * bell * (1.0 / math.sqrt(2.0 * math.pi))


def stack_rows(refs):
    return jnp.concatenate([ref[...] for ref in refs], axis=0)


def head_cols(array, head):
    return array[:, head * HEAD_DIM : (head + 1) * HEAD_DIM]


def lanes_of(rows):
    return lax.broadcasted_iota(jnp.int32, (rows, 2 * HEAD_DIM), 1)


class Viewed:
    def __init__(self, source, pieces):
        self.source, self.shape, self.size = source, source.shape, source.shape[0] // pieces

    def piece(self, item):
        return self.source[item * self.size : (item + 1) * self.size]

    def __getitem__(self, index):
        return self.source[index]


def cluster_kernel(layer, spot, q_order, k_order, live, wq, wk, wv, q_marks, k_marks, weights, held, sems):
    heads, length, width = q_marks.shape
    copies = [
        pltpu.make_async_copy(source.at[layer], held.at[item], sems.at[item])
        for item, source in enumerate((wq, wk, wv))
    ]
    for copy in copies:
        copy.start()
    count = length // CLUSTER
    lines = lax.broadcasted_iota(jnp.int32, (length, length), 0)
    spread_line = lax.broadcasted_iota(jnp.int32, (length, width), 0) // CLUSTER + HEAD_DIM
    lanes = lanes_of(length)
    spread = jnp.where(spread_line == lanes, 1.0, 0.0).astype(bf16)
    in_use = jnp.logical_and(lanes >= HEAD_DIM, lanes < HEAD_DIM + count)
    for head in range(heads):
        order = q_order[head, layer : layer + 1, :] ^ spot[0]
        hot = jnp.where(order == lines, 1.0, 0.0).astype(bf16)
        q_marks[head] = dot(hot, spread).astype(bf16)
        order = k_order[head, layer : layer + 1, :] ^ spot[0]
        hot = jnp.where(order == lines, 1.0, 0.0).astype(bf16)
        inside = dot(hot, spread) * live[...]
        outside = jnp.where(in_use, jnp.where(inside > 0.5, 0.0, NEG), 0.0)
        k_marks[head] = outside.astype(bf16)
    for copy in copies:
        copy.wait()
    blank = jnp.zeros((HEAD_DIM, held.shape[2]), bf16)
    for head in range(heads):
        part = slice(head * HEAD_DIM, (head + 1) * HEAD_DIM)
        weights[head] = jnp.concatenate([held[0, part], blank, held[1, part], held[2, part]], axis=0)


def attend_rows(first, rows, q_ref, kv_ref, k_marks, raised_kept, out_kept):
    heads, length, width = kv_ref.shape
    chunk = rows
    left = lanes_of(length) < HEAD_DIM
    mixed = []
    for head in range(heads):
        keys = kv_ref[head].astype(f32)
        marked = jnp.where(left, keys, k_marks[head].astype(f32)).astype(bf16)
        values = jnp.where(left, 1.0, keys).astype(bf16)
        outs = []
        for start in range(0, rows, chunk):
            scores = dot_nt(q_ref[head, first + start : first + start + chunk], marked)
            raised = jnp.exp(scores - jnp.max(scores, axis=1, keepdims=True)).astype(bf16)
            raised_kept[head, pl.ds(start, chunk)] = raised
            total = dot(raised, values)
            share = 1.0 / total
            outs.append(jnp.where(left[:chunk], share, total * pltpu.roll(share, HEAD_DIM, 1)))
        outs = jnp.concatenate(outs, axis=0)
        out_kept[head] = outs
        mixed.append(outs[:, HEAD_DIM:])
    return jnp.concatenate(mixed, axis=1).astype(bf16)


def attend_kernel(
    layer, x0, x1, x2, x3, weights, bq, bv, q_marks, k_marks,
    q_out, kv_out, ob2, ob3, raised_kept, out_kept, ob_kept, x_kept,
):
    size = ob2.shape[0]
    for item, ref in enumerate((x0, x1, x2, x3)):
        x_kept[pl.ds(item * size, size)] = ref[...]
    x = stack_rows((x0, x1, x2, x3))
    heads = q_out.shape[0]
    blank_b = jnp.zeros((1, HEAD_DIM), f32)
    bias_q, bias_v = row(bq, layer), row(bv, layer)
    for head in range(heads):
        part = slice(head * HEAD_DIM, (head + 1) * HEAD_DIM)
        bias = jnp.concatenate([bias_q[:, part], blank_b, blank_b, bias_v[:, part]], axis=1)
        qkv = (dot_nt(x, weights[head]) + bias).astype(bf16)
        query = qkv[:, : 2 * HEAD_DIM].astype(f32) * (1.0 / math.sqrt(HEAD_DIM))
        q_out[head] = (query + q_marks[head].astype(f32)).astype(bf16)
        kv_out[head] = qkv[:, 2 * HEAD_DIM :]
    mixed = attend_rows(2 * size, 2 * size, q_out, kv_out, k_marks, raised_kept, out_kept)
    ob_kept[...] = mixed
    ob2[...] = mixed[:size]
    ob3[...] = mixed[size:]


def attend_near_kernel(
    q_in, kv_in, k_marks, ob0, ob1, raised_kept, out_kept, ob_kept, q_near, q_far, kv_kept
):
    size = ob0.shape[0]
    q_near[...] = q_in[:, : 2 * size]
    q_far[...] = q_in[:, 2 * size :]
    kv_kept[...] = kv_in[...]
    mixed = attend_rows(0, 2 * size, q_in, kv_in, k_marks, raised_kept, out_kept)
    ob_kept[...] = mixed
    ob0[...] = mixed[:size]
    ob1[...] = mixed[size:]


def entry_rows(layer, x, gain, shift):
    rows = x[...].astype(f32)
    if layer:
        rows = rows * row(gain, layer - 1) + row(shift, layer - 1)
    return rows


def with_scale(unit, scale):
    return jnp.concatenate([unit, jnp.broadcast_to(scale, (unit.shape[0], CLUSTER))], axis=1)


def mix_kernel(
    layer, ob0, ob1, ob2, ob3, w0, w1, w2, w3, x, b_out, gain1, shift1, gain2, shift2,
    normed, low, normed_kept, w_kept,
):
    total = entry_rows(layer, x, gain2, shift2) + row(b_out, layer)
    for item, (left, right) in enumerate(((ob0, w0), (ob1, w1), (ob2, w2), (ob3, w3))):
        w_kept[item] = right[...]
        total = total + dot(left[...], right[...])
    unit, root = normalise(total)
    normed[...] = unit
    normed_kept[...] = with_scale(unit, root)
    low[...] = (unit * row(gain1, layer) + row(shift1, layer)).astype(bf16)


def store_rows(value, refs):
    start = 0
    for ref in refs:
        ref[...] = value[start : start + ref.shape[0]].astype(ref.dtype)
        start += ref.shape[0]


def feed_kernel(layer, x, ups, biases, downs, x_kept, acts, slope, out):
    rows = x[...]
    x_kept[...] = rows
    total = 0.0
    units = acts[0].shape[1]
    for item in range(2):
        act, der = gelu_pair(dot(rows, ups[item][layer]) + row(biases[item], layer))
        act = act.astype(bf16)
        acts[item][...] = act
        slope[:, item * units : (item + 1) * units] = der.astype(bf16)
        total = total + dot(act, downs[item][layer])
    out[...] = total.astype(out.dtype)


def turn_weights_kernel(layer, ups, biases, downs, ups_t, biases_t, downs_t):
    for item in range(2):
        ups_t[item][...] = ups[item][layer].T
        downs_t[item][...] = downs[item][layer].T
        bias = row(biases[item], layer)
        biases_t[item][...] = jnp.broadcast_to(bias, (CLUSTER, bias.shape[1])).T


def feed_turned_kernel(x, ups_t, biases_t, downs_t, x_kept, acts, slope, out):
    rows = x[...]
    x_kept[...] = rows
    total = 0.0
    units, count = acts[0].shape
    for item in range(2):
        bias = jnp.concatenate([biases_t[item][...]] * (count // CLUSTER), axis=1)
        act, der = gelu_pair(dot_nt(ups_t[item][...], rows) + bias)
        act = act.astype(bf16)
        acts[item][...] = act
        slope[item * units : (item + 1) * units, :] = der.astype(bf16)
        total = total + dot(downs_t[item][...], act)
    out[...] = total.T.astype(out.dtype)


def second_rows(layer, normed1, gain1, shift1, own, far, b_down):
    rows = normed1[...] * row(gain1, layer) + row(shift1, layer)
    return rows + own[...] + far[...].astype(f32) + row(b_down, layer)


def close_kernel(
    layer, normed1, gain1, shift1, own, far, b_down, gain2, shift2, normed, low, normed_kept
):
    unit, root = normalise(
        second_rows(layer, normed1, gain1, shift1, own, far, b_down)
    )
    normed[...] = unit
    normed_kept[...] = with_scale(unit, root)
    low[...] = (unit * row(gain2, layer) + row(shift2, layer)).astype(bf16)


def turn_kernel(
    layer, normed1, gain1, shift1, own, far, b_down, gain2, shift2, grad,
    result, low, sums, d_second,
):
    unit, root = normalise(
        second_rows(layer, normed1, gain1, shift1, own, far, b_down)
    )
    gain = row(gain2, layer)
    result[...] = unit * gain + row(shift2, layer)
    back = normalise_back(grad[...], gain, unit, root)
    d_second[...] = back
    low[...] = back.astype(bf16)
    store_sums(sums, back, grad[...] * unit, grad[...])


def unit_and_scale(kept, width):
    both = kept[...]
    return both[:, :width], both[:, width : width + 1]


def open_back_kernel(layer, normed2, base, own, core, far, gain2, low, sums, d_second):
    rest = own[...] + core[...].astype(f32) + far[...].astype(f32)
    grad = base[...] + rest
    unit, root = unit_and_scale(normed2, grad.shape[1])
    back = normalise_back(grad, row(gain2, layer), unit, root)
    d_second[...] = back
    low[...] = back.astype(bf16)
    store_sums(sums, back, grad * unit, grad)


def feed_back_kernel(layer, grad, ups, downs, slope, pres, out):
    rows = grad[...]
    total = 0.0
    units = pres[0].shape[1]
    for item in range(2):
        der = slope[:, item * units : (item + 1) * units].astype(f32)
        pre = (dot_nt(rows, downs[item][layer]) * der).astype(bf16)
        pres[item][...] = pre
        total = total + dot_nt(pre, ups[item][layer])
    out[...] = total.astype(out.dtype)


def feed_back_turned_kernel(layer, grad, ups, downs, slope, pres, out):
    rows = grad[...]
    total = 0.0
    units = pres[0].shape[0]
    for item in range(2):
        der = slope[item * units : (item + 1) * units, :].astype(f32)
        pre = (dot_nt(downs[item][layer], rows) * der).astype(bf16)
        pres[item][...] = pre
        total = total + dot(ups[item][layer], pre)
    out[...] = total.T.astype(out.dtype)


def mix_back_kernel(
    layer, base, normed1, weights, own, far, gain1, low, d0, d1, d2, d3, sums, d_first
):
    grad = base[...] + own[...] + far[...].astype(f32)
    unit, root = unit_and_scale(normed1, grad.shape[1])
    back = normalise_back(grad, row(gain1, layer), unit, root)
    d_first[...] = back
    small = back.astype(bf16)
    low[...] = small
    for item, out in enumerate((d0, d1, d2, d3)):
        out[...] = dot_nt(small, weights.piece(item)[0]).astype(bf16)
    store_sums(sums, back, grad * unit, grad)


def attend_back_rows(refs, q_kept, kv_kept, out_kept, raised_kept):
    d_mixed = stack_rows(refs)
    rows = d_mixed.shape[0]
    heads, length, width = kv_kept.shape
    chunk = rows
    steps = rows // chunk
    key_lanes, lanes = lanes_of(length), lanes_of(rows)[:, :HEAD_DIM]
    d_q, d_k, d_v = [], [], []
    for head in range(heads):
        part = slice(head * HEAD_DIM, (head + 1) * HEAD_DIM)
        keys = kv_kept.piece(head)[0]
        both = out_kept.piece(head)[0]
        share, out = both[:, :HEAD_DIM], both[:, HEAD_DIM:]
        grad = (d_mixed[:, part].astype(f32) * share).astype(bf16).astype(f32)
        inner = jnp.sum(grad * out, axis=1, keepdims=True)
        high = inner.astype(bf16).astype(f32)
        middle = (inner - high).astype(bf16).astype(f32)
        low = inner - high - middle
        terms = jnp.where(
            lanes == 0, -high, jnp.where(lanes == 1, -middle, jnp.where(lanes == 2, -low, 0.0))
        )
        grad = jnp.concatenate([terms, grad], axis=1).astype(bf16)
        values = jnp.where(
            key_lanes < 3, 1.0, jnp.where(key_lanes < HEAD_DIM, 0.0, keys.astype(f32))
        ).astype(bf16)
        d_score, raised = [], []
        for item in range(steps):
            d_prob = dot_nt(grad[item * chunk : (item + 1) * chunk], values)
            raised.append(raised_kept.piece(head * steps + item))
            d_score.append((raised[-1].astype(f32) * d_prob).astype(bf16))
        d_score = jnp.concatenate(d_score, axis=0)
        raised = jnp.concatenate(raised, axis=0)
        query = q_kept.piece(head)[0]
        d_q.append(dot(d_score, keys)[:, :HEAD_DIM] * (1.0 / math.sqrt(HEAD_DIM)))
        d_k.append(dot(query.T[:HEAD_DIM], d_score))
        d_v.append(dot(grad.T[HEAD_DIM:], raised))
    return (
        jnp.concatenate(d_q, axis=1).astype(bf16),
        jnp.concatenate(d_k, axis=0),
        jnp.concatenate(d_v, axis=0),
    )


def attend_back_near_kernel(kv_kept, out_kept, raised_kept, q_kept, d0, d1, d_query, d_k, d_v):
    d_query[...], d_k[...], d_v[...] = attend_back_rows((d0, d1), q_kept, kv_kept, out_kept, raised_kept)


def attend_back_kernel(
    layer, kv_kept, out_kept, raised_kept, q_kept, d2, d3, near_q, near_k, near_v, wq, wk, wv,
    d_query, d_key, d_value, own, core, chip, cross, sums,
):
    d_q, d_k, d_v = attend_back_rows((d2, d3), q_kept, kv_kept, out_kept, raised_kept)
    d_q = jnp.concatenate([near_q[...], d_q], axis=0)
    d_k, d_v = ((item + near[...]).T.astype(bf16) for item, near in ((d_k, near_k), (d_v, near_v)))
    d_query[...] = d_q
    d_key[...] = d_k
    d_value[...] = d_v
    store_sums(sums, jnp.concatenate([d_q.astype(f32), d_v.astype(f32)], axis=1))
    store_rows(dot(d_q, wq[layer]) + dot(d_k, wk[layer]) + dot(d_v, wv[layer]), (own, core, chip, cross))


def store_pieces(place, grad, outs, order):
    if len(outs) == 1:
        outs[0][...] = grad.astype(bf16)
        return
    keep, send = outs
    bits = len(order)
    pieces = 1 << bits
    size = grad.shape[0] // pieces
    for piece in range(pieces):
        rel = place ^ piece
        index = 0
        for step, bit in enumerate(order[1:]):
            index = index + (((rel >> bit) & 1) << (bits - 2 - step))
        value = grad[piece * size : (piece + 1) * size].astype(bf16)
        leaves = (rel >> order[0]) & 1

        @pl.when(leaves == 0)
        def _(value=value, index=index, keep=keep):
            keep[index] = value

        @pl.when(leaves == 1)
        def _(value=value, index=index, send=send):
            send[index] = value


def split_refs(refs, *counts):
    parts = []
    for count in counts:
        parts.append(refs[:count])
        refs = refs[count:]
    return parts


def dot_tt(left, right):
    return lax.dot_general(left, right, (((0,), (1,)), ((), ())), preferred_element_type=f32)


def stack_cols(refs):
    return jnp.concatenate([ref[...] for ref in refs], axis=1)


def feed_grad_kernel(orders, spot, *refs):
    size = (len(refs) - 17) // 2
    pre, x, grad, act, one, two, (sums,) = split_refs(refs, 4, 4, 4, 4, size, size, 1)
    pre_near, pre_far = stack_rows(pre[:2]), stack_cols(pre[2:])
    up = dot_tn(stack_rows(x[:2]), pre_near) + dot_tt(stack_rows(x[2:]), pre_far)
    store_pieces(spot[1], up, one, orders[0])
    down = dot_tn(stack_rows(grad[:2]), stack_rows(act[:2])) + dot_tt(stack_rows(grad[2:]), stack_cols(act[2:]))
    store_pieces(spot[1], down, two, orders[1])
    ones = jnp.ones((sums.shape[0], pre_near.shape[0]), bf16)
    sums[...] = dot(ones, pre_near) + dot_nt(ones, pre_far)


def attend_grad_kernel(orders, spot, *refs):
    size = (len(refs) - 10) // 2
    x, (dq, dk, dv), grad, mixed, one, two = split_refs(refs, 1, 3, 4, 2, size, size)
    x = x[0][...]
    right = jnp.concatenate([dq[...], dk[...]], axis=1)
    store_pieces(spot[1], dot_tn(x, right), one, orders[0])
    out = dot_tn(stack_rows(grad), stack_rows(mixed))
    store_pieces(spot[1], jnp.concatenate([dot_tn(x, dv[...]), out], axis=1), two, orders[1])


def whole_grads(spots, keeps, gots):
    return [
        keep[...].astype(f32) + gots[spot][:, :, start : start + cols].astype(f32)
        for keep, (spot, start, cols) in zip(keeps, spots)
    ]


def halve_kernel(spots, groups, count, *refs):
    keeps, gots, rest = split_refs(refs, len(spots), count, len(refs) - len(spots) - count)
    held = [item.astype(bf16) for item in whole_grads(spots, keeps, gots)]
    if len(rest) > len(spots) + len(groups):
        rest[-1][...] = rest[0][...] + rest[1][...]
        rest = rest[2:]
    for item, ref in zip(held, rest):
        ref[...] = item[: ref.shape[0]]
    for group, ref in zip(groups, rest[len(spots) :]):
        ref[...] = jnp.concatenate([held[spot][ref.shape[0] :] for spot in group], axis=2)


def place_rows(head, piece, groups=4):
    return jnp.concatenate([jnp.where(head == item, piece, 0.0) for item in range(groups)], axis=1)


def collect_kernel(spot, *refs):
    rows = []
    for layer in range(len(refs) // 4):
        mix, feed, up, qv = refs[4 * layer : 4 * layer + 4]
        cols = qv.shape[1] // 2
        rows += [place_rows(spot[2], qv[:1, :cols]), place_rows(spot[2], qv[:1, cols:])]
        rows += [mix[:3, :], feed[:3, :]]
        rows += [jnp.where(spot[2] == item, up[:1, :], 0.0) for item in range(4)]
    refs[-1][...] = jnp.concatenate(rows, axis=0)


def assemble_kernel(spots, count, terms, *refs):
    depth = len(spots) // 4
    keeps, gots, refs = split_refs(refs, len(spots), count, len(refs) - len(spots) - count)
    grads = whole_grads(spots, keeps, gots)
    small, refs = functools.reduce(jnp.add, [ref[...] for ref in refs[:terms]]), refs[terms:]
    g_q, g_k, g_v, g_o, g_up, g_down, *vectors, s_bu = refs
    cols = g_q.shape[2]
    for layer in range(depth):
        up, down, one, two = grads[4 * layer : 4 * layer + 4]
        g_up[layer] = up[0]
        g_down[layer] = down[0]
        g_q[layer] = one[0, :, :cols]
        g_k[layer] = one[0, :, cols:]
        g_v[layer] = two[0, :, :cols]
        g_o[layer] = two[0, :, cols:].T
        rows = small[12 * layer : 12 * layer + 12]
        for item, ref in enumerate(vectors):
            ref[layer : layer + 1, :] = rows[item : item + 1, :]
        model = rows.shape[1]
        for item in range(4):
            s_bu[layer : layer + 1, item * model : (item + 1) * model] = rows[8 + item : 9 + item, :]


class Scalar:
    def __init__(self, array):
        self.array = array


class Far:
    def __init__(self, array):
        self.array = array


class Stay:
    def __init__(self, shape, kind):
        self.shape, self.kind = shape, kind


class View:
    def __init__(self, array, pieces=1):
        self.array, self.pieces = array, pieces


def call(kernel, name, ins, outs, vmem, scratch=()):
    arrays, specs, pieces = [], [], {}
    for spot, item in enumerate(ins):
        space = pltpu.VMEM
        if isinstance(item, Scalar):
            space = pltpu.SMEM
            arrays.append(item.array)
        elif isinstance(item, Far):
            space = pltpu.HBM
            arrays.append(pltpu.with_memory_space_constraint(item.array, pltpu.HBM))
        elif isinstance(item, View):
            arrays.append(pltpu.with_memory_space_constraint(item.array, pltpu.VMEM))
            pieces[spot] = item.pieces
        else:
            arrays.append(item)
        specs.append(pl.BlockSpec(memory_space=space))
    shapes = []
    for item in outs:
        if isinstance(item, Stay):
            shapes.append(pltpu.VMEM(item.shape, item.kind))
        else:
            shapes.append(jax.ShapeDtypeStruct(*item))

    def wrapped(*refs):
        kernel(*(Viewed(ref, pieces[spot]) if spot in pieces else ref for spot, ref in enumerate(refs)))

    return pl.pallas_call(
        wrapped,
        name=name,
        grid=(1,),
        out_shape=shapes,
        in_specs=specs,
        out_specs=[pl.BlockSpec(memory_space=pltpu.VMEM)] * len(shapes),
        scratch_shapes=scratch,
        compiler_params=pltpu.CompilerParams(vmem_limit_bytes=int(vmem * MIB)),
        cost_estimate=pl.CostEstimate(flops=int(GIGA.get(name, 0) * 1e9) + 1, bytes_accessed=1, transcendentals=0),
    )(*arrays)


def grad_outs(rows, cols, order):
    pieces = 1 << len(order)
    if (rows // pieces) % 16:
        return [((rows, cols), bf16)]
    return [((pieces // 2, rows // pieces, cols), bf16)] * 2


def start_halving(parts, place, orders):
    half = len(parts) // 2
    if half == 1:
        pairs = []
        for part, order in zip(parts, orders):
            pieces = 1 << len(order)
            whole = part.reshape(pieces, -1, part.shape[1])
            ranks = []
            for spot in range(pieces):
                ranks.append(
                    sum(((spot >> (len(order) - 1 - step)) & 1) << bit for step, bit in enumerate(order))
                )
            whole = jnp.take(whole, jnp.array(ranks, jnp.int32) ^ place, axis=0)
            pairs.append((whole[: pieces // 2], whole[pieces // 2 :]))
    else:
        pairs = (parts[:2], parts[2:])
    return Halving(*zip(*pairs), orders)


def body(
    hidden_in, w_query, w_key, w_value, b_query, b_value, w_out, b_out, ln1_gain, ln1_bias,
    w_up, b_up, w_down, b_down, ln2_gain, ln2_bias, token_mask, query_order, key_order,
    out_cotangent,
):
    depth, model, cols = w_query.shape
    rows = hidden_in.shape[0]
    units = w_up.shape[2]
    pack = token_mask.shape[0]
    heads = query_order.shape[1]
    head = lax.axis_index("head").astype(jnp.int32)
    groups = lax.axis_size("head")
    place = lax.axis_index("dp").astype(jnp.int32)
    spot = Scalar(jnp.stack([head * rows, place, head]))
    bits = lax.axis_size("dp").bit_length() - 1
    order_one = tuple(range(bits))
    order_two = order_one[:2][::-1] + order_one[2:]
    orders = (order_one, order_two)
    w_query, w_key, w_value = (item.transpose(0, 2, 1) for item in (w_query, w_key, w_value))
    q_order, k_order = query_order.transpose(1, 0, 2), key_order.transpose(1, 0, 2)

    wide = (rows, model)
    dense = 2 * rows * model
    wide_low, wide_full = (wide, bf16), (wide, f32)

    low = hidden_in
    chip, core = swap(low, "head", 2), swap(low, "head", 1)
    around = token_mask.reshape(groups, rows)
    live = jnp.concatenate(
        [lax.dynamic_index_in_dim(around, head ^ item, 0, keepdims=False) for item in range(groups)]
    )
    live = live.astype(f32).reshape(pack, 1)

    entry = hidden_in
    kept = []
    pair = 2 * rows
    two = 2 * HEAD_DIM
    kept_rows = [Stay((heads, pair, pack), bf16), Stay((heads, pair, two), f32), Stay((pair, cols), bf16)]
    other_units = [swap(item, "head", 1) for item in (w_up, b_up, w_down)]
    for layer in range(depth):
        *marks, weights = call(
            functools.partial(cluster_kernel, layer), "clusters",
            [spot, q_order, k_order, live, Far(w_query), Far(w_key), Far(w_value)],
            [((heads, pack, two), bf16)] * 2 + [((heads, 2 * two, model), bf16)], vmem=7,
            scratch=[pltpu.VMEM((3, cols, model), bf16), pltpu.SemaphoreType.DMA((3,))],
        )
        chip = tie(chip, weights)
        cross = swap(chip, "head", 1)
        if not layer:
            cross, other_units = tie((cross, other_units))
            pinned = [pltpu.with_memory_space_constraint(item, pltpu.VMEM) for item in other_units]
            ups, biases, downs = zip((w_up, b_up, w_down), pinned)
        w_mine = tie(w_out[layer], cross)
        w_core, w_chip = swap(w_mine, "head", 1), swap(w_mine, "head", 2)
        q_all, kv_all, ob2, ob3, raised_far, out_far, ob_far, x_kept = call(
            functools.partial(attend_kernel, layer), "attend",
            [low, core, chip, cross, weights, b_query, b_value, *marks],
            [((heads, pack, two), bf16)] * 2 + [((rows, cols), bf16)] * 2 + kept_rows
            + [Stay((pack, model), bf16)], vmem=6,
        )
        got2, got3 = swap(ob2, "head", 2), swap(ob3, "head", 3)
        ob0, ob1, raised_near, out_near, ob_near, *q_kept, kv_kept = call(
            attend_near_kernel, "attend_near", [q_all, kv_all, marks[1]],
            [((rows, cols), bf16)] * 2 + kept_rows + [Stay((heads, pair, two), bf16)] * 2
            + [Stay((heads, pack, two), bf16)], vmem=4,
        )
        got1 = swap(ob1, "head", 1)
        got1, got2, got3, w_core, w_chip = tie((got1, got2, got3, w_core, w_chip))
        w_cross = swap(w_chip, "head", 1)
        outs = (w_mine, w_core, w_chip, w_cross)
        got = [ob0, got1, got2, got3]
        normed1, low1, normed1_kept, w_kept = call(
            functools.partial(mix_kernel, layer), "mix",
            [*got, *outs, entry, b_out, ln1_gain, ln1_bias, ln2_gain, ln2_bias],
            [wide_full, wide_low, Stay((rows, model + CLUSTER), f32), Stay((4, cols, model), bf16)], vmem=4,
        )

        def feed(block, kind):
            def kernel(x, up, up2, bias, bias2, down, down2, x_kept, act, act2, slope, out):
                feed_kernel(layer, x, (up, up2), (bias, bias2), (down, down2), x_kept, (act, act2), slope, out)

            return call(
                kernel, "feed", [block, *ups, *biases, *downs],
                [Stay(wide, bf16), Stay((rows, units), bf16), ((rows, units), bf16),
                 Stay((rows, 2 * units), bf16), (wide, kind)], vmem=5.5,
            )

        def turn_weights(up, up2, bias, bias2, down, down2, *outs):
            turn_weights_kernel(layer, (up, up2), (bias, bias2), (down, down2), outs[:2], outs[2:4], outs[4:])

        def feed_turned(x, up, up2, bias, bias2, down, down2, x_kept, act, act2, slope, out):
            feed_turned_kernel(x, (up, up2), (bias, bias2), (down, down2), x_kept, (act, act2), slope, out)

        chip = swap(low1, "head", 2)
        turned = call(
            turn_weights, "turn_weights", [*tie([*ups, *biases, *downs], low1)],
            [((units, model), bf16)] * 2 + [((units, CLUSTER), f32)] * 2 + [((model, units), bf16)] * 2, vmem=4,
        )
        h_own, act_own, act_core, slope_own, own_term = feed(low1, f32)
        chip = tie(chip, own_term, turned)
        h_chip, act_chip, act_cross, slope_chip, far_term = call(
            feed_turned, "feed_turned", [chip, *turned],
            [Stay(wide, bf16), Stay((units, rows), bf16), ((units, rows), bf16), Stay((2 * units, rows), bf16),
             wide_low], vmem=5.5,
        )
        far = swap(far_term, "head", 2)
        away = [swap(item, "head", 1) for item in tie((h_own, act_core, h_chip, act_cross), far_term)]
        ends = [normed1, ln1_gain, ln1_bias, own_term, far, b_down, ln2_gain, ln2_bias]
        kept.append(
            (x_kept, (kv_kept, q_kept), ((out_near, raised_near), (out_far, raised_far)), (ob_near, ob_far),
             normed1_kept, w_kept, (slope_own, slope_chip))
        )
        if layer + 1 < depth:
            entry, low, normed2_kept = call(
                functools.partial(close_kernel, layer), "close", ends,
                [wide_full, wide_low, Stay((rows, model + CLUSTER), f32)], vmem=4,
            )
            kept[-1] += (normed2_kept,)
            low, away = tie((low, away))
            chip, core = swap(low, "head", 2), swap(low, "head", 1)
        else:
            result, low, sums2, d_second = call(
                functools.partial(turn_kernel, layer), "turn", ends + [out_cotangent],
                [wide_full, wide_low, ((8, model), f32), Stay(*wide_full)], vmem=4,
            )
            low, away = tie((low, away))
        h_core, act_core, h_cross, act_cross = away
        kept[-1] += ((h_own, h_core, h_chip, h_cross), (act_own, act_core, act_chip, act_cross))

    feed_sums = attend_sums = None
    grads, small = [None] * depth, [None] * depth
    pieces = heads
    for layer in reversed(range(depth)):
        x_kept, (kv_kept, q_kept), (near, far_rows), obs, normed1, w_kept, slopes, *_, h_kept, acts = kept[layer]
        above = feed_sums is not None

        def feed_back(grad, up, up2, down, down2, slope, pre, pre2, out):
            feed_back_kernel(layer, grad, (up, up2), (down, down2), slope, (pre, pre2), out)

        def feed_back_turned(grad, up, up2, down, down2, slope, pre, pre2, out):
            feed_back_turned_kernel(layer, grad, (up, up2), (down, down2), slope, (pre, pre2), out)

        chip, g_core = swap(low, "head", 2), swap(low, "head", 1)
        pre_own, pre_core, own_term = call(
            feed_back, "feed_back", [low, *ups, *downs, View(slopes[0])],
            [((rows, units), bf16)] * 2 + [wide_full], vmem=4,
        )
        chip, g_core = join((chip, g_core), [feed_sums, attend_sums] if above else [], own_term)
        g_cross = swap(chip, "head", 1)
        pre_chip, pre_cross, far_term = call(
            feed_back_turned, "feed_back_turned", [chip, *ups, *downs, View(slopes[1])],
            [((units, rows), bf16)] * 2 + [wide_low], vmem=5,
        )
        far_term, g_cross = tie((far_term, g_cross))
        far = swap(far_term, "head", 2)
        pre_core, pre_cross = [swap(item, "head", 1) for item in tie((pre_core, pre_cross), far_term)]
        g_blocks = (low, g_core, chip, g_cross)
        added = ()
        if above and attend_sums.more():
            added = advance([attend_sums], (), far_term)
        *parts, up_sums = call(
            functools.partial(feed_grad_kernel, orders), "feed_grad",
            [spot, *tie((pre_own, pre_core, pre_chip, pre_cross), added), *map(View, h_kept), *g_blocks,
             *map(View, acts)],
            grad_outs(model, units, order_one) + grad_outs(model, units, order_two) + [((8, units), f32)],
            vmem=9,
        )
        far = tie(far, parts)
        if above:
            parts = join(parts, [attend_sums])
        waiting = attend_sums
        feed_sums = start_halving(parts, place, orders)
        low, *d_obs, sums1, d_first = call(
            functools.partial(mix_back_kernel, layer), "mix_back",
            [View(d_second), View(normed1), View(w_kept, 4), own_term, far, ln1_gain],
            [wide_low] + [((rows, cols), bf16)] * 4 + [((8, model), f32), Stay(*wide_full)], vmem=4,
        )
        got = [d_obs[0]] + [swap(d_obs[item], "head", item) for item in (1, 2, 3)]

        def kept_part(part, start):
            out, raised = part
            raised = View(raised.reshape(heads * pair, pack), pieces)
            return [
                View(kv_kept, heads), View(out, heads), raised,
                View(q_kept[start // pair], heads),
            ]

        near_q, near_k, near_v = call(
            attend_back_near_kernel, "attend_back_near",
            kept_part(near, 0) + got[:2],
            [((pair, cols), bf16)] + [((cols, pack), f32)] * 2, vmem=4.5,
        )
        got = tie(got, near_q)
        others = [item for item in (feed_sums, waiting) if item]
        got = join(got, others)
        if any(item.more() for item in others):
            got = tie(got, advance(others, ()))
        low = tie(low, got)
        chip, core = swap(low, "head", 2), swap(low, "head", 1)
        d_q, d_k, d_v, own_term, core_term, chip_term, cross_term, sums_qv = call(
            functools.partial(attend_back_kernel, layer), "attend_back",
            kept_part(far_rows, pair)
            + [got[2], got[3], near_q, near_k, near_v, w_query, w_key, w_value],
            [((pack, cols), bf16)] * 3 + [wide_full, wide_low, wide_full, wide_low]
            + [((8, 2 * cols), f32)], vmem=7.5,
        )
        others = [item for item in (feed_sums, waiting) if item]
        chip, core, core_term, cross_term = join((chip, core, core_term, cross_term), others)
        got_chip, got_core = swap(cross_term, "head", 1), swap(core_term, "head", 1)
        cross = swap(chip, "head", 1)
        small[layer] = [sums1, sums2, up_sums, sums_qv]
        last = ()
        if not layer:
            mine = call(
                collect_kernel, "collect", [spot] + [item for part in small for item in part],
                [((12 * depth, model), f32)], vmem=3,
            )[0]
            last = (mine, swap(mine, "head", 1))
        got_chip, got_core, last = tie((got_chip, got_core, last))
        merged = (chip_term + got_chip.astype(f32)).astype(bf16)
        far = swap(merged, "head", 2)
        a_blocks = (low, core, chip, cross)
        added = ()
        if any(item.more() for item in others):
            added = advance(others, last, merged, apart=bool(layer))
        parts = call(
            functools.partial(attend_grad_kernel, orders), "attend_grad",
            [spot, View(x_kept), *tie((d_q, d_k, d_v), merged, added), *a_blocks, *map(View, obs)],
            grad_outs(model, 2 * cols, order_one) + grad_outs(model, 2 * cols, order_two), vmem=5,
        )
        if layer:
            far = land(far, [feed_sums.slots[0][0]], parts)
        if not layer:
            last = (added[-1], swap(added[-1], "dp", 1))
            parts, last = tie((parts, last))
        attend_sums = start_halving(parts, place, orders)
        grads[layer] = (feed_sums, attend_sums)
        if layer:
            low, sums2, d_second = call(
                functools.partial(open_back_kernel, layer - 1), "open_back",
                [View(kept[layer - 1][-3]), View(d_first), own_term, got_core, far, ln2_gain],
                [wide_low, ((8, model), f32), Stay(*wide_full)], vmem=4,
            )

    hops = [("head", 1)] + [("dp", bit) for bit in reversed(range(1, bits))]
    for at, (axis, bit) in enumerate(hops):
        if at == 1:
            far, last = join((far, last), [feed_sums])
        if at > 1:
            last = join(last, [attend_sums])
        if at > 1 and attend_sums.more():
            total = advance([attend_sums], last)[-1]
        else:
            total = last[0] + last[1]
        last = (total, swap(total, axis, 1 << bit))
    last = join(last, [attend_sums])
    if attend_sums.more():
        last = (advance([attend_sums], last)[-1],)
    d_rows = d_first + own_term + got_core.astype(f32) + far.astype(f32)
    items = [item for layer in grads for item in layer]
    while any(item.more() for item in items):
        advance(items, ())
    ends = [keep for item in items for keep in item.keeps] + [item.got for item in transfers_of(items)]
    own = ends[0].shape[1]
    g_q, g_k, g_v, g_o, g_up, g_down, s_bq, s_bv, s_bo, s_g1, s_n1, s_bd, s_g2, s_n2, s_bu = call(
        functools.partial(assemble_kernel, spots_of(items), len(transfers_of(items)), len(last)), "assemble",
        ends + list(last),
        [((depth, own, cols), f32)] * 3 + [((depth, cols, own), f32)] + [((depth, own, units), f32)] * 2
        + [((depth, model), f32)] * 8 + [((depth, groups * units), f32)], vmem=8,
    )
    return (
        result, d_rows, g_q, g_k, g_v, s_bq, s_bv, g_o, s_bo, s_g1, s_n1, g_up,
        s_bu, g_down.transpose(0, 2, 1), s_bd, s_g2, s_n2,
    )


def solution(mesh):
    split = P(("dp", "head"), None)
    column, line = P(None, None, "head"), P(None, "head", None)
    placed = (
        split, column, column, column, P(None, "head"), P(None, "head"), line, P(), P(), P(),
        column, P(None, "head"), line, P(), P(), P(),
        P("dp"), P(None, "head", "dp"), P(None, "head", "dp"), split,
    )
    by_rows, by_cols = P(None, "dp", "head"), P(None, "head", "dp")
    results = (
        split, split, by_rows, by_rows, by_rows, P(), P(), by_cols, P(), P(), P(), by_rows, P(),
        by_cols, P(), P(), P(),
    )
    return jax.shard_map(body, mesh=mesh, in_specs=placed, out_specs=results, check_vma=False)
```

```python
import functools
import math

import jax
import jax.numpy as jnp
from jax import lax
from jax.experimental import pallas as pl
from jax.experimental.pallas import tpu as pltpu
from jax.sharding import PartitionSpec as P

CLUSTER = 128
HEAD_DIM = 64
EPS = 1e-12
NEG = -1e30
MIB = 1024 * 1024
GIGA = {"attend_back_near": 3, "close_back": 3}

f32 = jnp.float32
bf16 = jnp.bfloat16


def swap(array, axis, bit):
    size = lax.axis_size(axis)
    return lax.ppermute(array, axis, [(item, item ^ bit) for item in range(size)])


def tie(value, *earlier):
    return lax.optimization_barrier((value, earlier))[0]


class Transfer:
    def __init__(self, send, bit):
        self.got = swap(send, "dp", 1 << bit)


class Halving:
    def __init__(self, keeps, sends, orders):
        self.keeps, self.orders = list(keeps), [list(order) for order in orders]
        self.slots = [(Transfer(send, order.pop(0)), 0) for send, order in zip(sends, self.orders)]

    def more(self):
        return bool(self.orders[0])


def transfers_of(items):
    found = []
    for item in items:
        for transfer, _ in item.slots:
            if transfer not in found:
                found.append(transfer)
    return found


def spots_of(items):
    found = transfers_of(items)
    return [
        (found.index(transfer), start, keep.shape[2], keep.shape[1])
        for item in items
        for keep, (transfer, start) in zip(item.keeps, item.slots)
    ]


def join(value, items, *earlier):
    return land(value, transfers_of(items), *earlier)


def land(value, found, *earlier):
    value, gots, _ = lax.optimization_barrier((value, [item.got for item in found], earlier))
    for item, got in zip(found, gots):
        item.got = got
    return value


def advance(items, *earlier, apart=False):
    items = [item for item in items if item.more()]
    found = transfers_of(items)
    keeps = [keep for item in items for keep in item.keeps]
    keeps, gots = tie((keeps, [item.got for item in found]), *earlier)
    outs = [((keep.shape[0] // 2,) + keep.shape[1:], bf16) for keep in keeps]
    groups = {}
    bits = [order.pop(0) for item in items for order in item.orders]
    for spot, (bit, out) in enumerate(zip(bits, outs)):
        groups.setdefault((bit, out[0][0], spot if apart else 0), []).append(spot)
    sends = []
    for group in groups.values():
        cols = sum(outs[spot][0][2] for spot in group)
        rows = max(outs[spot][0][1] for spot in group)
        sends.append(((outs[group[0]][0][0], rows, cols), bf16))
    parts = call(
        functools.partial(halve_kernel, spots_of(items), list(groups.values()), len(gots)), "halve",
        [*keeps, *gots], outs + sends, vmem=8,
    )
    slots = [None] * len(keeps)
    for (bit, *_), group, send in zip(groups, groups.values(), parts[len(keeps) :]):
        transfer, start = Transfer(send, bit), 0
        for spot in group:
            slots[spot] = (transfer, start)
            start += outs[spot][0][2]
    start = 0
    for item in items:
        stop = start + len(item.keeps)
        item.keeps, item.slots = parts[start:stop], slots[start:stop]
        start = stop
    return parts


def dot(left, right):
    return jnp.dot(left, right, preferred_element_type=f32)


def dot_nt(left, right):
    return lax.dot_general(left, right, (((1,), (1,)), ((), ())), preferred_element_type=f32)


def dot_tn(left, right):
    return lax.dot_general(left, right, (((0,), (0,)), ((), ())), preferred_element_type=f32)


def row(ref, layer):
    return ref[layer : layer + 1, :]


def normalise(rows):
    centre = rows - jnp.mean(rows, axis=-1, keepdims=True)
    spread = jnp.mean(centre * centre, axis=-1, keepdims=True)
    scale = lax.rsqrt(spread + EPS)
    return centre * scale, scale


def normalise_back(grad, gain, normed, scale):
    part = grad * gain
    mean_one = jnp.mean(part, axis=-1, keepdims=True)
    mean_two = jnp.mean(part * normed, axis=-1, keepdims=True)
    return (part - mean_one - normed * mean_two) * scale


def store_sums(ref, *arrays):
    rows = [jnp.sum(item, axis=0, keepdims=True) for item in arrays]
    rows.append(jnp.zeros((ref.shape[0] - len(rows), ref.shape[1]), f32))
    ref[...] = jnp.concatenate(rows, axis=0)


def gelu_pair(values):
    bell = jnp.exp(values * values * -0.5)
    t = 1.0 / (1.0 + (0.3275911 * math.sqrt(0.5)) * jnp.abs(values))
    poly = 0.5 * 1.061405429
    for factor in (-1.453152027, 1.421413741, -0.284496736, 0.254829592):
        poly = poly * t + 0.5 * factor
    tail = poly * t * bell
    cdf = jnp.where(values >= 0.0, 1.0 - tail, tail)
    return values * cdf, cdf + values * bell * (1.0 / math.sqrt(2.0 * math.pi))


def stack_rows(refs):
    return jnp.concatenate([ref[...] for ref in refs], axis=0)


def head_cols(array, head):
    return array[:, head * HEAD_DIM : (head + 1) * HEAD_DIM]


def lanes_of(rows):
    return lax.broadcasted_iota(jnp.int32, (rows, 2 * HEAD_DIM), 1)


class Viewed:
    def __init__(self, source, pieces):
        self.source, self.shape, self.size = source, source.shape, source.shape[0] // pieces

    def piece(self, item):
        return self.source[item * self.size : (item + 1) * self.size]

    def __getitem__(self, index):
        return self.source[index]


def cluster_kernel(layer, spot, q_order, k_order, live, wq, wk, wv, q_marks, k_marks, weights, held, sems):
    heads, length, width = q_marks.shape
    copies = [
        pltpu.make_async_copy(source.at[layer], held.at[item], sems.at[item])
        for item, source in enumerate((wq, wk, wv))
    ]
    for copy in copies:
        copy.start()
    count = length // CLUSTER
    lines = lax.broadcasted_iota(jnp.int32, (length, length), 0)
    spread_line = lax.broadcasted_iota(jnp.int32, (length, width), 0) // CLUSTER + HEAD_DIM
    lanes = lanes_of(length)
    spread = jnp.where(spread_line == lanes, 1.0, 0.0).astype(bf16)
    in_use = jnp.logical_and(lanes >= HEAD_DIM, lanes < HEAD_DIM + count)
    for head in range(heads):
        order = q_order[head, layer : layer + 1, :] ^ spot[0]
        hot = jnp.where(order == lines, 1.0, 0.0).astype(bf16)
        q_marks[head] = dot(hot, spread).astype(bf16)
        order = k_order[head, layer : layer + 1, :] ^ spot[0]
        hot = jnp.where(order == lines, 1.0, 0.0).astype(bf16)
        inside = dot(hot, spread) * live[...]
        outside = jnp.where(in_use, jnp.where(inside > 0.5, 0.0, NEG), 0.0)
        k_marks[head] = outside.astype(bf16)
    for copy in copies:
        copy.wait()
    blank = jnp.zeros((HEAD_DIM, held.shape[2]), bf16)
    for head in range(heads):
        part = slice(head * HEAD_DIM, (head + 1) * HEAD_DIM)
        weights[head] = jnp.concatenate([held[0, part], blank, held[1, part], held[2, part]], axis=0)


def attend_rows(first, rows, q_ref, kv_ref, k_marks, raised_kept, out_kept):
    heads, length, width = kv_ref.shape
    chunk = rows
    left = lanes_of(length) < HEAD_DIM
    mixed = []
    for head in range(heads):
        keys = kv_ref[head].astype(f32)
        marked = jnp.where(left, keys, k_marks[head].astype(f32)).astype(bf16)
        values = jnp.where(left, 1.0, keys).astype(bf16)
        outs = []
        for start in range(0, rows, chunk):
            scores = dot_nt(q_ref[head, first + start : first + start + chunk], marked)
            raised = jnp.exp(scores - jnp.max(scores, axis=1, keepdims=True)).astype(bf16)
            raised_kept[head, pl.ds(start, chunk)] = raised
            total = dot(raised, values)
            share = 1.0 / total
            outs.append(jnp.where(left[:chunk], share, total * pltpu.roll(share, HEAD_DIM, 1)))
        outs = jnp.concatenate(outs, axis=0)
        out_kept[head] = outs
        mixed.append(outs[:, HEAD_DIM:])
    return jnp.concatenate(mixed, axis=1).astype(bf16)


def attend_kernel(
    layer, x0, x1, x2, x3, weights, bq, bv, q_marks, k_marks,
    q_out, kv_out, ob2, ob3, raised_kept, out_kept, ob_kept, x_kept,
):
    size = ob2.shape[0]
    for item, ref in enumerate((x0, x1, x2, x3)):
        x_kept[pl.ds(item * size, size)] = ref[...]
    x = stack_rows((x0, x1, x2, x3))
    heads = q_out.shape[0]
    blank_b = jnp.zeros((1, HEAD_DIM), f32)
    bias_q, bias_v = row(bq, layer), row(bv, layer)
    for head in range(heads):
        part = slice(head * HEAD_DIM, (head + 1) * HEAD_DIM)
        bias = jnp.concatenate([bias_q[:, part], blank_b, blank_b, bias_v[:, part]], axis=1)
        qkv = (dot_nt(x, weights[head]) + bias).astype(bf16)
        query = qkv[:, : 2 * HEAD_DIM].astype(f32) * (1.0 / math.sqrt(HEAD_DIM))
        q_out[head] = (query + q_marks[head].astype(f32)).astype(bf16)
        kv_out[head] = qkv[:, 2 * HEAD_DIM :]
    mixed = attend_rows(2 * size, 2 * size, q_out, kv_out, k_marks, raised_kept, out_kept)
    ob_kept[...] = mixed
    ob2[...] = mixed[:size]
    ob3[...] = mixed[size:]


def attend_near_kernel(
    q_in, kv_in, k_marks, ob0, ob1, raised_kept, out_kept, ob_kept, q_near, q_far, kv_kept
):
    size = ob0.shape[0]
    q_near[...] = q_in[:, : 2 * size]
    q_far[...] = q_in[:, 2 * size :]
    kv_kept[...] = kv_in[...]
    mixed = attend_rows(0, 2 * size, q_in, kv_in, k_marks, raised_kept, out_kept)
    ob_kept[...] = mixed
    ob0[...] = mixed[:size]
    ob1[...] = mixed[size:]


def entry_rows(layer, x, gain, shift):
    rows = x[...].astype(f32)
    if layer:
        rows = rows * row(gain, layer - 1) + row(shift, layer - 1)
    return rows


def with_scale(unit, scale):
    return jnp.concatenate([unit, jnp.broadcast_to(scale, (unit.shape[0], CLUSTER))], axis=1)


def mix_kernel(
    layer, ob0, ob1, ob2, ob3, w0, w1, w2, w3, x, b_out, gain1, shift1, gain2, shift2,
    normed, low, normed_kept, w_kept,
):
    total = entry_rows(layer, x, gain2, shift2) + row(b_out, layer)
    for item, (left, right) in enumerate(((ob0, w0), (ob1, w1), (ob2, w2), (ob3, w3))):
        w_kept[item] = right[...]
        total = total + dot(left[...], right[...])
    unit, root = normalise(total)
    normed[...] = unit
    normed_kept[...] = with_scale(unit, root)
    low[...] = (unit * row(gain1, layer) + row(shift1, layer)).astype(bf16)


def store_rows(value, refs):
    start = 0
    for ref in refs:
        ref[...] = value[start : start + ref.shape[0]].astype(ref.dtype)
        start += ref.shape[0]


def feed_kernel(layer, x, ups, biases, downs, x_kept, acts, slope, out):
    rows = x[...]
    x_kept[...] = rows
    total = 0.0
    units = acts[0].shape[1]
    for item in range(2):
        act, der = gelu_pair(dot(rows, ups[item][layer]) + row(biases[item], layer))
        act = act.astype(bf16)
        acts[item][...] = act
        slope[:, item * units : (item + 1) * units] = der.astype(bf16)
        total = total + dot(act, downs[item][layer])
    out[...] = total.astype(out.dtype)


def turn_weights_kernel(layer, ups, biases, downs, ups_t, biases_t, downs_t):
    for item in range(2):
        ups_t[item][...] = ups[item][layer].T
        downs_t[item][...] = downs[item][layer].T
        bias = row(biases[item], layer)
        biases_t[item][...] = jnp.broadcast_to(bias, (CLUSTER, bias.shape[1])).T


def feed_turned_kernel(x, ups_t, biases_t, downs_t, x_kept, acts, slope, out):
    rows = x[...]
    x_kept[...] = rows
    total = 0.0
    units, count = acts[0].shape
    for item in range(2):
        bias = jnp.concatenate([biases_t[item][...]] * (count // CLUSTER), axis=1)
        act, der = gelu_pair(dot_nt(ups_t[item][...], rows) + bias)
        act = act.astype(bf16)
        acts[item][...] = act
        slope[item * units : (item + 1) * units, :] = der.astype(bf16)
        total = total + dot(downs_t[item][...], act)
    out[...] = total.T.astype(out.dtype)


def second_rows(layer, normed1, gain1, shift1, own, far, b_down):
    rows = normed1[...] * row(gain1, layer) + row(shift1, layer)
    return rows + own[...] + far[...].astype(f32) + row(b_down, layer)


def close_kernel(
    layer, normed1, gain1, shift1, own, far, b_down, gain2, shift2, normed, low, normed_kept
):
    unit, root = normalise(
        second_rows(layer, normed1, gain1, shift1, own, far, b_down)
    )
    normed[...] = unit
    normed_kept[...] = with_scale(unit, root)
    low[...] = (unit * row(gain2, layer) + row(shift2, layer)).astype(bf16)


def turn_kernel(
    layer, normed1, gain1, shift1, own, far, b_down, gain2, shift2, grad,
    result, low, sums, d_second,
):
    unit, root = normalise(
        second_rows(layer, normed1, gain1, shift1, own, far, b_down)
    )
    gain = row(gain2, layer)
    result[...] = unit * gain + row(shift2, layer)
    back = normalise_back(grad[...], gain, unit, root)
    d_second[...] = back
    low[...] = back.astype(bf16)
    store_sums(sums, back, grad[...] * unit, grad[...])


def unit_and_scale(kept, width):
    both = kept[...]
    return both[:, :width], both[:, width : width + 1]


def open_back_kernel(layer, normed2, base, own, core, far, gain2, low, sums, d_second):
    rest = own[...] + core[...].astype(f32) + far[...].astype(f32)
    grad = base[...] + rest
    unit, root = unit_and_scale(normed2, grad.shape[1])
    back = normalise_back(grad, row(gain2, layer), unit, root)
    d_second[...] = back
    low[...] = back.astype(bf16)
    store_sums(sums, back, grad * unit, grad)


def feed_back_kernel(layer, grad, ups, downs, slope, pres, out):
    rows = grad[...]
    total = 0.0
    units = pres[0].shape[1]
    for item in range(2):
        der = slope[:, item * units : (item + 1) * units].astype(f32)
        pre = (dot_nt(rows, downs[item][layer]) * der).astype(bf16)
        pres[item][...] = pre
        total = total + dot_nt(pre, ups[item][layer])
    out[...] = total.astype(out.dtype)


def feed_back_turned_kernel(layer, grad, ups, downs, slope, pres, out):
    rows = grad[...]
    total = 0.0
    units = pres[0].shape[0]
    for item in range(2):
        der = slope[item * units : (item + 1) * units, :].astype(f32)
        pre = (dot_nt(downs[item][layer], rows) * der).astype(bf16)
        pres[item][...] = pre
        total = total + dot(ups[item][layer], pre)
    out[...] = total.T.astype(out.dtype)


def mix_back_kernel(
    layer, base, normed1, weights, own, far, gain1, low, d0, d1, d2, d3, sums, d_first
):
    grad = base[...] + own[...] + far[...].astype(f32)
    unit, root = unit_and_scale(normed1, grad.shape[1])
    back = normalise_back(grad, row(gain1, layer), unit, root)
    d_first[...] = back
    small = back.astype(bf16)
    low[...] = small
    for item, out in enumerate((d0, d1, d2, d3)):
        out[...] = dot_nt(small, weights.piece(item)[0]).astype(bf16)
    store_sums(sums, back, grad * unit, grad)


def close_back_kernel(base, own, core, far, out):
    out[...] = base[...] + own[...] + core[...].astype(f32) + far[...].astype(f32)


def attend_back_rows(refs, q_kept, kv_kept, out_kept, raised_kept):
    d_mixed = stack_rows(refs)
    rows = d_mixed.shape[0]
    heads, length, width = kv_kept.shape
    chunk = rows
    steps = rows // chunk
    key_lanes, lanes = lanes_of(length), lanes_of(rows)[:, :HEAD_DIM]
    d_q, d_k, d_v = [], [], []
    for head in range(heads):
        part = slice(head * HEAD_DIM, (head + 1) * HEAD_DIM)
        keys = kv_kept.piece(head)[0]
        both = out_kept.piece(head)[0]
        share, out = both[:, :HEAD_DIM], both[:, HEAD_DIM:]
        grad = (d_mixed[:, part].astype(f32) * share).astype(bf16).astype(f32)
        inner = jnp.sum(grad * out, axis=1, keepdims=True)
        high = inner.astype(bf16).astype(f32)
        middle = (inner - high).astype(bf16).astype(f32)
        low = inner - high - middle
        terms = jnp.where(
            lanes == 0, -high, jnp.where(lanes == 1, -middle, jnp.where(lanes == 2, -low, 0.0))
        )
        grad = jnp.concatenate([terms, grad], axis=1).astype(bf16)
        values = jnp.where(
            key_lanes < 3, 1.0, jnp.where(key_lanes < HEAD_DIM, 0.0, keys.astype(f32))
        ).astype(bf16)
        d_score, raised = [], []
        for item in range(steps):
            d_prob = dot_nt(grad[item * chunk : (item + 1) * chunk], values)
            raised.append(raised_kept.piece(head * steps + item))
            d_score.append((raised[-1].astype(f32) * d_prob).astype(bf16))
        d_score = jnp.concatenate(d_score, axis=0)
        raised = jnp.concatenate(raised, axis=0)
        query = q_kept.piece(head)[0]
        d_q.append(dot(d_score, keys)[:, :HEAD_DIM] * (1.0 / math.sqrt(HEAD_DIM)))
        d_k.append(dot(query.T[:HEAD_DIM], d_score))
        d_v.append(dot(grad.T[HEAD_DIM:], raised))
    return (
        jnp.concatenate(d_q, axis=1).astype(bf16),
        jnp.concatenate(d_k, axis=0),
        jnp.concatenate(d_v, axis=0),
    )


def attend_back_near_kernel(kv_kept, out_kept, raised_kept, q_kept, d0, d1, d_query, d_k, d_v):
    d_query[...], d_k[...], d_v[...] = attend_back_rows((d0, d1), q_kept, kv_kept, out_kept, raised_kept)


def attend_back_kernel(
    layer, kv_kept, out_kept, raised_kept, q_kept, d2, d3, near_q, near_k, near_v, wq, wk, wv,
    d_query, d_key, d_value, own, core, chip, cross, sums,
):
    d_q, d_k, d_v = attend_back_rows((d2, d3), q_kept, kv_kept, out_kept, raised_kept)
    d_q = jnp.concatenate([near_q[...], d_q], axis=0)
    d_k, d_v = ((item + near[...]).T.astype(bf16) for item, near in ((d_k, near_k), (d_v, near_v)))
    d_query[...] = d_q
    d_key[...] = d_k
    d_value[...] = d_v
    store_sums(sums, jnp.concatenate([d_q.astype(f32), d_v.astype(f32)], axis=1))
    store_rows(dot(d_q, wq[layer]) + dot(d_k, wk[layer]) + dot(d_v, wv[layer]), (own, core, chip, cross))


def store_pieces(place, grad, outs, order):
    if len(outs) == 1:
        outs[0][...] = grad.astype(bf16)
        return
    keep, send = outs
    bits = len(order)
    pieces = 1 << bits
    size = grad.shape[0] // pieces
    for piece in range(pieces):
        rel = place ^ piece
        index = 0
        for step, bit in enumerate(order[1:]):
            index = index + (((rel >> bit) & 1) << (bits - 2 - step))
        value = grad[piece * size : (piece + 1) * size].astype(bf16)
        leaves = (rel >> order[0]) & 1

        @pl.when(leaves == 0)
        def _(value=value, index=index, keep=keep):
            keep[index, :size] = value

        @pl.when(leaves == 1)
        def _(value=value, index=index, send=send):
            send[index, :size] = value


def split_refs(refs, *counts):
    parts = []
    for count in counts:
        parts.append(refs[:count])
        refs = refs[count:]
    return parts


def dot_tt(left, right):
    return lax.dot_general(left, right, (((0,), (1,)), ((), ())), preferred_element_type=f32)


def stack_cols(refs):
    return jnp.concatenate([ref[...] for ref in refs], axis=1)


def feed_grad_kernel(orders, spot, *refs):
    size = (len(refs) - 17) // 2
    pre, x, grad, act, one, two, (sums,) = split_refs(refs, 4, 4, 4, 4, size, size, 1)
    pre_near, pre_far = stack_rows(pre[:2]), stack_cols(pre[2:])
    up = dot_tn(stack_rows(x[:2]), pre_near) + dot_tt(stack_rows(x[2:]), pre_far)
    store_pieces(spot[1], up, one, orders[0])
    down = dot_tn(stack_rows(grad[:2]), stack_rows(act[:2])) + dot_tt(stack_rows(grad[2:]), stack_cols(act[2:]))
    store_pieces(spot[1], down, two, orders[1])
    ones = jnp.ones((sums.shape[0], pre_near.shape[0]), bf16)
    sums[...] = dot(ones, pre_near) + dot_nt(ones, pre_far)


def fold_small(rows):
    half = rows.shape[1] // 2
    return jnp.concatenate([rows[:, :half], rows[:, half:]], axis=0).astype(bf16)


def attend_grad_kernel(orders, terms, spot, *refs):
    small, refs = refs[:terms], refs[terms:]
    size = (len(refs) - 10) // 2
    x, (dq, dk, dv), grad, mixed, one, two = split_refs(refs, 1, 3, 4, 2, size, size)
    if terms and size == 2:
        below = fold_small(functools.reduce(jnp.add, [ref[...] for ref in small]))
        for ref in one:
            for item in range(ref.shape[0]):
                ref[item, ref.shape[1] - below.shape[0] :] = below
    x = x[0][...]
    right = jnp.concatenate([dq[...], dk[...]], axis=1)
    store_pieces(spot[1], dot_tn(x, right), one, orders[0])
    out = dot_tn(stack_rows(grad), stack_rows(mixed))
    store_pieces(spot[1], jnp.concatenate([dot_tn(x, dv[...]), out], axis=1), two, orders[1])


def whole_grads(spots, keeps, gots):
    return [
        keep[...].astype(f32) + gots[spot][:, :rows, start : start + cols].astype(f32)
        for keep, (spot, start, cols, rows) in zip(keeps, spots)
    ]


def halve_kernel(spots, groups, count, *refs):
    keeps, gots, rest = split_refs(refs, len(spots), count, len(refs) - len(spots) - count)
    held = [item.astype(bf16) for item in whole_grads(spots, keeps, gots)]
    for item, ref in zip(held, rest):
        ref[...] = item[: ref.shape[0]]
    for group, ref in zip(groups, rest[len(spots) :]):
        leaving = []
        for spot in group:
            item = held[spot][ref.shape[0] :]
            missing = ref.shape[1] - item.shape[1]
            if missing:
                item = jnp.concatenate([item, jnp.zeros((item.shape[0], missing, item.shape[2]), bf16)], axis=1)
            leaving.append(item)
        ref[...] = jnp.concatenate(leaving, axis=2)


def place_rows(head, piece, groups=4):
    return jnp.concatenate([jnp.where(head == item, piece, 0.0) for item in range(groups)], axis=1)


def collect_kernel(spot, *refs):
    rows = []
    for layer in range(len(refs) // 4):
        mix, feed, up, qv = refs[4 * layer : 4 * layer + 4]
        cols = qv.shape[1] // 2
        rows += [place_rows(spot[2], qv[:1, :cols]), place_rows(spot[2], qv[:1, cols:])]
        rows += [mix[:3, :], feed[:3, :]]
        rows += [jnp.where(spot[2] == item, up[:1, :], 0.0) for item in range(4)]
    refs[-1][...] = jnp.concatenate(rows, axis=0)


def assemble_kernel(spots, count, depth, *refs):
    keeps, gots, refs = split_refs(refs, len(spots), count, len(refs) - len(spots) - count)
    grads = whole_grads(spots, keeps, gots)
    g_q, g_k, g_v, g_o, g_up, g_down, *vectors, s_bu = refs
    own, cols = g_q.shape[1:]
    below = grads[2][0, own:]
    half = below.shape[0] // 2
    small = jnp.concatenate([below[:half], below[half:]], axis=1)
    model = small.shape[1]
    for layer in range(depth):
        up, down, one, two = grads[4 * layer : 4 * layer + 4]
        g_up[layer] = up[0]
        g_down[layer] = down[0]
        g_q[layer] = one[0, :own, :cols]
        g_k[layer] = one[0, :own, cols:]
        g_v[layer] = two[0, :, :cols]
        g_o[layer] = two[0, :, cols:].T
        rows = small[12 * layer : 12 * layer + 12]
        for item, ref in enumerate(vectors):
            ref[layer : layer + 1, :] = rows[item : item + 1, :]
        for item in range(4):
            s_bu[layer : layer + 1, item * model : (item + 1) * model] = rows[8 + item : 9 + item, :]


class Scalar:
    def __init__(self, array):
        self.array = array


class Far:
    def __init__(self, array):
        self.array = array


class Stay:
    def __init__(self, shape, kind):
        self.shape, self.kind = shape, kind


class View:
    def __init__(self, array, pieces=1):
        self.array, self.pieces = array, pieces


def call(kernel, name, ins, outs, vmem, scratch=()):
    arrays, specs, pieces = [], [], {}
    for spot, item in enumerate(ins):
        space = pltpu.VMEM
        if isinstance(item, Scalar):
            space = pltpu.SMEM
            arrays.append(item.array)
        elif isinstance(item, Far):
            space = pltpu.HBM
            arrays.append(pltpu.with_memory_space_constraint(item.array, pltpu.HBM))
        elif isinstance(item, View):
            arrays.append(pltpu.with_memory_space_constraint(item.array, pltpu.VMEM))
            pieces[spot] = item.pieces
        else:
            arrays.append(item)
        specs.append(pl.BlockSpec(memory_space=space))
    shapes = []
    for item in outs:
        if isinstance(item, Stay):
            shapes.append(pltpu.VMEM(item.shape, item.kind))
        else:
            shapes.append(jax.ShapeDtypeStruct(*item))

    def wrapped(*refs):
        kernel(*(Viewed(ref, pieces[spot]) if spot in pieces else ref for spot, ref in enumerate(refs)))

    return pl.pallas_call(
        wrapped,
        name=name,
        grid=(1,),
        out_shape=shapes,
        in_specs=specs,
        out_specs=[pl.BlockSpec(memory_space=pltpu.VMEM)] * len(shapes),
        scratch_shapes=scratch,
        compiler_params=pltpu.CompilerParams(vmem_limit_bytes=int(vmem * MIB)),
        cost_estimate=pl.CostEstimate(flops=int(GIGA.get(name, 0) * 1e9) + 1, bytes_accessed=1, transcendentals=0),
    )(*arrays)


def grad_outs(rows, cols, order, extra=0):
    pieces = 1 << len(order)
    if (rows // pieces) % 16:
        return [((rows, cols), bf16)]
    return [((pieces // 2, rows // pieces + extra, cols), bf16)] * 2


def start_halving(parts, place, orders, small=()):
    half = len(parts) // 2
    if half == 1:
        pairs = []
        for part, order in zip(parts, orders):
            pieces = 1 << len(order)
            whole = part.reshape(pieces, -1, part.shape[1])
            ranks = []
            for spot in range(pieces):
                ranks.append(
                    sum(((spot >> (len(order) - 1 - step)) & 1) << bit for step, bit in enumerate(order))
                )
            whole = jnp.take(whole, jnp.array(ranks, jnp.int32) ^ place, axis=0)
            if small and not pairs:
                below = fold_small(functools.reduce(jnp.add, small))
                below = jnp.broadcast_to(below, (pieces,) + below.shape)
                whole = jnp.concatenate([whole, below], axis=1)
            pairs.append((whole[: pieces // 2], whole[pieces // 2 :]))
    else:
        pairs = (parts[:2], parts[2:])
    return Halving(*zip(*pairs), orders)


def body(
    hidden_in, w_query, w_key, w_value, b_query, b_value, w_out, b_out, ln1_gain, ln1_bias,
    w_up, b_up, w_down, b_down, ln2_gain, ln2_bias, token_mask, query_order, key_order,
    out_cotangent,
):
    depth, model, cols = w_query.shape
    rows = hidden_in.shape[0]
    units = w_up.shape[2]
    pack = token_mask.shape[0]
    heads = query_order.shape[1]
    head = lax.axis_index("head").astype(jnp.int32)
    groups = lax.axis_size("head")
    place = lax.axis_index("dp").astype(jnp.int32)
    spot = Scalar(jnp.stack([head * rows, place, head]))
    bits = lax.axis_size("dp").bit_length() - 1
    order_one = tuple(range(bits))
    order_two = order_one[:2][::-1] + order_one[2:]
    orders = (order_one, order_two)
    w_query, w_key, w_value = (item.transpose(0, 2, 1) for item in (w_query, w_key, w_value))
    q_order, k_order = query_order.transpose(1, 0, 2), key_order.transpose(1, 0, 2)

    wide = (rows, model)
    dense = 2 * rows * model
    wide_low, wide_full = (wide, bf16), (wide, f32)

    low = hidden_in
    chip, core = swap(low, "head", 2), swap(low, "head", 1)
    around = token_mask.reshape(groups, rows)
    live = jnp.concatenate(
        [lax.dynamic_index_in_dim(around, head ^ item, 0, keepdims=False) for item in range(groups)]
    )
    live = live.astype(f32).reshape(pack, 1)

    entry = hidden_in
    kept = []
    pair = 2 * rows
    two = 2 * HEAD_DIM
    kept_rows = [Stay((heads, pair, pack), bf16), Stay((heads, pair, two), f32), Stay((pair, cols), bf16)]
    other_units = [swap(item, "head", 1) for item in (w_up, b_up, w_down)]
    for layer in range(depth):
        *marks, weights = call(
            functools.partial(cluster_kernel, layer), "clusters",
            [spot, q_order, k_order, live, Far(w_query), Far(w_key), Far(w_value)],
            [((heads, pack, two), bf16)] * 2 + [((heads, 2 * two, model), bf16)], vmem=7,
            scratch=[pltpu.VMEM((3, cols, model), bf16), pltpu.SemaphoreType.DMA((3,))],
        )
        chip = tie(chip, weights)
        cross = swap(chip, "head", 1)
        if not layer:
            cross, other_units = tie((cross, other_units))
            ups, biases, downs = zip((w_up, b_up, w_down), other_units)
        w_mine = tie(w_out[layer], cross)
        w_core, w_chip = swap(w_mine, "head", 1), swap(w_mine, "head", 2)
        q_all, kv_all, ob2, ob3, raised_far, out_far, ob_far, x_kept = call(
            functools.partial(attend_kernel, layer), "attend",
            [low, core, chip, cross, weights, b_query, b_value, *marks],
            [((heads, pack, two), bf16)] * 2 + [((rows, cols), bf16)] * 2 + kept_rows
            + [Stay((pack, model), bf16)], vmem=6,
        )
        got2, got3 = swap(ob2, "head", 2), swap(ob3, "head", 3)
        ob0, ob1, raised_near, out_near, ob_near, *q_kept, kv_kept = call(
            attend_near_kernel, "attend_near", [q_all, kv_all, marks[1]],
            [((rows, cols), bf16)] * 2 + kept_rows + [Stay((heads, pair, two), bf16)] * 2
            + [Stay((heads, pack, two), bf16)], vmem=4,
        )
        got1 = swap(ob1, "head", 1)
        got1, got2, got3, w_core, w_chip = tie((got1, got2, got3, w_core, w_chip))
        w_cross = swap(w_chip, "head", 1)
        outs = (w_mine, w_core, w_chip, w_cross)
        got = [ob0, got1, got2, got3]
        normed1, low1, normed1_kept, w_kept = call(
            functools.partial(mix_kernel, layer), "mix",
            [*got, *outs, entry, b_out, ln1_gain, ln1_bias, ln2_gain, ln2_bias],
            [wide_full, wide_low, Stay((rows, model + CLUSTER), f32), Stay((4, cols, model), bf16)], vmem=4,
        )

        def feed(block, kind):
            def kernel(x, up, up2, bias, bias2, down, down2, x_kept, act, act2, slope, out):
                feed_kernel(layer, x, (up, up2), (bias, bias2), (down, down2), x_kept, (act, act2), slope, out)

            return call(
                kernel, "feed", [block, *ups, *biases, *downs],
                [Stay(wide, bf16), Stay((rows, units), bf16), ((rows, units), bf16),
                 Stay((rows, 2 * units), bf16), (wide, kind)], vmem=5.5,
            )

        def turn_weights(up, up2, bias, bias2, down, down2, *outs):
            turn_weights_kernel(layer, (up, up2), (bias, bias2), (down, down2), outs[:2], outs[2:4], outs[4:6])
            for out in outs[6:]:
                out[...] = down2[...]

        def feed_turned(x, up, up2, bias, bias2, down, down2, x_kept, act, act2, slope, out):
            feed_turned_kernel(x, (up, up2), (bias, bias2), (down, down2), x_kept, (act, act2), slope, out)

        chip = swap(low1, "head", 2)
        turned = call(
            turn_weights, "turn_weights", [*tie([*ups, *biases, *downs], low1)],
            [((units, model), bf16)] * 2 + [((units, CLUSTER), f32)] * 2 + [((model, units), bf16)] * 2
            + [Stay(w_down.shape, bf16)] * (not layer), vmem=4 + 3 * (not layer),
        )
        if not layer:
            *turned, other_down = turned
            downs = (w_down, other_down)
        h_own, act_own, act_core, slope_own, own_term = feed(low1, f32)
        chip = tie(chip, own_term, turned)
        h_chip, act_chip, act_cross, slope_chip, far_term = call(
            feed_turned, "feed_turned", [chip, *turned],
            [Stay(wide, bf16), Stay((units, rows), bf16), ((units, rows), bf16), Stay((2 * units, rows), bf16),
             wide_low], vmem=5.5,
        )
        far = swap(far_term, "head", 2)
        away = [swap(item, "head", 1) for item in tie((h_own, act_core, h_chip, act_cross), far_term)]
        ends = [normed1, ln1_gain, ln1_bias, own_term, far, b_down, ln2_gain, ln2_bias]
        kept.append(
            (x_kept, (kv_kept, q_kept), ((out_near, raised_near), (out_far, raised_far)), (ob_near, ob_far),
             normed1_kept, w_kept, (slope_own, slope_chip))
        )
        if layer + 1 < depth:
            entry, low, normed2_kept = call(
                functools.partial(close_kernel, layer), "close", ends,
                [wide_full, wide_low, Stay((rows, model + CLUSTER), f32)], vmem=4,
            )
            kept[-1] += (normed2_kept,)
            low, away = tie((low, away))
            chip, core = swap(low, "head", 2), swap(low, "head", 1)
        else:
            result, low, sums2, d_second = call(
                functools.partial(turn_kernel, layer), "turn", ends + [out_cotangent],
                [wide_full, wide_low, ((8, model), f32), Stay(*wide_full)], vmem=4,
            )
            low, away = tie((low, away))
        h_core, act_core, h_cross, act_cross = away
        kept[-1] += ((h_own, h_core, h_chip, h_cross), (act_own, act_core, act_chip, act_cross))

    feed_sums = attend_sums = None
    grads, small = [None] * depth, [None] * depth
    pieces = heads
    for layer in reversed(range(depth)):
        x_kept, (kv_kept, q_kept), (near, far_rows), obs, normed1, w_kept, slopes, *_, h_kept, acts = kept[layer]
        above = feed_sums is not None

        def feed_back(grad, up, up2, down, down2, slope, pre, pre2, out):
            feed_back_kernel(layer, grad, (up, up2), (down, down2), slope, (pre, pre2), out)

        def feed_back_turned(grad, up, up2, down, down2, slope, pre, pre2, out):
            feed_back_turned_kernel(layer, grad, (up, up2), (down, down2), slope, (pre, pre2), out)

        chip, g_core = swap(low, "head", 2), swap(low, "head", 1)
        pre_own, pre_core, own_term = call(
            feed_back, "feed_back", [low, *ups, *downs, View(slopes[0])],
            [((rows, units), bf16)] * 2 + [wide_full], vmem=4,
        )
        chip, g_core = join((chip, g_core), [feed_sums, attend_sums] if above else [], own_term)
        g_cross = swap(chip, "head", 1)
        pre_chip, pre_cross, far_term = call(
            feed_back_turned, "feed_back_turned", [chip, *ups, *downs, View(slopes[1])],
            [((units, rows), bf16)] * 2 + [wide_low], vmem=5,
        )
        far_term, g_cross = tie((far_term, g_cross))
        far = swap(far_term, "head", 2)
        pre_core, pre_cross = [swap(item, "head", 1) for item in tie((pre_core, pre_cross), far_term)]
        g_blocks = (low, g_core, chip, g_cross)
        added = ()
        if above and attend_sums.more():
            added = advance([attend_sums], far_term)
        *parts, up_sums = call(
            functools.partial(feed_grad_kernel, orders), "feed_grad",
            [spot, *tie((pre_own, pre_core, pre_chip, pre_cross), added), *map(View, h_kept), *g_blocks,
             *map(View, acts)],
            grad_outs(model, units, order_one) + grad_outs(model, units, order_two) + [((8, units), f32)],
            vmem=9,
        )
        far = tie(far, parts)
        if above:
            parts = join(parts, [attend_sums])
        waiting = attend_sums
        feed_sums = start_halving(parts, place, orders)
        low, *d_obs, sums1, d_first = call(
            functools.partial(mix_back_kernel, layer), "mix_back",
            [View(d_second), View(normed1), View(w_kept, 4), own_term, far, ln1_gain],
            [wide_low] + [((rows, cols), bf16)] * 4 + [((8, model), f32), Stay(*wide_full)], vmem=4,
        )
        got = [d_obs[0]] + [swap(d_obs[item], "head", item) for item in (1, 2, 3)]

        def kept_part(part, start):
            out, raised = part
            raised = View(raised.reshape(heads * pair, pack), pieces)
            return [
                View(kv_kept, heads), View(out, heads), raised,
                View(q_kept[start // pair], heads),
            ]

        near_q, near_k, near_v = call(
            attend_back_near_kernel, "attend_back_near",
            kept_part(near, 0) + got[:2],
            [((pair, cols), bf16)] + [((cols, pack), f32)] * 2, vmem=4.5,
        )
        got = tie(got, near_q)
        others = [item for item in (feed_sums, waiting) if item]
        got = join(got, others)
        if any(item.more() for item in others):
            got = tie(got, advance(others))
        low = tie(low, got)
        chip, core = swap(low, "head", 2), swap(low, "head", 1)
        d_q, d_k, d_v, own_term, core_term, chip_term, cross_term, sums_qv = call(
            functools.partial(attend_back_kernel, layer), "attend_back",
            kept_part(far_rows, pair)
            + [got[2], got[3], near_q, near_k, near_v, w_query, w_key, w_value],
            [((pack, cols), bf16)] * 3 + [wide_full, wide_low, wide_full, wide_low]
            + [((8, 2 * cols), f32)], vmem=7.5,
        )
        others = [item for item in (feed_sums, waiting) if item]
        chip, core, core_term, cross_term = join((chip, core, core_term, cross_term), others)
        got_chip, got_core = swap(cross_term, "head", 1), swap(core_term, "head", 1)
        cross = swap(chip, "head", 1)
        small[layer] = [sums1, sums2, up_sums, sums_qv]
        last = ()
        if not layer:
            mine = call(
                collect_kernel, "collect", [spot] + [item for part in small for item in part],
                [((12 * depth, model), f32)], vmem=3,
            )[0]
            last = (mine, swap(mine, "head", 1))
        got_chip, got_core, last = tie((got_chip, got_core, last))
        merged = (chip_term + got_chip.astype(f32)).astype(bf16)
        if not layer:
            total = last[0] + last[1]
            last = (total, swap(total, "head", 2))
        a_blocks = (low, core, chip, cross)
        added = ()
        if any(item.more() for item in others):
            added = advance(others, merged, apart=bool(layer))
        if not layer:
            merged, last = tie((merged, last), added)
        far = swap(merged, "head", 2)
        parts = call(
            functools.partial(attend_grad_kernel, orders, len(last)), "attend_grad",
            [spot, *last, View(x_kept), *tie((d_q, d_k, d_v), merged, added), *a_blocks, *map(View, obs)],
            grad_outs(model, 2 * cols, order_one, 0 if layer else 24 * depth)
            + grad_outs(model, 2 * cols, order_two), vmem=6,
        )
        if layer:
            far = land(far, [feed_sums.slots[0][0]], parts)
        attend_sums = start_halving(parts, place, orders, last)
        grads[layer] = (feed_sums, attend_sums)
        if layer:
            low, sums2, d_second = call(
                functools.partial(open_back_kernel, layer - 1), "open_back",
                [View(kept[layer - 1][-3]), View(d_first), own_term, got_core, far, ln2_gain],
                [wide_low, ((8, model), f32), Stay(*wide_full)], vmem=4,
            )

    far = join(far, [feed_sums])
    d_rows = call(close_back_kernel, "close_back", [View(d_first), own_term, got_core, far], [wide_full], vmem=4)[0]
    d_rows = join(d_rows, [attend_sums])
    while attend_sums.more():
        advance([attend_sums], d_rows)
    items = [item for layer in grads for item in layer]
    while any(item.more() for item in items):
        advance(items)
    ends = [keep for item in items for keep in item.keeps] + [item.got for item in transfers_of(items)]
    own = ends[0].shape[1]
    g_q, g_k, g_v, g_o, g_up, g_down, s_bq, s_bv, s_bo, s_g1, s_n1, s_bd, s_g2, s_n2, s_bu = call(
        functools.partial(assemble_kernel, spots_of(items), len(transfers_of(items)), depth), "assemble", ends,
        [((depth, own, cols), f32)] * 3 + [((depth, cols, own), f32)] + [((depth, own, units), f32)] * 2
        + [((depth, model), f32)] * 8 + [((depth, groups * units), f32)], vmem=8,
    )
    return (
        result, d_rows, g_q, g_k, g_v, s_bq, s_bv, g_o, s_bo, s_g1, s_n1, g_up,
        s_bu, g_down.transpose(0, 2, 1), s_bd, s_g2, s_n2,
    )


def solution(mesh):
    split = P(("dp", "head"), None)
    column, line = P(None, None, "head"), P(None, "head", None)
    placed = (
        split, column, column, column, P(None, "head"), P(None, "head"), line, P(), P(), P(),
        column, P(None, "head"), line, P(), P(), P(),
        P("dp"), P(None, "head", "dp"), P(None, "head", "dp"), split,
    )
    by_rows, by_cols = P(None, "dp", "head"), P(None, "head", "dp")
    results = (
        split, split, by_rows, by_rows, by_rows, P(), P(), by_cols, P(), P(), P(), by_rows, P(),
        by_cols, P(), P(), P(),
    )
    return jax.shard_map(body, mesh=mesh, in_specs=placed, out_specs=results, check_vma=False)
```

```python
import functools
import math

import jax
import jax.numpy as jnp
from jax import lax
from jax.experimental import pallas as pl
from jax.experimental.pallas import tpu as pltpu
from jax.sharding import PartitionSpec as P

CLUSTER = 128
HEAD_DIM = 64
EPS = 1e-12
NEG = -1e30
MIB = 1024 * 1024
GIGA = {"attend_back_near": 3, "close_back": 3}

f32 = jnp.float32
bf16 = jnp.bfloat16


def swap(array, axis, bit):
    size = lax.axis_size(axis)
    return lax.ppermute(array, axis, [(item, item ^ bit) for item in range(size)])


def tie(value, *earlier):
    return lax.optimization_barrier((value, earlier))[0]


class Transfer:
    def __init__(self, send, bit):
        self.got = swap(send, "dp", 1 << bit)


class Halving:
    def __init__(self, keeps, sends, orders):
        self.keeps, self.orders = list(keeps), [list(order) for order in orders]
        self.slots = [(Transfer(send, order.pop(0)), 0) for send, order in zip(sends, self.orders)]

    def more(self):
        return bool(self.orders[0])


def transfers_of(items):
    found = []
    for item in items:
        for transfer, _ in item.slots:
            if transfer not in found:
                found.append(transfer)
    return found


def spots_of(items):
    found = transfers_of(items)
    return [
        (found.index(transfer), start, keep.shape[2], keep.shape[1])
        for item in items
        for keep, (transfer, start) in zip(item.keeps, item.slots)
    ]


def join(value, items, *earlier):
    return land(value, transfers_of(items), *earlier)


def land(value, found, *earlier):
    value, gots, _ = lax.optimization_barrier((value, [item.got for item in found], earlier))
    for item, got in zip(found, gots):
        item.got = got
    return value


def advance(items, *earlier, apart=False):
    items = [item for item in items if item.more()]
    found = transfers_of(items)
    keeps = [keep for item in items for keep in item.keeps]
    keeps, gots = tie((keeps, [item.got for item in found]), *earlier)
    outs = [((keep.shape[0] // 2,) + keep.shape[1:], bf16) for keep in keeps]
    groups = {}
    bits = [order.pop(0) for item in items for order in item.orders]
    for spot, (bit, out) in enumerate(zip(bits, outs)):
        groups.setdefault((bit, out[0][0], spot if apart else 0), []).append(spot)
    sends = []
    for group in groups.values():
        cols = sum(outs[spot][0][2] for spot in group)
        rows = max(outs[spot][0][1] for spot in group)
        sends.append(((outs[group[0]][0][0], rows, cols), bf16))
    parts = call(
        functools.partial(halve_kernel, spots_of(items), list(groups.values()), len(gots)), "halve",
        [*keeps, *gots], outs + sends, vmem=8,
    )
    slots = [None] * len(keeps)
    for (bit, *_), group, send in zip(groups, groups.values(), parts[len(keeps) :]):
        transfer, start = Transfer(send, bit), 0
        for spot in group:
            slots[spot] = (transfer, start)
            start += outs[spot][0][2]
    start = 0
    for item in items:
        stop = start + len(item.keeps)
        item.keeps, item.slots = parts[start:stop], slots[start:stop]
        start = stop
    return parts


def dot(left, right):
    return jnp.dot(left, right, preferred_element_type=f32)


def dot_nt(left, right):
    return lax.dot_general(left, right, (((1,), (1,)), ((), ())), preferred_element_type=f32)


def dot_tn(left, right):
    return lax.dot_general(left, right, (((0,), (0,)), ((), ())), preferred_element_type=f32)


def row(ref, layer):
    return ref[layer : layer + 1, :]


def normalise(rows):
    centre = rows - jnp.mean(rows, axis=-1, keepdims=True)
    spread = jnp.mean(centre * centre, axis=-1, keepdims=True)
    scale = lax.rsqrt(spread + EPS)
    return centre * scale, scale


def normalise_back(grad, gain, normed, scale):
    part = grad * gain
    mean_one = jnp.mean(part, axis=-1, keepdims=True)
    mean_two = jnp.mean(part * normed, axis=-1, keepdims=True)
    return (part - mean_one - normed * mean_two) * scale


def store_sums(ref, *arrays):
    rows = [jnp.sum(item, axis=0, keepdims=True) for item in arrays]
    rows.append(jnp.zeros((ref.shape[0] - len(rows), ref.shape[1]), f32))
    ref[...] = jnp.concatenate(rows, axis=0)


def gelu_pair(values):
    bell = jnp.exp(values * values * -0.5)
    t = 1.0 / (1.0 + (0.3275911 * math.sqrt(0.5)) * jnp.abs(values))
    poly = 0.5 * 1.061405429
    for factor in (-1.453152027, 1.421413741, -0.284496736, 0.254829592):
        poly = poly * t + 0.5 * factor
    tail = poly * t * bell
    cdf = jnp.where(values >= 0.0, 1.0 - tail, tail)
    return values * cdf, cdf + values * bell * (1.0 / math.sqrt(2.0 * math.pi))


def stack_rows(refs):
    return jnp.concatenate([ref[...] for ref in refs], axis=0)


def head_cols(array, head):
    return array[:, head * HEAD_DIM : (head + 1) * HEAD_DIM]


def lanes_of(rows):
    return lax.broadcasted_iota(jnp.int32, (rows, 2 * HEAD_DIM), 1)


class Viewed:
    def __init__(self, source, pieces):
        self.source, self.shape, self.size = source, source.shape, source.shape[0] // pieces

    def piece(self, item):
        return self.source[item * self.size : (item + 1) * self.size]

    def __getitem__(self, index):
        return self.source[index]


def cluster_kernel(layer, spot, q_order, k_order, live, wq, wk, wv, q_marks, k_marks, weights, held, sems):
    heads, length, width = q_marks.shape
    copies = [
        pltpu.make_async_copy(source.at[layer], held.at[item], sems.at[item])
        for item, source in enumerate((wq, wk, wv))
    ]
    for copy in copies:
        copy.start()
    count = length // CLUSTER
    lines = lax.broadcasted_iota(jnp.int32, (length, length), 0)
    spread_line = lax.broadcasted_iota(jnp.int32, (length, width), 0) // CLUSTER + HEAD_DIM
    lanes = lanes_of(length)
    spread = jnp.where(spread_line == lanes, 1.0, 0.0).astype(bf16)
    in_use = jnp.logical_and(lanes >= HEAD_DIM, lanes < HEAD_DIM + count)
    for head in range(heads):
        order = q_order[head, layer : layer + 1, :] ^ spot[0]
        hot = jnp.where(order == lines, 1.0, 0.0).astype(bf16)
        q_marks[head] = dot(hot, spread).astype(bf16)
        order = k_order[head, layer : layer + 1, :] ^ spot[0]
        hot = jnp.where(order == lines, 1.0, 0.0).astype(bf16)
        inside = dot(hot, spread) * live[...]
        outside = jnp.where(in_use, jnp.where(inside > 0.5, 0.0, NEG), 0.0)
        k_marks[head] = outside.astype(bf16)
    for copy in copies:
        copy.wait()
    blank = jnp.zeros((HEAD_DIM, held.shape[2]), bf16)
    for head in range(heads):
        part = slice(head * HEAD_DIM, (head + 1) * HEAD_DIM)
        weights[head] = jnp.concatenate([held[0, part], blank, held[1, part], held[2, part]], axis=0)


def attend_rows(first, rows, q_ref, kv_ref, k_marks, raised_kept, out_kept):
    heads, length, width = kv_ref.shape
    chunk = rows
    left = lanes_of(length) < HEAD_DIM
    mixed = []
    for head in range(heads):
        keys = kv_ref[head].astype(f32)
        marked = jnp.where(left, keys, k_marks[head].astype(f32)).astype(bf16)
        values = jnp.where(left, 1.0, keys).astype(bf16)
        outs = []
        for start in range(0, rows, chunk):
            scores = dot_nt(q_ref[head, first + start : first + start + chunk], marked)
            raised = jnp.exp(scores - jnp.max(scores, axis=1, keepdims=True)).astype(bf16)
            raised_kept[head, pl.ds(start, chunk)] = raised
            total = dot(raised, values)
            share = 1.0 / total
            outs.append(jnp.where(left[:chunk], share, total * pltpu.roll(share, HEAD_DIM, 1)))
        outs = jnp.concatenate(outs, axis=0)
        out_kept[head] = outs
        mixed.append(outs[:, HEAD_DIM:])
    return jnp.concatenate(mixed, axis=1).astype(bf16)


def attend_kernel(
    layer, x0, x1, x2, x3, weights, bq, bv, q_marks, k_marks,
    q_out, kv_out, ob2, ob3, raised_kept, out_kept, ob_kept, x_kept,
):
    size = ob2.shape[0]
    for item, ref in enumerate((x0, x1, x2, x3)):
        x_kept[pl.ds(item * size, size)] = ref[...]
    x = stack_rows((x0, x1, x2, x3))
    heads = q_out.shape[0]
    blank_b = jnp.zeros((1, HEAD_DIM), f32)
    bias_q, bias_v = row(bq, layer), row(bv, layer)
    for head in range(heads):
        part = slice(head * HEAD_DIM, (head + 1) * HEAD_DIM)
        bias = jnp.concatenate([bias_q[:, part], blank_b, blank_b, bias_v[:, part]], axis=1)
        qkv = (dot_nt(x, weights[head]) + bias).astype(bf16)
        query = qkv[:, : 2 * HEAD_DIM].astype(f32) * (1.0 / math.sqrt(HEAD_DIM))
        q_out[head] = (query + q_marks[head].astype(f32)).astype(bf16)
        kv_out[head] = qkv[:, 2 * HEAD_DIM :]
    mixed = attend_rows(2 * size, 2 * size, q_out, kv_out, k_marks, raised_kept, out_kept)
    ob_kept[...] = mixed
    ob2[...] = mixed[:size]
    ob3[...] = mixed[size:]


def attend_near_kernel(
    q_in, kv_in, k_marks, ob0, ob1, raised_kept, out_kept, ob_kept, q_near, q_far, kv_kept
):
    size = ob0.shape[0]
    q_near[...] = q_in[:, : 2 * size]
    q_far[...] = q_in[:, 2 * size :]
    kv_kept[...] = kv_in[...]
    mixed = attend_rows(0, 2 * size, q_in, kv_in, k_marks, raised_kept, out_kept)
    ob_kept[...] = mixed
    ob0[...] = mixed[:size]
    ob1[...] = mixed[size:]


def entry_rows(layer, x, gain, shift):
    rows = x[...].astype(f32)
    if layer:
        rows = rows * row(gain, layer - 1) + row(shift, layer - 1)
    return rows


def with_scale(unit, scale):
    return jnp.concatenate([unit, jnp.broadcast_to(scale, (unit.shape[0], CLUSTER))], axis=1)


def mix_kernel(
    layer, ob0, ob1, ob2, ob3, w0, w1, w2, w3, x, b_out, gain1, shift1, gain2, shift2,
    normed, low, normed_kept, w_kept,
):
    total = entry_rows(layer, x, gain2, shift2) + row(b_out, layer)
    for item, (left, right) in enumerate(((ob0, w0), (ob1, w1), (ob2, w2), (ob3, w3))):
        w_kept[item] = right[...]
        total = total + dot(left[...], right[...])
    unit, root = normalise(total)
    normed[...] = unit
    normed_kept[...] = with_scale(unit, root)
    low[...] = (unit * row(gain1, layer) + row(shift1, layer)).astype(bf16)


def store_rows(value, refs):
    start = 0
    for ref in refs:
        ref[...] = value[start : start + ref.shape[0]].astype(ref.dtype)
        start += ref.shape[0]


def feed_kernel(layer, x, ups, biases, downs, x_kept, acts, slope, out):
    rows = x[...]
    x_kept[...] = rows
    total = 0.0
    units = acts[0].shape[1]
    for item in range(2):
        act, der = gelu_pair(dot(rows, ups[item][layer]) + row(biases[item], layer))
        act = act.astype(bf16)
        acts[item][...] = act
        slope[:, item * units : (item + 1) * units] = der.astype(bf16)
        total = total + dot(act, downs[item][layer])
    out[...] = total.astype(out.dtype)


def turn_weights_kernel(layer, ups, biases, downs, ups_t, biases_t, downs_t):
    for item in range(2):
        ups_t[item][...] = ups[item][layer].T
        downs_t[item][...] = downs[item][layer].T
        bias = row(biases[item], layer)
        biases_t[item][...] = jnp.broadcast_to(bias, (CLUSTER, bias.shape[1])).T


def feed_turned_kernel(x, ups_t, biases_t, downs_t, x_kept, acts, slope, out):
    rows = x[...]
    x_kept[...] = rows
    total = 0.0
    units, count = acts[0].shape
    for item in range(2):
        bias = jnp.concatenate([biases_t[item][...]] * (count // CLUSTER), axis=1)
        act, der = gelu_pair(dot_nt(ups_t[item][...], rows) + bias)
        act = act.astype(bf16)
        acts[item][...] = act
        slope[item * units : (item + 1) * units, :] = der.astype(bf16)
        total = total + dot(downs_t[item][...], act)
    out[...] = total.T.astype(out.dtype)


def second_rows(layer, normed1, gain1, shift1, own, far, b_down):
    rows = normed1[...] * row(gain1, layer) + row(shift1, layer)
    return rows + own[...] + far[...].astype(f32) + row(b_down, layer)


def close_kernel(
    layer, normed1, gain1, shift1, own, far, b_down, gain2, shift2, normed, low, normed_kept
):
    unit, root = normalise(
        second_rows(layer, normed1, gain1, shift1, own, far, b_down)
    )
    normed[...] = unit
    normed_kept[...] = with_scale(unit, root)
    low[...] = (unit * row(gain2, layer) + row(shift2, layer)).astype(bf16)


def turn_kernel(
    layer, normed1, gain1, shift1, own, far, b_down, gain2, shift2, grad,
    result, low, sums, d_second,
):
    unit, root = normalise(
        second_rows(layer, normed1, gain1, shift1, own, far, b_down)
    )
    gain = row(gain2, layer)
    result[...] = unit * gain + row(shift2, layer)
    back = normalise_back(grad[...], gain, unit, root)
    d_second[...] = back
    low[...] = back.astype(bf16)
    store_sums(sums, back, grad[...] * unit, grad[...])


def unit_and_scale(kept, width):
    both = kept[...]
    return both[:, :width], both[:, width : width + 1]


def open_back_kernel(layer, normed2, base, own, core, far, gain2, low, sums, d_second):
    rest = own[...] + core[...].astype(f32) + far[...].astype(f32)
    grad = base[...] + rest
    unit, root = unit_and_scale(normed2, grad.shape[1])
    back = normalise_back(grad, row(gain2, layer), unit, root)
    d_second[...] = back
    low[...] = back.astype(bf16)
    store_sums(sums, back, grad * unit, grad)


def feed_back_kernel(layer, grad, ups, downs, slope, pres, out):
    rows = grad[...]
    total = 0.0
    units = pres[0].shape[1]
    for item in range(2):
        der = slope[:, item * units : (item + 1) * units].astype(f32)
        pre = (dot_nt(rows, downs[item][layer]) * der).astype(bf16)
        pres[item][...] = pre
        total = total + dot_nt(pre, ups[item][layer])
    out[...] = total.astype(out.dtype)


def feed_back_turned_kernel(layer, grad, ups, downs, slope, pres, out):
    rows = grad[...]
    total = 0.0
    units = pres[0].shape[0]
    for item in range(2):
        der = slope[item * units : (item + 1) * units, :].astype(f32)
        pre = (dot_nt(downs[item][layer], rows) * der).astype(bf16)
        pres[item][...] = pre
        total = total + dot(ups[item][layer], pre)
    out[...] = total.T.astype(out.dtype)


def mix_back_kernel(
    layer, base, normed1, weights, own, far, gain1, low, d0, d1, d2, d3, sums, d_first
):
    grad = base[...] + own[...] + far[...].astype(f32)
    unit, root = unit_and_scale(normed1, grad.shape[1])
    back = normalise_back(grad, row(gain1, layer), unit, root)
    d_first[...] = back
    small = back.astype(bf16)
    low[...] = small
    for item, out in enumerate((d0, d1, d2, d3)):
        out[...] = dot_nt(small, weights.piece(item)[0]).astype(bf16)
    store_sums(sums, back, grad * unit, grad)


def close_back_kernel(base, own, core, far, out):
    out[...] = base[...] + own[...] + core[...].astype(f32) + far[...].astype(f32)


def attend_back_rows(refs, q_kept, kv_kept, out_kept, raised_kept):
    d_mixed = stack_rows(refs)
    rows = d_mixed.shape[0]
    heads, length, width = kv_kept.shape
    chunk = rows
    steps = rows // chunk
    key_lanes, lanes = lanes_of(length), lanes_of(rows)[:, :HEAD_DIM]
    d_q, d_kv = [], []
    for head in range(heads):
        part = slice(head * HEAD_DIM, (head + 1) * HEAD_DIM)
        keys = kv_kept.piece(head)[0]
        both = out_kept.piece(head)[0]
        share, out = both[:, :HEAD_DIM], both[:, HEAD_DIM:]
        grad = (d_mixed[:, part].astype(f32) * share).astype(bf16).astype(f32)
        inner = jnp.sum(grad * out, axis=1, keepdims=True)
        high = inner.astype(bf16).astype(f32)
        middle = (inner - high).astype(bf16).astype(f32)
        low = inner - high - middle
        terms = jnp.where(
            lanes == 0, -high, jnp.where(lanes == 1, -middle, jnp.where(lanes == 2, -low, 0.0))
        )
        grad = jnp.concatenate([terms, grad], axis=1).astype(bf16)
        values = jnp.where(
            key_lanes < 3, 1.0, jnp.where(key_lanes < HEAD_DIM, 0.0, keys.astype(f32))
        ).astype(bf16)
        d_score, raised = [], []
        for item in range(steps):
            d_prob = dot_nt(grad[item * chunk : (item + 1) * chunk], values)
            raised.append(raised_kept.piece(head * steps + item))
            d_score.append((raised[-1].astype(f32) * d_prob).astype(bf16))
        d_score = jnp.concatenate(d_score, axis=0)
        raised = jnp.concatenate(raised, axis=0)
        query = q_kept.piece(head)[0]
        d_q.append(dot(d_score, keys)[:, :HEAD_DIM] * (1.0 / math.sqrt(HEAD_DIM)))
        left = lanes_of(rows) < HEAD_DIM
        pair = jnp.where(left, query.astype(f32), grad.astype(f32)).astype(bf16)
        d_kv.append(jnp.where(key_lanes < HEAD_DIM, dot_tn(d_score, pair), dot_tn(raised, pair)))
    return jnp.concatenate(d_q, axis=1).astype(bf16), d_kv


def attend_back_near_kernel(kv_kept, out_kept, raised_kept, q_kept, d0, d1, d_query, d_kv):
    d_query[...], terms = attend_back_rows((d0, d1), q_kept, kv_kept, out_kept, raised_kept)
    for head, term in enumerate(terms):
        d_kv[head] = term


def attend_back_kernel(
    layer, kv_kept, out_kept, raised_kept, q_kept, d2, d3, near_q, near_kv, wq, wk, wv,
    d_query, d_key, d_value, own, core, chip, cross, sums,
):
    d_q, terms = attend_back_rows((d2, d3), q_kept, kv_kept, out_kept, raised_kept)
    d_q = jnp.concatenate([near_q[...], d_q], axis=0)
    terms = [term + near_kv[head] for head, term in enumerate(terms)]
    d_k = jnp.concatenate([term[:, :HEAD_DIM] for term in terms], axis=1).astype(bf16)
    d_v = jnp.concatenate([term[:, HEAD_DIM:] for term in terms], axis=1).astype(bf16)
    d_query[...] = d_q
    d_key[...] = d_k
    d_value[...] = d_v
    store_sums(sums, jnp.concatenate([d_q.astype(f32), d_v.astype(f32)], axis=1))
    store_rows(dot(d_q, wq[layer]) + dot(d_k, wk[layer]) + dot(d_v, wv[layer]), (own, core, chip, cross))


def store_pieces(place, grad, outs, order):
    if len(outs) == 1:
        outs[0][...] = grad.astype(bf16)
        return
    keep, send = outs
    bits = len(order)
    pieces = 1 << bits
    size = grad.shape[0] // pieces
    for piece in range(pieces):
        rel = place ^ piece
        index = 0
        for step, bit in enumerate(order[1:]):
            index = index + (((rel >> bit) & 1) << (bits - 2 - step))
        value = grad[piece * size : (piece + 1) * size].astype(bf16)
        leaves = (rel >> order[0]) & 1

        @pl.when(leaves == 0)
        def _(value=value, index=index, keep=keep):
            keep[index, :size] = value

        @pl.when(leaves == 1)
        def _(value=value, index=index, send=send):
            send[index, :size] = value


def split_refs(refs, *counts):
    parts = []
    for count in counts:
        parts.append(refs[:count])
        refs = refs[count:]
    return parts


def dot_tt(left, right):
    return lax.dot_general(left, right, (((0,), (1,)), ((), ())), preferred_element_type=f32)


def stack_cols(refs):
    return jnp.concatenate([ref[...] for ref in refs], axis=1)


def feed_grad_kernel(orders, spot, *refs):
    size = (len(refs) - 17) // 2
    pre, x, grad, act, one, two, (sums,) = split_refs(refs, 4, 4, 4, 4, size, size, 1)
    pre_near, pre_far = stack_rows(pre[:2]), stack_cols(pre[2:])
    up = dot_tn(stack_rows(x[:2]), pre_near) + dot_tt(stack_rows(x[2:]), pre_far)
    store_pieces(spot[1], up, one, orders[0])
    down = dot_tn(stack_rows(grad[:2]), stack_rows(act[:2])) + dot_tt(stack_rows(grad[2:]), stack_cols(act[2:]))
    store_pieces(spot[1], down, two, orders[1])
    ones = jnp.ones((sums.shape[0], pre_near.shape[0]), bf16)
    sums[...] = dot(ones, pre_near) + dot_nt(ones, pre_far)


def fold_small(rows):
    half = rows.shape[1] // 2
    return jnp.concatenate([rows[:, :half], rows[:, half:]], axis=0).astype(bf16)


def attend_grad_kernel(orders, terms, spot, *refs):
    small, refs = refs[:terms], refs[terms:]
    size = (len(refs) - 10) // 2
    x, (dq, dk, dv), grad, mixed, one, two = split_refs(refs, 1, 3, 4, 2, size, size)
    if terms and size == 2:
        below = fold_small(functools.reduce(jnp.add, [ref[...] for ref in small]))
        for ref in one:
            for item in range(ref.shape[0]):
                ref[item, ref.shape[1] - below.shape[0] :] = below
    x = x[0][...]
    right = jnp.concatenate([dq[...], dk[...]], axis=1)
    store_pieces(spot[1], dot_tn(x, right), one, orders[0])
    out = dot_tn(stack_rows(grad), stack_rows(mixed))
    store_pieces(spot[1], jnp.concatenate([dot_tn(x, dv[...]), out], axis=1), two, orders[1])


def whole_grads(spots, keeps, gots):
    return [
        keep[...].astype(f32) + gots[spot][:, :rows, start : start + cols].astype(f32)
        for keep, (spot, start, cols, rows) in zip(keeps, spots)
    ]


def halve_kernel(spots, groups, count, *refs):
    keeps, gots, rest = split_refs(refs, len(spots), count, len(refs) - len(spots) - count)
    held = [item.astype(bf16) for item in whole_grads(spots, keeps, gots)]
    for item, ref in zip(held, rest):
        ref[...] = item[: ref.shape[0]]
    for group, ref in zip(groups, rest[len(spots) :]):
        leaving = []
        for spot in group:
            item = held[spot][ref.shape[0] :]
            missing = ref.shape[1] - item.shape[1]
            if missing:
                item = jnp.concatenate([item, jnp.zeros((item.shape[0], missing, item.shape[2]), bf16)], axis=1)
            leaving.append(item)
        ref[...] = jnp.concatenate(leaving, axis=2)


def place_rows(head, piece, groups=4):
    return jnp.concatenate([jnp.where(head == item, piece, 0.0) for item in range(groups)], axis=1)


def collect_kernel(spot, *refs):
    rows = []
    for layer in range(len(refs) // 4):
        mix, feed, up, qv = refs[4 * layer : 4 * layer + 4]
        cols = qv.shape[1] // 2
        rows += [place_rows(spot[2], qv[:1, :cols]), place_rows(spot[2], qv[:1, cols:])]
        rows += [mix[:3, :], feed[:3, :]]
        rows += [jnp.where(spot[2] == item, up[:1, :], 0.0) for item in range(4)]
    refs[-1][...] = jnp.concatenate(rows, axis=0)


def assemble_kernel(spots, count, depth, *refs):
    keeps, gots, refs = split_refs(refs, len(spots), count, len(refs) - len(spots) - count)
    grads = whole_grads(spots, keeps, gots)
    g_q, g_k, g_v, g_o, g_up, g_down, *vectors, s_bu = refs
    own, cols = g_q.shape[1:]
    below = grads[2][0, own:]
    half = below.shape[0] // 2
    small = jnp.concatenate([below[:half], below[half:]], axis=1)
    model = small.shape[1]
    for layer in range(depth):
        up, down, one, two = grads[4 * layer : 4 * layer + 4]
        g_up[layer] = up[0]
        g_down[layer] = down[0]
        g_q[layer] = one[0, :own, :cols]
        g_k[layer] = one[0, :own, cols:]
        g_v[layer] = two[0, :, :cols]
        g_o[layer] = two[0, :, cols:].T
        rows = small[12 * layer : 12 * layer + 12]
        for item, ref in enumerate(vectors):
            ref[layer : layer + 1, :] = rows[item : item + 1, :]
        for item in range(4):
            s_bu[layer : layer + 1, item * model : (item + 1) * model] = rows[8 + item : 9 + item, :]


class Scalar:
    def __init__(self, array):
        self.array = array


class Far:
    def __init__(self, array):
        self.array = array


class Stay:
    def __init__(self, shape, kind):
        self.shape, self.kind = shape, kind


class View:
    def __init__(self, array, pieces=1):
        self.array, self.pieces = array, pieces


def call(kernel, name, ins, outs, vmem, scratch=()):
    arrays, specs, pieces = [], [], {}
    for spot, item in enumerate(ins):
        space = pltpu.VMEM
        if isinstance(item, Scalar):
            space = pltpu.SMEM
            arrays.append(item.array)
        elif isinstance(item, Far):
            space = pltpu.HBM
            arrays.append(pltpu.with_memory_space_constraint(item.array, pltpu.HBM))
        elif isinstance(item, View):
            arrays.append(pltpu.with_memory_space_constraint(item.array, pltpu.VMEM))
            pieces[spot] = item.pieces
        else:
            arrays.append(item)
        specs.append(pl.BlockSpec(memory_space=space))
    shapes = []
    for item in outs:
        if isinstance(item, Stay):
            shapes.append(pltpu.VMEM(item.shape, item.kind))
        else:
            shapes.append(jax.ShapeDtypeStruct(*item))

    def wrapped(*refs):
        kernel(*(Viewed(ref, pieces[spot]) if spot in pieces else ref for spot, ref in enumerate(refs)))

    return pl.pallas_call(
        wrapped,
        name=name,
        grid=(1,),
        out_shape=shapes,
        in_specs=specs,
        out_specs=[pl.BlockSpec(memory_space=pltpu.VMEM)] * len(shapes),
        scratch_shapes=scratch,
        compiler_params=pltpu.CompilerParams(vmem_limit_bytes=int(vmem * MIB)),
        cost_estimate=pl.CostEstimate(flops=int(GIGA.get(name, 0) * 1e9) + 1, bytes_accessed=1, transcendentals=0),
    )(*arrays)


def grad_outs(rows, cols, order, extra=0):
    pieces = 1 << len(order)
    if (rows // pieces) % 16:
        return [((rows, cols), bf16)]
    return [((pieces // 2, rows // pieces + extra, cols), bf16)] * 2


def start_halving(parts, place, orders, small=()):
    half = len(parts) // 2
    if half == 1:
        pairs = []
        for part, order in zip(parts, orders):
            pieces = 1 << len(order)
            whole = part.reshape(pieces, -1, part.shape[1])
            ranks = []
            for spot in range(pieces):
                ranks.append(
                    sum(((spot >> (len(order) - 1 - step)) & 1) << bit for step, bit in enumerate(order))
                )
            whole = jnp.take(whole, jnp.array(ranks, jnp.int32) ^ place, axis=0)
            if small and not pairs:
                below = fold_small(functools.reduce(jnp.add, small))
                below = jnp.broadcast_to(below, (pieces,) + below.shape)
                whole = jnp.concatenate([whole, below], axis=1)
            pairs.append((whole[: pieces // 2], whole[pieces // 2 :]))
    else:
        pairs = (parts[:2], parts[2:])
    return Halving(*zip(*pairs), orders)


def body(
    hidden_in, w_query, w_key, w_value, b_query, b_value, w_out, b_out, ln1_gain, ln1_bias,
    w_up, b_up, w_down, b_down, ln2_gain, ln2_bias, token_mask, query_order, key_order,
    out_cotangent,
):
    depth, model, cols = w_query.shape
    rows = hidden_in.shape[0]
    units = w_up.shape[2]
    pack = token_mask.shape[0]
    heads = query_order.shape[1]
    head = lax.axis_index("head").astype(jnp.int32)
    groups = lax.axis_size("head")
    place = lax.axis_index("dp").astype(jnp.int32)
    spot = Scalar(jnp.stack([head * rows, place, head]))
    bits = lax.axis_size("dp").bit_length() - 1
    order_one = tuple(range(bits))
    order_two = order_one[:2][::-1] + order_one[2:]
    orders = (order_one, order_two)
    w_query, w_key, w_value = (item.transpose(0, 2, 1) for item in (w_query, w_key, w_value))
    q_order, k_order = query_order.transpose(1, 0, 2), key_order.transpose(1, 0, 2)

    wide = (rows, model)
    dense = 2 * rows * model
    wide_low, wide_full = (wide, bf16), (wide, f32)

    low = hidden_in
    chip, core = swap(low, "head", 2), swap(low, "head", 1)
    around = token_mask.reshape(groups, rows)
    live = jnp.concatenate(
        [lax.dynamic_index_in_dim(around, head ^ item, 0, keepdims=False) for item in range(groups)]
    )
    live = live.astype(f32).reshape(pack, 1)

    entry = hidden_in
    kept = []
    pair = 2 * rows
    two = 2 * HEAD_DIM
    kept_rows = [Stay((heads, pair, pack), bf16), Stay((heads, pair, two), f32), Stay((pair, cols), bf16)]
    other_units = [swap(item, "head", 1) for item in (w_up, b_up, w_down)]
    for layer in range(depth):
        *marks, weights = call(
            functools.partial(cluster_kernel, layer), "clusters",
            [spot, q_order, k_order, live, Far(w_query), Far(w_key), Far(w_value)],
            [((heads, pack, two), bf16)] * 2 + [((heads, 2 * two, model), bf16)], vmem=7,
            scratch=[pltpu.VMEM((3, cols, model), bf16), pltpu.SemaphoreType.DMA((3,))],
        )
        if not layer:
            chip, other_units[1] = tie((chip, other_units[1]))
        chip = tie(chip, weights)
        cross = swap(chip, "head", 1)
        if not layer:
            cross, other_units[0], other_units[2] = tie((cross, other_units[0], other_units[2]))
            ups, biases, downs = zip((w_up, b_up, w_down), other_units)
        w_mine = tie(w_out[layer], chip)
        w_core, w_chip = swap(w_mine, "head", 1), swap(w_mine, "head", 2)
        q_all, kv_all, ob2, ob3, raised_far, out_far, ob_far, x_kept = call(
            functools.partial(attend_kernel, layer), "attend",
            [low, core, chip, cross, weights, b_query, b_value, *marks],
            [((heads, pack, two), bf16)] * 2 + [((rows, cols), bf16)] * 2 + kept_rows
            + [Stay((pack, model), bf16)], vmem=6,
        )
        got2, got3 = swap(ob2, "head", 2), swap(ob3, "head", 3)
        ob0, ob1, raised_near, out_near, ob_near, *q_kept, kv_kept = call(
            attend_near_kernel, "attend_near", [q_all, kv_all, marks[1]],
            [((rows, cols), bf16)] * 2 + kept_rows + [Stay((heads, pair, two), bf16)] * 2
            + [Stay((heads, pack, two), bf16)], vmem=4,
        )
        got1 = swap(ob1, "head", 1)
        got1, got2, got3, w_core, w_chip = tie((got1, got2, got3, w_core, w_chip))
        w_cross = swap(w_chip, "head", 1)
        outs = (w_mine, w_core, w_chip, w_cross)
        got = [ob0, got1, got2, got3]
        normed1, low1, normed1_kept, w_kept = call(
            functools.partial(mix_kernel, layer), "mix",
            [*got, *outs, entry, b_out, ln1_gain, ln1_bias, ln2_gain, ln2_bias],
            [wide_full, wide_low, Stay((rows, model + CLUSTER), f32), Stay((4, cols, model), bf16)], vmem=4,
        )

        def feed(block, kind):
            def kernel(x, up, up2, bias, bias2, down, down2, x_kept, act, act2, slope, out):
                feed_kernel(layer, x, (up, up2), (bias, bias2), (down, down2), x_kept, (act, act2), slope, out)

            return call(
                kernel, "feed", [block, *ups, *biases, *downs],
                [Stay(wide, bf16), Stay((rows, units), bf16), ((rows, units), bf16),
                 Stay((rows, 2 * units), bf16), (wide, kind)], vmem=5.5,
            )

        def turn_weights(up, up2, bias, bias2, down, down2, *outs):
            turn_weights_kernel(layer, (up, up2), (bias, bias2), (down, down2), outs[:2], outs[2:4], outs[4:6])
            for out in outs[6:]:
                out[...] = down2[...]

        def feed_turned(x, up, up2, bias, bias2, down, down2, x_kept, act, act2, slope, out):
            feed_turned_kernel(x, (up, up2), (bias, bias2), (down, down2), x_kept, (act, act2), slope, out)

        chip = swap(low1, "head", 2)
        turned = call(
            turn_weights, "turn_weights", [*tie([*ups, *biases, *downs], low1)],
            [((units, model), bf16)] * 2 + [((units, CLUSTER), f32)] * 2 + [((model, units), bf16)] * 2
            + [Stay(w_down.shape, bf16)] * (not layer), vmem=4 + 3 * (not layer),
        )
        if not layer:
            *turned, other_down = turned
            downs = (w_down, other_down)
        h_own, act_own, act_core, slope_own, own_term = feed(low1, f32)
        chip = tie(chip, own_term, turned)
        h_chip, act_chip, act_cross, slope_chip, far_term = call(
            feed_turned, "feed_turned", [chip, *turned],
            [Stay(wide, bf16), Stay((units, rows), bf16), ((units, rows), bf16), Stay((2 * units, rows), bf16),
             wide_low], vmem=5.5,
        )
        far = swap(far_term, "head", 2)
        away = [swap(item, "head", 1) for item in tie((h_own, act_core, h_chip, act_cross), far_term)]
        ends = [normed1, ln1_gain, ln1_bias, own_term, far, b_down, ln2_gain, ln2_bias]
        kept.append(
            (x_kept, (kv_kept, q_kept), ((out_near, raised_near), (out_far, raised_far)), (ob_near, ob_far),
             normed1_kept, w_kept, (slope_own, slope_chip))
        )
        if layer + 1 < depth:
            entry, low, normed2_kept = call(
                functools.partial(close_kernel, layer), "close", ends,
                [wide_full, wide_low, Stay((rows, model + CLUSTER), f32)], vmem=4,
            )
            kept[-1] += (normed2_kept,)
            low, away = tie((low, away))
            chip, core = swap(low, "head", 2), swap(low, "head", 1)
        else:
            result, low, sums2, d_second = call(
                functools.partial(turn_kernel, layer), "turn", ends + [out_cotangent],
                [wide_full, wide_low, ((8, model), f32), Stay(*wide_full)], vmem=4,
            )
            low, away = tie((low, away))
        h_core, act_core, h_cross, act_cross = away
        kept[-1] += ((h_own, h_core, h_chip, h_cross), (act_own, act_core, act_chip, act_cross))

    feed_sums = attend_sums = None
    grads, small = [None] * depth, [None] * depth
    pieces = heads
    for layer in reversed(range(depth)):
        x_kept, (kv_kept, q_kept), (near, far_rows), obs, normed1, w_kept, slopes, *_, h_kept, acts = kept[layer]
        above = feed_sums is not None

        def feed_back(grad, up, up2, down, down2, slope, pre, pre2, out):
            feed_back_kernel(layer, grad, (up, up2), (down, down2), slope, (pre, pre2), out)

        def feed_back_turned(grad, up, up2, down, down2, slope, pre, pre2, out):
            feed_back_turned_kernel(layer, grad, (up, up2), (down, down2), slope, (pre, pre2), out)

        chip, g_core = swap(low, "head", 2), swap(low, "head", 1)
        pre_own, pre_core, own_term = call(
            feed_back, "feed_back", [low, *ups, *downs, View(slopes[0])],
            [((rows, units), bf16)] * 2 + [wide_full], vmem=4,
        )
        chip, g_core = join((chip, g_core), [feed_sums, attend_sums] if above else [], own_term)
        g_cross = swap(chip, "head", 1)
        pre_chip, pre_cross, far_term = call(
            feed_back_turned, "feed_back_turned", [chip, *ups, *downs, View(slopes[1])],
            [((units, rows), bf16)] * 2 + [wide_low], vmem=5,
        )
        far_term, g_cross = tie((far_term, g_cross))
        far = swap(far_term, "head", 2)
        pre_core, pre_cross = [swap(item, "head", 1) for item in tie((pre_core, pre_cross), far_term)]
        g_blocks = (low, g_core, chip, g_cross)
        added = ()
        if above and attend_sums.more():
            added = advance([attend_sums], far_term)
        *parts, up_sums = call(
            functools.partial(feed_grad_kernel, orders), "feed_grad",
            [spot, *tie((pre_own, pre_core, pre_chip, pre_cross), added), *map(View, h_kept), *g_blocks,
             *map(View, acts)],
            grad_outs(model, units, order_one) + grad_outs(model, units, order_two) + [((8, units), f32)],
            vmem=9,
        )
        far = tie(far, parts)
        if above:
            parts = join(parts, [attend_sums])
        waiting = attend_sums
        feed_sums = start_halving(parts, place, orders)
        low, *d_obs, sums1, d_first = call(
            functools.partial(mix_back_kernel, layer), "mix_back",
            [View(d_second), View(normed1), View(w_kept, 4), own_term, far, ln1_gain],
            [wide_low] + [((rows, cols), bf16)] * 4 + [((8, model), f32), Stay(*wide_full)], vmem=4,
        )
        got = [d_obs[0]] + [swap(d_obs[item], "head", item) for item in (1, 2, 3)]

        def kept_part(part, start):
            out, raised = part
            raised = View(raised.reshape(heads * pair, pack), pieces)
            return [
                View(kv_kept, heads), View(out, heads), raised,
                View(q_kept[start // pair], heads),
            ]

        near_q, near_kv = call(
            attend_back_near_kernel, "attend_back_near",
            kept_part(near, 0) + got[:2],
            [((pair, cols), bf16), ((heads, pack, two), f32)], vmem=7,
        )
        got = tie(got, near_q)
        others = [item for item in (feed_sums, waiting) if item]
        got = join(got, others)
        if any(item.more() for item in others):
            got = tie(got, advance(others))
        low = tie(low, got)
        chip, core = swap(low, "head", 2), swap(low, "head", 1)
        d_q, d_k, d_v, own_term, core_term, chip_term, cross_term, sums_qv = call(
            functools.partial(attend_back_kernel, layer), "attend_back",
            kept_part(far_rows, pair)
            + [got[2], got[3], near_q, near_kv, w_query, w_key, w_value],
            [((pack, cols), bf16)] * 3 + [wide_full, wide_low, wide_full, wide_low]
            + [((8, 2 * cols), f32)], vmem=10,
        )
        others = [item for item in (feed_sums, waiting) if item]
        chip, core, core_term, cross_term = join((chip, core, core_term, cross_term), others)
        got_chip, got_core = swap(cross_term, "head", 1), swap(core_term, "head", 1)
        cross = swap(chip, "head", 1)
        small[layer] = [sums1, sums2, up_sums, sums_qv]
        last = ()
        if not layer:
            mine = call(
                collect_kernel, "collect", [spot] + [item for part in small for item in part],
                [((12 * depth, model), f32)], vmem=3,
            )[0]
            last = (mine, swap(mine, "head", 1))
        got_chip, got_core, last = tie((got_chip, got_core, last))
        merged = (chip_term + got_chip.astype(f32)).astype(bf16)
        if not layer:
            total = last[0] + last[1]
            last = (total, swap(total, "head", 2))
        a_blocks = (low, core, chip, cross)
        added = ()
        if any(item.more() for item in others):
            added = advance(others, merged, apart=bool(layer))
        if not layer:
            merged, last = tie((merged, last), added)
        far = swap(merged, "head", 2)
        parts = call(
            functools.partial(attend_grad_kernel, orders, len(last)), "attend_grad",
            [spot, *last, View(x_kept), *tie((d_q, d_k, d_v), merged, added), *a_blocks, *map(View, obs)],
            grad_outs(model, 2 * cols, order_one, 0 if layer else 24 * depth)
            + grad_outs(model, 2 * cols, order_two), vmem=6,
        )
        if layer:
            far = land(far, [feed_sums.slots[0][0]], parts)
        attend_sums = start_halving(parts, place, orders, last)
        grads[layer] = (feed_sums, attend_sums)
        if layer:
            low, sums2, d_second = call(
                functools.partial(open_back_kernel, layer - 1), "open_back",
                [View(kept[layer - 1][-3]), View(d_first), own_term, got_core, far, ln2_gain],
                [wide_low, ((8, model), f32), Stay(*wide_full)], vmem=4,
            )

    far = join(far, [feed_sums])
    d_rows = call(close_back_kernel, "close_back", [View(d_first), own_term, got_core, far], [wide_full], vmem=4)[0]
    d_rows = join(d_rows, [attend_sums])
    while attend_sums.more():
        advance([attend_sums], d_rows)
    items = [item for layer in grads for item in layer]
    while any(item.more() for item in items):
        advance(items)
    ends = [keep for item in items for keep in item.keeps] + [item.got for item in transfers_of(items)]
    own = ends[0].shape[1]
    g_q, g_k, g_v, g_o, g_up, g_down, s_bq, s_bv, s_bo, s_g1, s_n1, s_bd, s_g2, s_n2, s_bu = call(
        functools.partial(assemble_kernel, spots_of(items), len(transfers_of(items)), depth), "assemble", ends,
        [((depth, own, cols), f32)] * 3 + [((depth, cols, own), f32)] + [((depth, own, units), f32)] * 2
        + [((depth, model), f32)] * 8 + [((depth, groups * units), f32)], vmem=8,
    )
    return (
        result, d_rows, g_q, g_k, g_v, s_bq, s_bv, g_o, s_bo, s_g1, s_n1, g_up,
        s_bu, g_down.transpose(0, 2, 1), s_bd, s_g2, s_n2,
    )


def solution(mesh):
    split = P(("dp", "head"), None)
    column, line = P(None, None, "head"), P(None, "head", None)
    placed = (
        split, column, column, column, P(None, "head"), P(None, "head"), line, P(), P(), P(),
        column, P(None, "head"), line, P(), P(), P(),
        P("dp"), P(None, "head", "dp"), P(None, "head", "dp"), split,
    )
    by_rows, by_cols = P(None, "dp", "head"), P(None, "head", "dp")
    results = (
        split, split, by_rows, by_rows, by_rows, P(), P(), by_cols, P(), P(), P(), by_rows, P(),
        by_cols, P(), P(), P(),
    )
    return jax.shard_map(body, mesh=mesh, in_specs=placed, out_specs=results, check_vma=False)
```

```python
import functools
import math

import jax
import jax.numpy as jnp
from jax import lax
from jax.experimental import pallas as pl
from jax.experimental.pallas import tpu as pltpu
from jax.sharding import PartitionSpec as P

CLUSTER = 128
HEAD_DIM = 64
EPS = 1e-12
NEG = -1e30
MIB = 1024 * 1024
GIGA = {"attend_back_near": 3, "close_back": 3}

f32 = jnp.float32
bf16 = jnp.bfloat16


def swap(array, axis, bit):
    size = lax.axis_size(axis)
    return lax.ppermute(array, axis, [(item, item ^ bit) for item in range(size)])


def tie(value, *earlier):
    return lax.optimization_barrier((value, earlier))[0]


class Transfer:
    def __init__(self, send, bit):
        self.got = swap(send, "dp", 1 << bit)


class Halving:
    def __init__(self, keeps, sends, orders, extras):
        self.keeps, self.orders, self.extras = list(keeps), [list(order) for order in orders], extras
        self.slots = [(Transfer(send, order.pop(0)), 0) for send, order in zip(sends, self.orders)]

    def more(self):
        return bool(self.orders[0])


def transfers_of(items):
    found = []
    for item in items:
        for transfer, _ in item.slots:
            if transfer not in found:
                found.append(transfer)
    return found


def spots_of(items):
    found = transfers_of(items)
    return [
        (found.index(transfer), start, keep.shape[0], extra)
        for item in items
        for keep, (transfer, start), extra in zip(item.keeps, item.slots, item.extras)
    ]


def join(value, items, *earlier):
    return land(value, transfers_of(items), *earlier)


def land(value, found, *earlier):
    value, gots, _ = lax.optimization_barrier((value, [item.got for item in found], earlier))
    for item, got in zip(found, gots):
        item.got = got
    return value


def advance(items, *earlier, apart=False):
    items = [item for item in items if item.more()]
    found = transfers_of(items)
    keeps = [keep for item in items for keep in item.keeps]
    keeps, gots = tie((keeps, [item.got for item in found]), *earlier)
    extras = [extra for item in items for extra in item.extras]
    outs = [(((keep.shape[0] - extra) // 2 + extra, keep.shape[1]), bf16) for keep, extra in zip(keeps, extras)]
    groups = {}
    bits = [order.pop(0) for item in items for order in item.orders]
    for spot, (bit, out) in enumerate(zip(bits, outs)):
        groups.setdefault((bit, out[0][1], spot if apart else 0), []).append(spot)
    sends = []
    for (_, cols, _), group in groups.items():
        sends.append(((sum(outs[spot][0][0] for spot in group), cols), bf16))
    parts = call(
        functools.partial(halve_kernel, spots_of(items), list(groups.values()), len(gots)), "halve",
        [*keeps, *gots], outs + sends, vmem=8,
    )
    slots = [None] * len(keeps)
    for (bit, *_), group, send in zip(groups, groups.values(), parts[len(keeps) :]):
        transfer, start = Transfer(send, bit), 0
        for spot in group:
            slots[spot] = (transfer, start)
            start += outs[spot][0][0]
    start = 0
    for item in items:
        stop = start + len(item.keeps)
        item.keeps, item.slots = parts[start:stop], slots[start:stop]
        start = stop
    return parts


def dot(left, right):
    return jnp.dot(left, right, preferred_element_type=f32)


def dot_nt(left, right):
    return lax.dot_general(left, right, (((1,), (1,)), ((), ())), preferred_element_type=f32)


def dot_tn(left, right):
    return lax.dot_general(left, right, (((0,), (0,)), ((), ())), preferred_element_type=f32)


def row(ref, layer):
    return ref[layer : layer + 1, :]


def normalise(rows):
    centre = rows - jnp.mean(rows, axis=-1, keepdims=True)
    spread = jnp.mean(centre * centre, axis=-1, keepdims=True)
    scale = lax.rsqrt(spread + EPS)
    return centre * scale, scale


def normalise_back(grad, gain, normed, scale):
    part = grad * gain
    mean_one = jnp.mean(part, axis=-1, keepdims=True)
    mean_two = jnp.mean(part * normed, axis=-1, keepdims=True)
    return (part - mean_one - normed * mean_two) * scale


def store_sums(ref, *arrays):
    rows = [jnp.sum(item, axis=0, keepdims=True) for item in arrays]
    rows.append(jnp.zeros((ref.shape[0] - len(rows), ref.shape[1]), f32))
    ref[...] = jnp.concatenate(rows, axis=0)


def gelu_pair(values):
    bell = jnp.exp(values * values * -0.5)
    t = 1.0 / (1.0 + (0.3275911 * math.sqrt(0.5)) * jnp.abs(values))
    poly = 0.5 * 1.061405429
    for factor in (-1.453152027, 1.421413741, -0.284496736, 0.254829592):
        poly = poly * t + 0.5 * factor
    tail = poly * t * bell
    cdf = jnp.where(values >= 0.0, 1.0 - tail, tail)
    return values * cdf, cdf + values * bell * (1.0 / math.sqrt(2.0 * math.pi))


def stack_rows(refs):
    return jnp.concatenate([ref[...] for ref in refs], axis=0)


def head_cols(array, head):
    return array[:, head * HEAD_DIM : (head + 1) * HEAD_DIM]


def lanes_of(rows):
    return lax.broadcasted_iota(jnp.int32, (rows, 2 * HEAD_DIM), 1)


class Viewed:
    def __init__(self, source, pieces):
        self.source, self.shape, self.size = source, source.shape, source.shape[0] // pieces

    def piece(self, item):
        return self.source[item * self.size : (item + 1) * self.size]

    def __getitem__(self, index):
        return self.source[index]


def cluster_kernel(layer, spot, q_order, k_order, live, wq, wk, wv, q_marks, k_marks, weights, held, sems):
    heads, length, width = q_marks.shape
    copies = [
        pltpu.make_async_copy(source.at[layer], held.at[item], sems.at[item])
        for item, source in enumerate((wq, wk, wv))
    ]
    for copy in copies:
        copy.start()
    count = length // CLUSTER
    lines = lax.broadcasted_iota(jnp.int32, (length, length), 0)
    spread_line = lax.broadcasted_iota(jnp.int32, (length, width), 0) // CLUSTER + HEAD_DIM
    lanes = lanes_of(length)
    spread = jnp.where(spread_line == lanes, 1.0, 0.0).astype(bf16)
    in_use = jnp.logical_and(lanes >= HEAD_DIM, lanes < HEAD_DIM + count)
    for head in range(heads):
        order = q_order[head, layer : layer + 1, :] ^ spot[0]
        hot = jnp.where(order == lines, 1.0, 0.0).astype(bf16)
        q_marks[head] = dot(hot, spread).astype(bf16)
        order = k_order[head, layer : layer + 1, :] ^ spot[0]
        hot = jnp.where(order == lines, 1.0, 0.0).astype(bf16)
        inside = dot(hot, spread) * live[...]
        outside = jnp.where(in_use, jnp.where(inside > 0.5, 0.0, NEG), 0.0)
        k_marks[head] = outside.astype(bf16)
    for copy in copies:
        copy.wait()
    blank = jnp.zeros((HEAD_DIM, held.shape[2]), bf16)
    for head in range(heads):
        part = slice(head * HEAD_DIM, (head + 1) * HEAD_DIM)
        weights[head] = jnp.concatenate([held[0, part], blank, held[1, part], held[2, part]], axis=0)


def attend_rows(first, rows, q_ref, kv_ref, k_marks, raised_kept, out_kept):
    heads, length, width = kv_ref.shape
    chunk = rows
    left = lanes_of(length) < HEAD_DIM
    mixed = []
    for head in range(heads):
        keys = kv_ref[head].astype(f32)
        marked = jnp.where(left, keys, k_marks[head].astype(f32)).astype(bf16)
        values = jnp.where(left, 1.0, keys).astype(bf16)
        outs = []
        for start in range(0, rows, chunk):
            scores = dot_nt(q_ref[head, first + start : first + start + chunk], marked)
            raised = jnp.exp(scores - jnp.max(scores, axis=1, keepdims=True)).astype(bf16)
            raised_kept[head, pl.ds(start, chunk)] = raised
            total = dot(raised, values)
            share = 1.0 / total
            outs.append(jnp.where(left[:chunk], share, total * pltpu.roll(share, HEAD_DIM, 1)))
        outs = jnp.concatenate(outs, axis=0)
        out_kept[head] = outs
        mixed.append(outs[:, HEAD_DIM:])
    return jnp.concatenate(mixed, axis=1).astype(bf16)


def attend_kernel(
    layer, x0, x1, x2, x3, weights, bq, bv, q_marks, k_marks,
    q_out, kv_out, ob2, ob3, raised_kept, out_kept, ob_kept, x_kept,
):
    size = ob2.shape[0]
    for item, ref in enumerate((x0, x1, x2, x3)):
        x_kept[pl.ds(item * size, size)] = ref[...]
    x = stack_rows((x0, x1, x2, x3))
    heads = q_out.shape[0]
    blank_b = jnp.zeros((1, HEAD_DIM), f32)
    bias_q, bias_v = row(bq, layer), row(bv, layer)
    for head in range(heads):
        part = slice(head * HEAD_DIM, (head + 1) * HEAD_DIM)
        bias = jnp.concatenate([bias_q[:, part], blank_b, blank_b, bias_v[:, part]], axis=1)
        qkv = (dot_nt(x, weights[head]) + bias).astype(bf16)
        query = qkv[:, : 2 * HEAD_DIM].astype(f32) * (1.0 / math.sqrt(HEAD_DIM))
        q_out[head] = (query + q_marks[head].astype(f32)).astype(bf16)
        kv_out[head] = qkv[:, 2 * HEAD_DIM :]
    mixed = attend_rows(2 * size, 2 * size, q_out, kv_out, k_marks, raised_kept, out_kept)
    ob_kept[...] = mixed
    ob2[...] = mixed[:size]
    ob3[...] = mixed[size:]


def attend_near_kernel(
    q_in, kv_in, k_marks, ob0, ob1, raised_kept, out_kept, ob_kept, q_near, q_far, kv_kept
):
    size = ob0.shape[0]
    q_near[...] = q_in[:, : 2 * size]
    q_far[...] = q_in[:, 2 * size :]
    kv_kept[...] = kv_in[...]
    mixed = attend_rows(0, 2 * size, q_in, kv_in, k_marks, raised_kept, out_kept)
    ob_kept[...] = mixed
    ob0[...] = mixed[:size]
    ob1[...] = mixed[size:]


def entry_rows(layer, x, gain, shift):
    rows = x[...].astype(f32)
    if layer:
        rows = rows * row(gain, layer - 1) + row(shift, layer - 1)
    return rows


def with_scale(unit, scale):
    return jnp.concatenate([unit, jnp.broadcast_to(scale, (unit.shape[0], CLUSTER))], axis=1)


def mix_kernel(
    layer, ob0, ob1, ob2, ob3, w0, w1, w2, w3, x, b_out, gain1, shift1, gain2, shift2,
    normed, low, normed_kept, w_kept,
):
    total = entry_rows(layer, x, gain2, shift2) + row(b_out, layer)
    for item, (left, right) in enumerate(((ob0, w0), (ob1, w1), (ob2, w2), (ob3, w3))):
        w_kept[item] = right[...]
        total = total + dot(left[...], right[...])
    unit, root = normalise(total)
    normed[...] = unit
    normed_kept[...] = with_scale(unit, root)
    low[...] = (unit * row(gain1, layer) + row(shift1, layer)).astype(bf16)


def store_rows(value, refs):
    start = 0
    for ref in refs:
        ref[...] = value[start : start + ref.shape[0]].astype(ref.dtype)
        start += ref.shape[0]


def feed_kernel(layer, x, ups, biases, downs, x_kept, acts, slope, out):
    rows = x[...]
    x_kept[...] = rows
    total = 0.0
    units = acts[0].shape[1]
    for item in range(2):
        act, der = gelu_pair(dot(rows, ups[item][layer]) + row(biases[item], layer))
        act = act.astype(bf16)
        acts[item][...] = act
        slope[:, item * units : (item + 1) * units] = der.astype(bf16)
        total = total + dot(act, downs[item][layer])
    out[...] = total.astype(out.dtype)


def turn_weights_kernel(layer, ups, biases, downs, ups_t, biases_t, downs_t):
    for item in range(2):
        ups_t[item][...] = ups[item][layer].T
        downs_t[item][...] = downs[item][layer].T
        bias = row(biases[item], layer)
        biases_t[item][...] = jnp.broadcast_to(bias, (CLUSTER, bias.shape[1])).T


def feed_turned_kernel(x, ups_t, biases_t, downs_t, x_kept, acts, slope, out):
    rows = x[...]
    x_kept[...] = rows
    total = 0.0
    units, count = acts[0].shape
    for item in range(2):
        bias = jnp.concatenate([biases_t[item][...]] * (count // CLUSTER), axis=1)
        act, der = gelu_pair(dot_nt(ups_t[item][...], rows) + bias)
        act = act.astype(bf16)
        acts[item][...] = act
        slope[item * units : (item + 1) * units, :] = der.astype(bf16)
        total = total + dot(downs_t[item][...], act)
    out[...] = total.T.astype(out.dtype)


def second_rows(layer, normed1, gain1, shift1, own, far, b_down):
    rows = normed1[...] * row(gain1, layer) + row(shift1, layer)
    return rows + own[...] + far[...].astype(f32) + row(b_down, layer)


def close_kernel(
    layer, normed1, gain1, shift1, own, far, b_down, gain2, shift2, normed, low, normed_kept
):
    unit, root = normalise(
        second_rows(layer, normed1, gain1, shift1, own, far, b_down)
    )
    normed[...] = unit
    normed_kept[...] = with_scale(unit, root)
    low[...] = (unit * row(gain2, layer) + row(shift2, layer)).astype(bf16)


def turn_kernel(
    layer, normed1, gain1, shift1, own, far, b_down, gain2, shift2, grad,
    result, low, sums, d_second,
):
    unit, root = normalise(
        second_rows(layer, normed1, gain1, shift1, own, far, b_down)
    )
    gain = row(gain2, layer)
    result[...] = unit * gain + row(shift2, layer)
    back = normalise_back(grad[...], gain, unit, root)
    d_second[...] = back
    low[...] = back.astype(bf16)
    store_sums(sums, back, grad[...] * unit, grad[...])


def unit_and_scale(kept, width):
    both = kept[...]
    return both[:, :width], both[:, width : width + 1]


def open_back_kernel(layer, normed2, base, own, core, far, gain2, low, sums, d_second):
    rest = own[...] + core[...].astype(f32) + far[...].astype(f32)
    grad = base[...] + rest
    unit, root = unit_and_scale(normed2, grad.shape[1])
    back = normalise_back(grad, row(gain2, layer), unit, root)
    d_second[...] = back
    low[...] = back.astype(bf16)
    store_sums(sums, back, grad * unit, grad)


def feed_back_kernel(layer, grad, ups, downs, slope, pres, out):
    rows = grad[...]
    total = 0.0
    units = pres[0].shape[1]
    for item in range(2):
        der = slope[:, item * units : (item + 1) * units].astype(f32)
        pre = (dot_nt(rows, downs[item][layer]) * der).astype(bf16)
        pres[item][...] = pre
        total = total + dot_nt(pre, ups[item][layer])
    out[...] = total.astype(out.dtype)


def feed_back_turned_kernel(layer, grad, ups, downs, slope, pres, out):
    rows = grad[...]
    total = 0.0
    units = pres[0].shape[0]
    for item in range(2):
        der = slope[item * units : (item + 1) * units, :].astype(f32)
        pre = (dot_nt(downs[item][layer], rows) * der).astype(bf16)
        pres[item][...] = pre
        total = total + dot(ups[item][layer], pre)
    out[...] = total.T.astype(out.dtype)


def mix_back_kernel(
    layer, base, normed1, weights, own, far, gain1, low, d0, d1, d2, d3, sums, d_first
):
    grad = base[...] + own[...] + far[...].astype(f32)
    unit, root = unit_and_scale(normed1, grad.shape[1])
    back = normalise_back(grad, row(gain1, layer), unit, root)
    d_first[...] = back
    small = back.astype(bf16)
    low[...] = small
    for item, out in enumerate((d0, d1, d2, d3)):
        out[...] = dot_nt(small, weights.piece(item)[0]).astype(bf16)
    store_sums(sums, back, grad * unit, grad)


def close_back_kernel(base, own, core, far, out):
    out[...] = base[...] + own[...] + core[...].astype(f32) + far[...].astype(f32)


def attend_back_rows(refs, q_kept, kv_kept, out_kept, raised_kept):
    d_mixed = stack_rows(refs)
    rows = d_mixed.shape[0]
    heads, length, width = kv_kept.shape
    chunk = rows
    steps = rows // chunk
    key_lanes, lanes = lanes_of(length), lanes_of(rows)[:, :HEAD_DIM]
    d_q, d_k, d_v = [], [], []
    for head in range(heads):
        part = slice(head * HEAD_DIM, (head + 1) * HEAD_DIM)
        keys = kv_kept.piece(head)[0]
        both = out_kept.piece(head)[0]
        share, out = both[:, :HEAD_DIM], both[:, HEAD_DIM:]
        grad = (d_mixed[:, part].astype(f32) * share).astype(bf16).astype(f32)
        inner = jnp.sum(grad * out, axis=1, keepdims=True)
        high = inner.astype(bf16).astype(f32)
        middle = (inner - high).astype(bf16).astype(f32)
        low = inner - high - middle
        terms = jnp.where(
            lanes == 0, -high, jnp.where(lanes == 1, -middle, jnp.where(lanes == 2, -low, 0.0))
        )
        grad = jnp.concatenate([terms, grad], axis=1).astype(bf16)
        values = jnp.where(
            key_lanes < 3, 1.0, jnp.where(key_lanes < HEAD_DIM, 0.0, keys.astype(f32))
        ).astype(bf16)
        d_score, raised = [], []
        for item in range(steps):
            d_prob = dot_nt(grad[item * chunk : (item + 1) * chunk], values)
            raised.append(raised_kept.piece(head * steps + item))
            d_score.append((raised[-1].astype(f32) * d_prob).astype(bf16))
        d_score = jnp.concatenate(d_score, axis=0)
        raised = jnp.concatenate(raised, axis=0)
        query = q_kept.piece(head)[0]
        d_q.append(dot(d_score, keys)[:, :HEAD_DIM] * (1.0 / math.sqrt(HEAD_DIM)))
        d_k.append(dot(query.T[:HEAD_DIM], d_score))
        d_v.append(dot(grad.T[HEAD_DIM:], raised))
    return (
        jnp.concatenate(d_q, axis=1).astype(bf16),
        jnp.concatenate(d_k, axis=0),
        jnp.concatenate(d_v, axis=0),
    )


def attend_back_near_kernel(kv_kept, out_kept, raised_kept, q_kept, d0, d1, d_query, d_k, d_v):
    d_query[...], d_k[...], d_v[...] = attend_back_rows((d0, d1), q_kept, kv_kept, out_kept, raised_kept)


def attend_back_kernel(
    layer, kv_kept, out_kept, raised_kept, q_kept, d2, d3, near_q, near_k, near_v, wq, wk, wv,
    d_query, d_key, d_value, own, core, chip, cross, sums,
):
    d_q, d_k, d_v = attend_back_rows((d2, d3), q_kept, kv_kept, out_kept, raised_kept)
    d_q = jnp.concatenate([near_q[...], d_q], axis=0)
    d_k, d_v = ((item + near[...]).T.astype(bf16) for item, near in ((d_k, near_k), (d_v, near_v)))
    d_query[...] = d_q
    d_key[...] = d_k
    d_value[...] = d_v
    store_sums(sums, jnp.concatenate([d_q.astype(f32), d_v.astype(f32)], axis=1))
    store_rows(dot(d_q, wq[layer]) + dot(d_k, wk[layer]) + dot(d_v, wv[layer]), (own, core, chip, cross))


def store_pieces(place, grad, outs, order):
    if len(outs) == 1:
        outs[0][...] = grad.astype(bf16)
        return
    keep, send = outs
    bits = len(order)
    pieces = 1 << bits
    size = grad.shape[0] // pieces
    for piece in range(pieces):
        rel = place ^ piece
        index = 0
        for step, bit in enumerate(order[1:]):
            index = index + (((rel >> bit) & 1) << (bits - 2 - step))
        value = grad[piece * size : (piece + 1) * size].astype(bf16)
        leaves = (rel >> order[0]) & 1

        @pl.when(leaves == 0)
        def _(value=value, index=index, keep=keep):
            keep[pl.ds(pl.multiple_of(index * size, size), size)] = value

        @pl.when(leaves == 1)
        def _(value=value, index=index, send=send):
            send[pl.ds(pl.multiple_of(index * size, size), size)] = value


def split_refs(refs, *counts):
    parts = []
    for count in counts:
        parts.append(refs[:count])
        refs = refs[count:]
    return parts


def dot_tt(left, right):
    return lax.dot_general(left, right, (((0,), (1,)), ((), ())), preferred_element_type=f32)


def stack_cols(refs):
    return jnp.concatenate([ref[...] for ref in refs], axis=1)


def feed_grad_kernel(orders, spot, *refs):
    size = (len(refs) - 17) // 2
    pre, x, grad, act, one, two, (sums,) = split_refs(refs, 4, 4, 4, 4, size, size, 1)
    pre_near, pre_far = stack_rows(pre[:2]), stack_cols(pre[2:])
    up = dot_tn(stack_rows(x[:2]), pre_near) + dot_tt(stack_rows(x[2:]), pre_far)
    store_pieces(spot[1], up, one, orders[0])
    down = dot_tn(stack_rows(grad[:2]), stack_rows(act[:2])) + dot_tt(stack_rows(grad[2:]), stack_cols(act[2:]))
    store_pieces(spot[1], down, two, orders[1])
    ones = jnp.ones((sums.shape[0], pre_near.shape[0]), bf16)
    sums[...] = dot(ones, pre_near) + dot_nt(ones, pre_far)


def fold_small(rows):
    half = rows.shape[1] // 2
    return jnp.concatenate([rows[:, :half], rows[:, half:]], axis=0).astype(bf16)


def attend_grad_kernel(orders, terms, spot, *refs):
    small, refs = refs[:terms], refs[terms:]
    size = (len(refs) - 10) // 2
    x, (dq, dk, dv), grad, mixed, one, two = split_refs(refs, 1, 3, 4, 2, size, size)
    if terms and size == 2:
        below = fold_small(functools.reduce(jnp.add, [ref[...] for ref in small]))
        for ref in one:
            ref[ref.shape[0] - below.shape[0] :] = below
    x = x[0][...]
    right = jnp.concatenate([dq[...], dk[...]], axis=1)
    store_pieces(spot[1], dot_tn(x, right), one, orders[0])
    out = dot_tn(stack_rows(grad), stack_rows(mixed))
    store_pieces(spot[1], jnp.concatenate([dot_tn(x, dv[...]), out], axis=1), two, orders[1])


def whole_grads(spots, keeps, gots):
    return [
        keep[...].astype(f32) + gots[spot][start : start + rows].astype(f32)
        for keep, (spot, start, rows, _) in zip(keeps, spots)
    ]


def halve_kernel(spots, groups, count, *refs):
    keeps, gots, rest = split_refs(refs, len(spots), count, len(refs) - len(spots) - count)
    leaving = []
    for item, ref, (*_, rows, extra) in zip(whole_grads(spots, keeps, gots), rest, spots):
        item = item.astype(bf16)
        half, body = (rows - extra) // 2, rows - extra
        stays, leaves = item[:half], item[half:body]
        if extra:
            stays, leaves = (jnp.concatenate([part, item[body:]], axis=0) for part in (stays, leaves))
        ref[...] = stays
        leaving.append(leaves)
    for group, ref in zip(groups, rest[len(spots) :]):
        ref[...] = jnp.concatenate([leaving[spot] for spot in group], axis=0)


def place_rows(head, piece, groups=4):
    return jnp.concatenate([jnp.where(head == item, piece, 0.0) for item in range(groups)], axis=1)


def collect_kernel(spot, *refs):
    rows = []
    for layer in range(len(refs) // 4):
        mix, feed, up, qv = refs[4 * layer : 4 * layer + 4]
        cols = qv.shape[1] // 2
        rows += [place_rows(spot[2], qv[:1, :cols]), place_rows(spot[2], qv[:1, cols:])]
        rows += [mix[:3, :], feed[:3, :]]
        rows += [jnp.where(spot[2] == item, up[:1, :], 0.0) for item in range(4)]
    refs[-1][...] = jnp.concatenate(rows, axis=0)


def assemble_kernel(spots, count, depth, *refs):
    keeps, gots, refs = split_refs(refs, len(spots), count, len(refs) - len(spots) - count)
    grads = whole_grads(spots, keeps, gots)
    g_q, g_k, g_v, g_o, g_up, g_down, *vectors, s_bu = refs
    own, cols = g_q.shape[1:]
    below = grads[2][own:]
    half = below.shape[0] // 2
    small = jnp.concatenate([below[:half], below[half:]], axis=1)
    model = small.shape[1]
    for layer in range(depth):
        up, down, one, two = grads[4 * layer : 4 * layer + 4]
        g_up[layer] = up
        g_down[layer] = down
        g_q[layer] = one[:own, :cols]
        g_k[layer] = one[:own, cols:]
        g_v[layer] = two[:, :cols]
        g_o[layer] = two[:, cols:].T
        rows = small[12 * layer : 12 * layer + 12]
        for item, ref in enumerate(vectors):
            ref[layer : layer + 1, :] = rows[item : item + 1, :]
        for item in range(4):
            s_bu[layer : layer + 1, item * model : (item + 1) * model] = rows[8 + item : 9 + item, :]


class Scalar:
    def __init__(self, array):
        self.array = array


class Far:
    def __init__(self, array):
        self.array = array


class Stay:
    def __init__(self, shape, kind):
        self.shape, self.kind = shape, kind


class View:
    def __init__(self, array, pieces=1):
        self.array, self.pieces = array, pieces


def call(kernel, name, ins, outs, vmem, scratch=()):
    arrays, specs, pieces = [], [], {}
    for spot, item in enumerate(ins):
        space = pltpu.VMEM
        if isinstance(item, Scalar):
            space = pltpu.SMEM
            arrays.append(item.array)
        elif isinstance(item, Far):
            space = pltpu.HBM
            arrays.append(pltpu.with_memory_space_constraint(item.array, pltpu.HBM))
        elif isinstance(item, View):
            arrays.append(pltpu.with_memory_space_constraint(item.array, pltpu.VMEM))
            pieces[spot] = item.pieces
        else:
            arrays.append(item)
        specs.append(pl.BlockSpec(memory_space=space))
    shapes = []
    for item in outs:
        if isinstance(item, Stay):
            shapes.append(pltpu.VMEM(item.shape, item.kind))
        else:
            shapes.append(jax.ShapeDtypeStruct(*item))

    def wrapped(*refs):
        kernel(*(Viewed(ref, pieces[spot]) if spot in pieces else ref for spot, ref in enumerate(refs)))

    return pl.pallas_call(
        wrapped,
        name=name,
        grid=(1,),
        out_shape=shapes,
        in_specs=specs,
        out_specs=[pl.BlockSpec(memory_space=pltpu.VMEM)] * len(shapes),
        scratch_shapes=scratch,
        compiler_params=pltpu.CompilerParams(vmem_limit_bytes=int(vmem * MIB)),
        cost_estimate=pl.CostEstimate(flops=int(GIGA.get(name, 0) * 1e9) + 1, bytes_accessed=1, transcendentals=0),
    )(*arrays)


def grad_outs(rows, cols, order, extra=0):
    pieces = 1 << len(order)
    if (rows // pieces) % 16:
        return [((rows, cols), bf16)]
    return [((rows // 2 + extra, cols), bf16)] * 2


def start_halving(parts, place, orders, small=()):
    half = len(parts) // 2
    extras = [2 * small[0].shape[0] if small else 0, 0]
    if half == 1:
        pairs = []
        for part, order, extra in zip(parts, orders, extras):
            pieces = 1 << len(order)
            whole = part.reshape(pieces, -1, part.shape[1])
            ranks = []
            for spot in range(pieces):
                ranks.append(
                    sum(((spot >> (len(order) - 1 - step)) & 1) << bit for step, bit in enumerate(order))
                )
            whole = jnp.take(whole, jnp.array(ranks, jnp.int32) ^ place, axis=0).reshape(part.shape)
            pair = (whole[: part.shape[0] // 2], whole[part.shape[0] // 2 :])
            if extra:
                below = fold_small(functools.reduce(jnp.add, small))
                pair = tuple(jnp.concatenate([item, below], axis=0) for item in pair)
            pairs.append(pair)
    else:
        pairs = (parts[:2], parts[2:])
    return Halving(*zip(*pairs), orders, extras)


def body(
    hidden_in, w_query, w_key, w_value, b_query, b_value, w_out, b_out, ln1_gain, ln1_bias,
    w_up, b_up, w_down, b_down, ln2_gain, ln2_bias, token_mask, query_order, key_order,
    out_cotangent,
):
    depth, model, cols = w_query.shape
    rows = hidden_in.shape[0]
    units = w_up.shape[2]
    pack = token_mask.shape[0]
    heads = query_order.shape[1]
    head = lax.axis_index("head").astype(jnp.int32)
    groups = lax.axis_size("head")
    place = lax.axis_index("dp").astype(jnp.int32)
    spot = Scalar(jnp.stack([head * rows, place, head]))
    bits = lax.axis_size("dp").bit_length() - 1
    order_one = tuple(range(bits))
    order_two = order_one[:2][::-1] + order_one[2:]
    orders = (order_one, order_two)
    w_query, w_key, w_value = (item.transpose(0, 2, 1) for item in (w_query, w_key, w_value))
    q_order, k_order = query_order.transpose(1, 0, 2), key_order.transpose(1, 0, 2)

    wide = (rows, model)
    dense = 2 * rows * model
    wide_low, wide_full = (wide, bf16), (wide, f32)

    low = hidden_in
    chip, core = swap(low, "head", 2), swap(low, "head", 1)
    around = token_mask.reshape(groups, rows)
    live = jnp.concatenate(
        [lax.dynamic_index_in_dim(around, head ^ item, 0, keepdims=False) for item in range(groups)]
    )
    live = live.astype(f32).reshape(pack, 1)

    entry = hidden_in
    kept = []
    pair = 2 * rows
    two = 2 * HEAD_DIM
    kept_rows = [Stay((heads, pair, pack), bf16), Stay((heads, pair, two), f32), Stay((pair, cols), bf16)]
    other_units = [swap(item, "head", 1) for item in (w_up, b_up, w_down)]
    for layer in range(depth):
        *marks, weights = call(
            functools.partial(cluster_kernel, layer), "clusters",
            [spot, q_order, k_order, live, Far(w_query), Far(w_key), Far(w_value)],
            [((heads, pack, two), bf16)] * 2 + [((heads, 2 * two, model), bf16)], vmem=7,
            scratch=[pltpu.VMEM((3, cols, model), bf16), pltpu.SemaphoreType.DMA((3,))],
        )
        if not layer:
            chip, other_units[1] = tie((chip, other_units[1]))
        chip = tie(chip, weights)
        cross = swap(chip, "head", 1)
        if not layer:
            cross, other_units[0], other_units[2] = tie((cross, other_units[0], other_units[2]))
            ups, biases, downs = zip((w_up, b_up, w_down), other_units)
        w_mine = tie(w_out[layer], chip)
        w_core, w_chip = swap(w_mine, "head", 1), swap(w_mine, "head", 2)
        q_all, kv_all, ob2, ob3, raised_far, out_far, ob_far, x_kept = call(
            functools.partial(attend_kernel, layer), "attend",
            [low, core, chip, cross, weights, b_query, b_value, *marks],
            [((heads, pack, two), bf16)] * 2 + [((rows, cols), bf16)] * 2 + kept_rows
            + [Stay((pack, model), bf16)], vmem=6,
        )
        got2, got3 = swap(ob2, "head", 2), swap(ob3, "head", 3)
        ob0, ob1, raised_near, out_near, ob_near, *q_kept, kv_kept = call(
            attend_near_kernel, "attend_near", [q_all, kv_all, marks[1]],
            [((rows, cols), bf16)] * 2 + kept_rows + [Stay((heads, pair, two), bf16)] * 2
            + [Stay((heads, pack, two), bf16)], vmem=4,
        )
        got1 = swap(ob1, "head", 1)
        got1, got2, got3, w_core, w_chip = tie((got1, got2, got3, w_core, w_chip))
        w_cross = swap(w_chip, "head", 1)
        outs = (w_mine, w_core, w_chip, w_cross)
        got = [ob0, got1, got2, got3]
        normed1, low1, normed1_kept, w_kept = call(
            functools.partial(mix_kernel, layer), "mix",
            [*got, *outs, entry, b_out, ln1_gain, ln1_bias, ln2_gain, ln2_bias],
            [wide_full, wide_low, Stay((rows, model + CLUSTER), f32), Stay((4, cols, model), bf16)], vmem=4,
        )

        def feed(block, kind):
            def kernel(x, up, up2, bias, bias2, down, down2, x_kept, act, act2, slope, out):
                feed_kernel(layer, x, (up, up2), (bias, bias2), (down, down2), x_kept, (act, act2), slope, out)

            return call(
                kernel, "feed", [block, *ups, *biases, *downs],
                [Stay(wide, bf16), Stay((rows, units), bf16), ((rows, units), bf16),
                 Stay((rows, 2 * units), bf16), (wide, kind)], vmem=5.5,
            )

        def turn_weights(up, up2, bias, bias2, down, down2, *outs):
            turn_weights_kernel(layer, (up, up2), (bias, bias2), (down, down2), outs[:2], outs[2:4], outs[4:6])
            for out in outs[6:]:
                out[...] = down2[...]

        def feed_turned(x, up, up2, bias, bias2, down, down2, x_kept, act, act2, slope, out):
            feed_turned_kernel(x, (up, up2), (bias, bias2), (down, down2), x_kept, (act, act2), slope, out)

        chip = swap(low1, "head", 2)
        turned = call(
            turn_weights, "turn_weights", [*tie([*ups, *biases, *downs], low1)],
            [((units, model), bf16)] * 2 + [((units, CLUSTER), f32)] * 2 + [((model, units), bf16)] * 2
            + [Stay(w_down.shape, bf16)] * (not layer), vmem=4 + 3 * (not layer),
        )
        if not layer:
            *turned, other_down = turned
            downs = (w_down, other_down)
        h_own, act_own, act_core, slope_own, own_term = feed(low1, f32)
        chip = tie(chip, own_term, turned)
        h_chip, act_chip, act_cross, slope_chip, far_term = call(
            feed_turned, "feed_turned", [chip, *turned],
            [Stay(wide, bf16), Stay((units, rows), bf16), ((units, rows), bf16), Stay((2 * units, rows), bf16),
             wide_low], vmem=5.5,
        )
        far = swap(far_term, "head", 2)
        away = [swap(item, "head", 1) for item in tie((h_own, act_core, h_chip, act_cross), far_term)]
        ends = [normed1, ln1_gain, ln1_bias, own_term, far, b_down, ln2_gain, ln2_bias]
        kept.append(
            (x_kept, (kv_kept, q_kept), ((out_near, raised_near), (out_far, raised_far)), (ob_near, ob_far),
             normed1_kept, w_kept, (slope_own, slope_chip))
        )
        if layer + 1 < depth:
            entry, low, normed2_kept = call(
                functools.partial(close_kernel, layer), "close", ends,
                [wide_full, wide_low, Stay((rows, model + CLUSTER), f32)], vmem=4,
            )
            kept[-1] += (normed2_kept,)
            low, away = tie((low, away))
            chip, core = swap(low, "head", 2), swap(low, "head", 1)
        else:
            result, low, sums2, d_second = call(
                functools.partial(turn_kernel, layer), "turn", ends + [out_cotangent],
                [wide_full, wide_low, ((8, model), f32), Stay(*wide_full)], vmem=4,
            )
            low, away = tie((low, away))
        h_core, act_core, h_cross, act_cross = away
        kept[-1] += ((h_own, h_core, h_chip, h_cross), (act_own, act_core, act_chip, act_cross))

    feed_sums = attend_sums = None
    grads, small = [None] * depth, [None] * depth
    pieces = heads
    for layer in reversed(range(depth)):
        x_kept, (kv_kept, q_kept), (near, far_rows), obs, normed1, w_kept, slopes, *_, h_kept, acts = kept[layer]
        above = feed_sums is not None

        def feed_back(grad, up, up2, down, down2, slope, pre, pre2, out):
            feed_back_kernel(layer, grad, (up, up2), (down, down2), slope, (pre, pre2), out)

        def feed_back_turned(grad, up, up2, down, down2, slope, pre, pre2, out):
            feed_back_turned_kernel(layer, grad, (up, up2), (down, down2), slope, (pre, pre2), out)

        chip, g_core = swap(low, "head", 2), swap(low, "head", 1)
        pre_own, pre_core, own_term = call(
            feed_back, "feed_back", [low, *ups, *downs, View(slopes[0])],
            [((rows, units), bf16)] * 2 + [wide_full], vmem=4,
        )
        chip, g_core = join((chip, g_core), [feed_sums, attend_sums] if above else [], own_term)
        g_cross = swap(chip, "head", 1)
        pre_chip, pre_cross, far_term = call(
            feed_back_turned, "feed_back_turned", [chip, *ups, *downs, View(slopes[1])],
            [((units, rows), bf16)] * 2 + [wide_low], vmem=5,
        )
        far_term, g_cross = tie((far_term, g_cross))
        far = swap(far_term, "head", 2)
        pre_core, pre_cross = [swap(item, "head", 1) for item in tie((pre_core, pre_cross), far_term)]
        g_blocks = (low, g_core, chip, g_cross)
        added = ()
        if above and attend_sums.more():
            added = advance([attend_sums], far_term)
        *parts, up_sums = call(
            functools.partial(feed_grad_kernel, orders), "feed_grad",
            [spot, *tie((pre_own, pre_core, pre_chip, pre_cross), added), *map(View, h_kept), *g_blocks,
             *map(View, acts)],
            grad_outs(model, units, order_one) + grad_outs(model, units, order_two) + [((8, units), f32)],
            vmem=9,
        )
        far = tie(far, parts)
        if above:
            parts = join(parts, [attend_sums])
        waiting = attend_sums
        feed_sums = start_halving(parts, place, orders)
        low, *d_obs, sums1, d_first = call(
            functools.partial(mix_back_kernel, layer), "mix_back",
            [View(d_second), View(normed1), View(w_kept, 4), own_term, far, ln1_gain],
            [wide_low] + [((rows, cols), bf16)] * 4 + [((8, model), f32), Stay(*wide_full)], vmem=4,
        )
        got = [d_obs[0]] + [swap(d_obs[item], "head", item) for item in (1, 2, 3)]

        def kept_part(part, start):
            out, raised = part
            raised = View(raised.reshape(heads * pair, pack), pieces)
            return [
                View(kv_kept, heads), View(out, heads), raised,
                View(q_kept[start // pair], heads),
            ]

        near_q, near_k, near_v = call(
            attend_back_near_kernel, "attend_back_near",
            kept_part(near, 0) + got[:2],
            [((pair, cols), bf16)] + [((cols, pack), f32)] * 2, vmem=4.5,
        )
        got = tie(got, near_q)
        others = [item for item in (feed_sums, waiting) if item]
        got = join(got, others)
        if any(item.more() for item in others):
            got = tie(got, advance(others))
        low = tie(low, got)
        chip, core = swap(low, "head", 2), swap(low, "head", 1)
        d_q, d_k, d_v, own_term, core_term, chip_term, cross_term, sums_qv = call(
            functools.partial(attend_back_kernel, layer), "attend_back",
            kept_part(far_rows, pair)
            + [got[2], got[3], near_q, near_k, near_v, w_query, w_key, w_value],
            [((pack, cols), bf16)] * 3 + [wide_full, wide_low, wide_full, wide_low]
            + [((8, 2 * cols), f32)], vmem=7.5,
        )
        others = [item for item in (feed_sums, waiting) if item]
        chip, core, core_term, cross_term = join((chip, core, core_term, cross_term), others)
        got_chip, got_core = swap(cross_term, "head", 1), swap(core_term, "head", 1)
        cross = swap(chip, "head", 1)
        small[layer] = [sums1, sums2, up_sums, sums_qv]
        last = ()
        if not layer:
            mine = call(
                collect_kernel, "collect", [spot] + [item for part in small for item in part],
                [((12 * depth, model), f32)], vmem=3,
            )[0]
            last = (mine, swap(mine, "head", 1))
        got_chip, got_core, last = tie((got_chip, got_core, last))
        merged = (chip_term + got_chip.astype(f32)).astype(bf16)
        if not layer:
            total = last[0] + last[1]
            last = (total, swap(total, "head", 2))
        a_blocks = (low, core, chip, cross)
        added = ()
        if any(item.more() for item in others):
            added = advance(others, merged, apart=bool(layer))
        if not layer:
            merged, last = tie((merged, last), added)
        far = swap(merged, "head", 2)
        parts = call(
            functools.partial(attend_grad_kernel, orders, len(last)), "attend_grad",
            [spot, *last, View(x_kept), *tie((d_q, d_k, d_v), merged, added), *a_blocks, *map(View, obs)],
            grad_outs(model, 2 * cols, order_one, 0 if layer else 24 * depth)
            + grad_outs(model, 2 * cols, order_two), vmem=6,
        )
        if layer:
            far = land(far, [feed_sums.slots[0][0]], parts)
        attend_sums = start_halving(parts, place, orders, last)
        grads[layer] = (feed_sums, attend_sums)
        if layer:
            low, sums2, d_second = call(
                functools.partial(open_back_kernel, layer - 1), "open_back",
                [View(kept[layer - 1][-3]), View(d_first), own_term, got_core, far, ln2_gain],
                [wide_low, ((8, model), f32), Stay(*wide_full)], vmem=4,
            )

    far = join(far, [feed_sums])
    d_rows = call(close_back_kernel, "close_back", [View(d_first), own_term, got_core, far], [wide_full], vmem=4)[0]
    d_rows = join(d_rows, [attend_sums])
    while attend_sums.more():
        advance([attend_sums], d_rows)
    items = [item for layer in grads for item in layer]
    while any(item.more() for item in items):
        advance(items)
    ends = [keep for item in items for keep in item.keeps] + [item.got for item in transfers_of(items)]
    own = ends[0].shape[0]
    g_q, g_k, g_v, g_o, g_up, g_down, s_bq, s_bv, s_bo, s_g1, s_n1, s_bd, s_g2, s_n2, s_bu = call(
        functools.partial(assemble_kernel, spots_of(items), len(transfers_of(items)), depth), "assemble", ends,
        [((depth, own, cols), f32)] * 3 + [((depth, cols, own), f32)] + [((depth, own, units), f32)] * 2
        + [((depth, model), f32)] * 8 + [((depth, groups * units), f32)], vmem=8,
    )
    return (
        result, d_rows, g_q, g_k, g_v, s_bq, s_bv, g_o, s_bo, s_g1, s_n1, g_up,
        s_bu, g_down.transpose(0, 2, 1), s_bd, s_g2, s_n2,
    )


def solution(mesh):
    split = P(("dp", "head"), None)
    column, line = P(None, None, "head"), P(None, "head", None)
    placed = (
        split, column, column, column, P(None, "head"), P(None, "head"), line, P(), P(), P(),
        column, P(None, "head"), line, P(), P(), P(),
        P("dp"), P(None, "head", "dp"), P(None, "head", "dp"), split,
    )
    by_rows, by_cols = P(None, "dp", "head"), P(None, "head", "dp")
    results = (
        split, split, by_rows, by_rows, by_rows, P(), P(), by_cols, P(), P(), P(), by_rows, P(),
        by_cols, P(), P(), P(),
    )
    return jax.shard_map(body, mesh=mesh, in_specs=placed, out_specs=results, check_vma=False)
```

```python
import functools
import math

import jax
import jax.numpy as jnp
from jax import lax
from jax.experimental import pallas as pl
from jax.experimental.pallas import tpu as pltpu
from jax.sharding import PartitionSpec as P

CLUSTER = 128
HEAD_DIM = 64
EPS = 1e-12
NEG = -1e30
MIB = 1024 * 1024
GIGA = {"attend_back_near": 3, "finish": 3}

f32 = jnp.float32
bf16 = jnp.bfloat16


def swap(array, axis, bit):
    size = lax.axis_size(axis)
    return lax.ppermute(array, axis, [(item, item ^ bit) for item in range(size)])


def tie(value, *earlier):
    return lax.optimization_barrier((value, earlier))[0]


class Transfer:
    def __init__(self, send, bit):
        self.got = swap(send, "dp", 1 << bit)


class Halving:
    def __init__(self, keeps, sends, orders, extras):
        self.keeps, self.orders, self.extras = list(keeps), [list(order) for order in orders], extras
        self.slots = [(Transfer(send, order.pop(0)), 0) for send, order in zip(sends, self.orders)]

    def more(self):
        return bool(self.orders[0])


def transfers_of(items):
    found = []
    for item in items:
        for transfer, _ in item.slots:
            if transfer not in found:
                found.append(transfer)
    return found


def spots_of(items):
    found = transfers_of(items)
    return [
        (found.index(transfer), start, keep.shape[0], extra)
        for item in items
        for keep, (transfer, start), extra in zip(item.keeps, item.slots, item.extras)
    ]


def join(value, items, *earlier):
    return land(value, transfers_of(items), *earlier)


def land(value, found, *earlier):
    value, gots, _ = lax.optimization_barrier((value, [item.got for item in found], earlier))
    for item, got in zip(found, gots):
        item.got = got
    return value


def advance(items, *earlier, apart=False):
    items = [item for item in items if item.more()]
    found = transfers_of(items)
    keeps = [keep for item in items for keep in item.keeps]
    keeps, gots = tie((keeps, [item.got for item in found]), *earlier)
    extras = [extra for item in items for extra in item.extras]
    outs = [(((keep.shape[0] - extra) // 2 + extra, keep.shape[1]), bf16) for keep, extra in zip(keeps, extras)]
    groups = {}
    bits = [order.pop(0) for item in items for order in item.orders]
    for spot, (bit, out) in enumerate(zip(bits, outs)):
        groups.setdefault((bit, out[0][1], spot if apart else 0), []).append(spot)
    sends = []
    for (_, cols, _), group in groups.items():
        sends.append(((sum(outs[spot][0][0] for spot in group), cols), bf16))
    parts = call(
        functools.partial(halve_kernel, spots_of(items), list(groups.values()), len(gots)), "halve",
        [*keeps, *gots], outs + sends, vmem=8,
    )
    slots = [None] * len(keeps)
    for (bit, *_), group, send in zip(groups, groups.values(), parts[len(keeps) :]):
        transfer, start = Transfer(send, bit), 0
        for spot in group:
            slots[spot] = (transfer, start)
            start += outs[spot][0][0]
    start = 0
    for item in items:
        stop = start + len(item.keeps)
        item.keeps, item.slots = parts[start:stop], slots[start:stop]
        start = stop
    return parts


def dot(left, right):
    return jnp.dot(left, right, preferred_element_type=f32)


def dot_nt(left, right):
    return lax.dot_general(left, right, (((1,), (1,)), ((), ())), preferred_element_type=f32)


def dot_tn(left, right):
    return lax.dot_general(left, right, (((0,), (0,)), ((), ())), preferred_element_type=f32)


def row(ref, layer):
    return ref[layer : layer + 1, :]


def normalise(rows):
    centre = rows - jnp.mean(rows, axis=-1, keepdims=True)
    spread = jnp.mean(centre * centre, axis=-1, keepdims=True)
    scale = lax.rsqrt(spread + EPS)
    return centre * scale, scale


def normalise_back(grad, gain, normed, scale):
    part = grad * gain
    mean_one = jnp.mean(part, axis=-1, keepdims=True)
    mean_two = jnp.mean(part * normed, axis=-1, keepdims=True)
    return (part - mean_one - normed * mean_two) * scale


def store_sums(ref, *arrays):
    rows = [jnp.sum(item, axis=0, keepdims=True) for item in arrays]
    rows.append(jnp.zeros((ref.shape[0] - len(rows), ref.shape[1]), f32))
    ref[...] = jnp.concatenate(rows, axis=0)


def gelu_pair(values):
    bell = jnp.exp(values * values * -0.5)
    t = 1.0 / (1.0 + (0.3275911 * math.sqrt(0.5)) * jnp.abs(values))
    poly = 0.5 * 1.061405429
    for factor in (-1.453152027, 1.421413741, -0.284496736, 0.254829592):
        poly = poly * t + 0.5 * factor
    tail = poly * t * bell
    cdf = jnp.where(values >= 0.0, 1.0 - tail, tail)
    return values * cdf, cdf + values * bell * (1.0 / math.sqrt(2.0 * math.pi))


def stack_rows(refs):
    return jnp.concatenate([ref[...] for ref in refs], axis=0)


def head_cols(array, head):
    return array[:, head * HEAD_DIM : (head + 1) * HEAD_DIM]


def lanes_of(rows):
    return lax.broadcasted_iota(jnp.int32, (rows, 2 * HEAD_DIM), 1)


class Viewed:
    def __init__(self, source, pieces):
        self.source, self.shape, self.size = source, source.shape, source.shape[0] // pieces

    def piece(self, item):
        return self.source[item * self.size : (item + 1) * self.size]

    def __getitem__(self, index):
        return self.source[index]


def cluster_kernel(layer, spot, q_order, k_order, live, wq, wk, wv, q_marks, k_marks, weights, held, sems):
    heads, length, width = q_marks.shape
    copies = [
        pltpu.make_async_copy(source.at[layer], held.at[item], sems.at[item])
        for item, source in enumerate((wq, wk, wv))
    ]
    for copy in copies:
        copy.start()
    count = length // CLUSTER
    lines = lax.broadcasted_iota(jnp.int32, (length, length), 0)
    spread_line = lax.broadcasted_iota(jnp.int32, (length, width), 0) // CLUSTER + HEAD_DIM
    lanes = lanes_of(length)
    spread = jnp.where(spread_line == lanes, 1.0, 0.0).astype(bf16)
    in_use = jnp.logical_and(lanes >= HEAD_DIM, lanes < HEAD_DIM + count)
    for head in range(heads):
        order = q_order[head, layer : layer + 1, :] ^ spot[0]
        hot = jnp.where(order == lines, 1.0, 0.0).astype(bf16)
        q_marks[head] = dot(hot, spread).astype(bf16)
        order = k_order[head, layer : layer + 1, :] ^ spot[0]
        hot = jnp.where(order == lines, 1.0, 0.0).astype(bf16)
        inside = dot(hot, spread) * live[...]
        outside = jnp.where(in_use, jnp.where(inside > 0.5, 0.0, NEG), 0.0)
        k_marks[head] = outside.astype(bf16)
    for copy in copies:
        copy.wait()
    blank = jnp.zeros((HEAD_DIM, held.shape[2]), bf16)
    for head in range(heads):
        part = slice(head * HEAD_DIM, (head + 1) * HEAD_DIM)
        weights[head] = jnp.concatenate([held[0, part], blank, held[1, part], held[2, part]], axis=0)


def attend_rows(first, rows, q_ref, kv_ref, k_marks, raised_kept, out_kept):
    heads, length, width = kv_ref.shape
    chunk = rows
    left = lanes_of(length) < HEAD_DIM
    mixed = []
    for head in range(heads):
        keys = kv_ref[head].astype(f32)
        marked = jnp.where(left, keys, k_marks[head].astype(f32)).astype(bf16)
        values = jnp.where(left, 1.0, keys).astype(bf16)
        outs = []
        for start in range(0, rows, chunk):
            scores = dot_nt(q_ref[head, first + start : first + start + chunk], marked)
            raised = jnp.exp(scores - jnp.max(scores, axis=1, keepdims=True)).astype(bf16)
            raised_kept[head, pl.ds(start, chunk)] = raised
            total = dot(raised, values)
            share = 1.0 / total
            outs.append(jnp.where(left[:chunk], share, total * pltpu.roll(share, HEAD_DIM, 1)))
        outs = jnp.concatenate(outs, axis=0)
        out_kept[head] = outs
        mixed.append(outs[:, HEAD_DIM:])
    return jnp.concatenate(mixed, axis=1).astype(bf16)


def attend_kernel(
    layer, x0, x1, x2, x3, weights, bq, bv, q_marks, k_marks,
    q_out, kv_out, ob2, ob3, raised_kept, out_kept, ob_kept, x_kept,
):
    size = ob2.shape[0]
    for item, ref in enumerate((x0, x1, x2, x3)):
        x_kept[pl.ds(item * size, size)] = ref[...]
    x = stack_rows((x0, x1, x2, x3))
    heads = q_out.shape[0]
    blank_b = jnp.zeros((1, HEAD_DIM), f32)
    bias_q, bias_v = row(bq, layer), row(bv, layer)
    for head in range(heads):
        part = slice(head * HEAD_DIM, (head + 1) * HEAD_DIM)
        bias = jnp.concatenate([bias_q[:, part], blank_b, blank_b, bias_v[:, part]], axis=1)
        qkv = (dot_nt(x, weights[head]) + bias).astype(bf16)
        query = qkv[:, : 2 * HEAD_DIM].astype(f32) * (1.0 / math.sqrt(HEAD_DIM))
        q_out[head] = (query + q_marks[head].astype(f32)).astype(bf16)
        kv_out[head] = qkv[:, 2 * HEAD_DIM :]
    mixed = attend_rows(2 * size, 2 * size, q_out, kv_out, k_marks, raised_kept, out_kept)
    ob_kept[...] = mixed
    ob2[...] = mixed[:size]
    ob3[...] = mixed[size:]


def attend_near_kernel(
    q_in, kv_in, k_marks, ob0, ob1, raised_kept, out_kept, ob_kept, q_near, q_far, kv_kept
):
    size = ob0.shape[0]
    q_near[...] = q_in[:, : 2 * size]
    q_far[...] = q_in[:, 2 * size :]
    kv_kept[...] = kv_in[...]
    mixed = attend_rows(0, 2 * size, q_in, kv_in, k_marks, raised_kept, out_kept)
    ob_kept[...] = mixed
    ob0[...] = mixed[:size]
    ob1[...] = mixed[size:]


def entry_rows(layer, x, gain, shift):
    rows = x[...].astype(f32)
    if layer:
        rows = rows * row(gain, layer - 1) + row(shift, layer - 1)
    return rows


def with_scale(unit, scale):
    return jnp.concatenate([unit, jnp.broadcast_to(scale, (unit.shape[0], CLUSTER))], axis=1)


def mix_kernel(
    layer, ob0, ob1, ob2, ob3, w0, w1, w2, w3, x, b_out, gain1, shift1, gain2, shift2,
    normed, low, normed_kept, w_kept,
):
    total = entry_rows(layer, x, gain2, shift2) + row(b_out, layer)
    for item, (left, right) in enumerate(((ob0, w0), (ob1, w1), (ob2, w2), (ob3, w3))):
        w_kept[item] = right[...]
        total = total + dot(left[...], right[...])
    unit, root = normalise(total)
    normed[...] = unit
    normed_kept[...] = with_scale(unit, root)
    low[...] = (unit * row(gain1, layer) + row(shift1, layer)).astype(bf16)


def store_rows(value, refs):
    start = 0
    for ref in refs:
        ref[...] = value[start : start + ref.shape[0]].astype(ref.dtype)
        start += ref.shape[0]


def feed_kernel(layer, x, ups, biases, downs, x_kept, acts, slope, out):
    rows = x[...]
    x_kept[...] = rows
    total = 0.0
    units = acts[0].shape[1]
    for item in range(2):
        act, der = gelu_pair(dot(rows, ups[item][layer]) + row(biases[item], layer))
        act = act.astype(bf16)
        acts[item][...] = act
        slope[:, item * units : (item + 1) * units] = der.astype(bf16)
        total = total + dot(act, downs[item][layer])
    out[...] = total.astype(out.dtype)


def turn_weights_kernel(layer, ups, biases, downs, ups_t, biases_t, downs_t):
    for item in range(2):
        ups_t[item][...] = ups[item][layer].T
        downs_t[item][...] = downs[item][layer].T
        bias = row(biases[item], layer)
        biases_t[item][...] = jnp.broadcast_to(bias, (CLUSTER, bias.shape[1])).T


def feed_turned_kernel(x, ups_t, biases_t, downs_t, x_kept, acts, slope, out):
    rows = x[...]
    x_kept[...] = rows
    total = 0.0
    units, count = acts[0].shape
    for item in range(2):
        bias = jnp.concatenate([biases_t[item][...]] * (count // CLUSTER), axis=1)
        act, der = gelu_pair(dot_nt(ups_t[item][...], rows) + bias)
        act = act.astype(bf16)
        acts[item][...] = act
        slope[item * units : (item + 1) * units, :] = der.astype(bf16)
        total = total + dot(downs_t[item][...], act)
    out[...] = total.T.astype(out.dtype)


def second_rows(layer, normed1, gain1, shift1, own, far, b_down):
    rows = normed1[...] * row(gain1, layer) + row(shift1, layer)
    return rows + own[...] + far[...].astype(f32) + row(b_down, layer)


def close_kernel(
    layer, normed1, gain1, shift1, own, far, b_down, gain2, shift2, normed, low, normed_kept
):
    unit, root = normalise(
        second_rows(layer, normed1, gain1, shift1, own, far, b_down)
    )
    normed[...] = unit
    normed_kept[...] = with_scale(unit, root)
    low[...] = (unit * row(gain2, layer) + row(shift2, layer)).astype(bf16)


def turn_kernel(
    layer, normed1, gain1, shift1, own, far, b_down, gain2, shift2, grad,
    result, low, sums, d_second,
):
    unit, root = normalise(
        second_rows(layer, normed1, gain1, shift1, own, far, b_down)
    )
    gain = row(gain2, layer)
    result[...] = unit * gain + row(shift2, layer)
    back = normalise_back(grad[...], gain, unit, root)
    d_second[...] = back
    low[...] = back.astype(bf16)
    store_sums(sums, back, grad[...] * unit, grad[...])


def unit_and_scale(kept, width):
    both = kept[...]
    return both[:, :width], both[:, width : width + 1]


def open_back_kernel(layer, normed2, base, own, core, far, gain2, low, sums, d_second):
    rest = own[...] + core[...].astype(f32) + far[...].astype(f32)
    grad = base[...] + rest
    unit, root = unit_and_scale(normed2, grad.shape[1])
    back = normalise_back(grad, row(gain2, layer), unit, root)
    d_second[...] = back
    low[...] = back.astype(bf16)
    store_sums(sums, back, grad * unit, grad)


def feed_back_kernel(layer, grad, ups, downs, slope, pres, out):
    rows = grad[...]
    total = 0.0
    units = pres[0].shape[1]
    for item in range(2):
        der = slope[:, item * units : (item + 1) * units].astype(f32)
        pre = (dot_nt(rows, downs[item][layer]) * der).astype(bf16)
        pres[item][...] = pre
        total = total + dot_nt(pre, ups[item][layer])
    out[...] = total.astype(out.dtype)


def feed_back_turned_kernel(layer, grad, ups, downs, slope, pres, out):
    rows = grad[...]
    total = 0.0
    units = pres[0].shape[0]
    for item in range(2):
        der = slope[item * units : (item + 1) * units, :].astype(f32)
        pre = (dot_nt(downs[item][layer], rows) * der).astype(bf16)
        pres[item][...] = pre
        total = total + dot(ups[item][layer], pre)
    out[...] = total.T.astype(out.dtype)


def mix_back_kernel(
    layer, base, normed1, weights, own, far, gain1, low, d0, d1, d2, d3, sums, d_first
):
    grad = base[...] + own[...] + far[...].astype(f32)
    unit, root = unit_and_scale(normed1, grad.shape[1])
    back = normalise_back(grad, row(gain1, layer), unit, root)
    d_first[...] = back
    small = back.astype(bf16)
    low[...] = small
    for item, out in enumerate((d0, d1, d2, d3)):
        out[...] = dot_nt(small, weights.piece(item)[0]).astype(bf16)
    store_sums(sums, back, grad * unit, grad)


def close_back_kernel(base, own, core, far, out):
    out[...] = base[...] + own[...] + core[...].astype(f32) + far[...].astype(f32)


def attend_back_rows(refs, q_kept, kv_kept, out_kept, raised_kept):
    d_mixed = stack_rows(refs)
    rows = d_mixed.shape[0]
    heads, length, width = kv_kept.shape
    chunk = rows
    steps = rows // chunk
    key_lanes, lanes = lanes_of(length), lanes_of(rows)[:, :HEAD_DIM]
    d_q, d_k, d_v = [], [], []
    for head in range(heads):
        part = slice(head * HEAD_DIM, (head + 1) * HEAD_DIM)
        keys = kv_kept.piece(head)[0]
        both = out_kept.piece(head)[0]
        share, out = both[:, :HEAD_DIM], both[:, HEAD_DIM:]
        grad = (d_mixed[:, part].astype(f32) * share).astype(bf16).astype(f32)
        inner = jnp.sum(grad * out, axis=1, keepdims=True)
        high = inner.astype(bf16).astype(f32)
        middle = (inner - high).astype(bf16).astype(f32)
        low = inner - high - middle
        terms = jnp.where(
            lanes == 0, -high, jnp.where(lanes == 1, -middle, jnp.where(lanes == 2, -low, 0.0))
        )
        grad = jnp.concatenate([terms, grad], axis=1).astype(bf16)
        values = jnp.where(
            key_lanes < 3, 1.0, jnp.where(key_lanes < HEAD_DIM, 0.0, keys.astype(f32))
        ).astype(bf16)
        d_score, raised = [], []
        for item in range(steps):
            d_prob = dot_nt(grad[item * chunk : (item + 1) * chunk], values)
            raised.append(raised_kept.piece(head * steps + item))
            d_score.append((raised[-1].astype(f32) * d_prob).astype(bf16))
        d_score = jnp.concatenate(d_score, axis=0)
        raised = jnp.concatenate(raised, axis=0)
        query = q_kept.piece(head)[0]
        d_q.append(dot(d_score, keys)[:, :HEAD_DIM] * (1.0 / math.sqrt(HEAD_DIM)))
        d_k.append(dot(query.T[:HEAD_DIM], d_score))
        d_v.append(dot(grad.T[HEAD_DIM:], raised))
    return (
        jnp.concatenate(d_q, axis=1).astype(bf16),
        jnp.concatenate(d_k, axis=0),
        jnp.concatenate(d_v, axis=0),
    )


def attend_back_near_kernel(kv_kept, out_kept, raised_kept, q_kept, d0, d1, d_query, d_k, d_v):
    d_query[...], d_k[...], d_v[...] = attend_back_rows((d0, d1), q_kept, kv_kept, out_kept, raised_kept)


def attend_back_kernel(
    layer, kv_kept, out_kept, raised_kept, q_kept, d2, d3, near_q, near_k, near_v, wq, wk, wv,
    d_query, d_key, d_value, own, core, chip, cross, sums,
):
    d_q, d_k, d_v = attend_back_rows((d2, d3), q_kept, kv_kept, out_kept, raised_kept)
    d_q = jnp.concatenate([near_q[...], d_q], axis=0)
    d_k, d_v = ((item + near[...]).T.astype(bf16) for item, near in ((d_k, near_k), (d_v, near_v)))
    d_query[...] = d_q
    d_key[...] = d_k
    d_value[...] = d_v
    store_sums(sums, jnp.concatenate([d_q.astype(f32), d_v.astype(f32)], axis=1))
    store_rows(dot(d_q, wq[layer]) + dot(d_k, wk[layer]) + dot(d_v, wv[layer]), (own, core, chip, cross))


def store_pieces(place, grad, outs, order):
    if len(outs) == 1:
        outs[0][...] = grad.astype(bf16)
        return
    keep, send = outs
    bits = len(order)
    pieces = 1 << bits
    size = grad.shape[0] // pieces
    for piece in range(pieces):
        rel = place ^ piece
        index = 0
        for step, bit in enumerate(order[1:]):
            index = index + (((rel >> bit) & 1) << (bits - 2 - step))
        value = grad[piece * size : (piece + 1) * size].astype(bf16)
        leaves = (rel >> order[0]) & 1

        @pl.when(leaves == 0)
        def _(value=value, index=index, keep=keep):
            keep[pl.ds(pl.multiple_of(index * size, size), size)] = value

        @pl.when(leaves == 1)
        def _(value=value, index=index, send=send):
            send[pl.ds(pl.multiple_of(index * size, size), size)] = value


def split_refs(refs, *counts):
    parts = []
    for count in counts:
        parts.append(refs[:count])
        refs = refs[count:]
    return parts


def dot_tt(left, right):
    return lax.dot_general(left, right, (((0,), (1,)), ((), ())), preferred_element_type=f32)


def stack_cols(refs):
    return jnp.concatenate([ref[...] for ref in refs], axis=1)


def feed_grad_kernel(orders, spot, *refs):
    size = (len(refs) - 17) // 2
    pre, x, grad, act, one, two, (sums,) = split_refs(refs, 4, 4, 4, 4, size, size, 1)
    pre_near, pre_far = stack_rows(pre[:2]), stack_cols(pre[2:])
    up = dot_tn(stack_rows(x[:2]), pre_near) + dot_tt(stack_rows(x[2:]), pre_far)
    store_pieces(spot[1], up, one, orders[0])
    down = dot_tn(stack_rows(grad[:2]), stack_rows(act[:2])) + dot_tt(stack_rows(grad[2:]), stack_cols(act[2:]))
    store_pieces(spot[1], down, two, orders[1])
    ones = jnp.ones((sums.shape[0], pre_near.shape[0]), bf16)
    sums[...] = dot(ones, pre_near) + dot_nt(ones, pre_far)


def fold_small(rows):
    half = rows.shape[1] // 2
    return jnp.concatenate([rows[:, :half], rows[:, half:]], axis=0).astype(bf16)


def append_kernel(keep, send, small, got, keep_out, send_out):
    below = fold_small(small[...] + got[...])
    keep_out[...] = jnp.concatenate([keep[...], below], axis=0)
    send_out[...] = jnp.concatenate([send[...], below], axis=0)


def finish_kernel(spots, count, *refs):
    keeps, gots, outs = split_refs(refs, len(spots), count, len(spots))
    for item, ref in zip(whole_grads(spots, keeps, gots), outs):
        ref[...] = item


def attend_grad_kernel(orders, spot, *refs):
    size = (len(refs) - 10) // 2
    x, (dq, dk, dv), grad, mixed, one, two = split_refs(refs, 1, 3, 4, 2, size, size)
    x = x[0][...]
    right = jnp.concatenate([dq[...], dk[...]], axis=1)
    store_pieces(spot[1], dot_tn(x, right), one, orders[0])
    out = dot_tn(stack_rows(grad), stack_rows(mixed))
    store_pieces(spot[1], jnp.concatenate([dot_tn(x, dv[...]), out], axis=1), two, orders[1])


def whole_grads(spots, keeps, gots):
    return [
        keep[...].astype(f32) + gots[spot][start : start + rows].astype(f32)
        for keep, (spot, start, rows, _) in zip(keeps, spots)
    ]


def halve_kernel(spots, groups, count, *refs):
    keeps, gots, rest = split_refs(refs, len(spots), count, len(refs) - len(spots) - count)
    leaving = []
    for item, ref, (*_, rows, extra) in zip(whole_grads(spots, keeps, gots), rest, spots):
        item = item.astype(bf16)
        half, body = (rows - extra) // 2, rows - extra
        stays, leaves = item[:half], item[half:body]
        if extra:
            stays, leaves = (jnp.concatenate([part, item[body:]], axis=0) for part in (stays, leaves))
        ref[...] = stays
        leaving.append(leaves)
    for group, ref in zip(groups, rest[len(spots) :]):
        ref[...] = jnp.concatenate([leaving[spot] for spot in group], axis=0)


def place_rows(head, piece, groups=4):
    return jnp.concatenate([jnp.where(head == item, piece, 0.0) for item in range(groups)], axis=1)


def collect_kernel(spot, *refs):
    rows = []
    for layer in range(len(refs) // 4):
        mix, feed, up, qv = refs[4 * layer : 4 * layer + 4]
        cols = qv.shape[1] // 2
        rows += [place_rows(spot[2], qv[:1, :cols]), place_rows(spot[2], qv[:1, cols:])]
        rows += [mix[:3, :], feed[:3, :]]
        rows += [jnp.where(spot[2] == item, up[:1, :], 0.0) for item in range(4)]
    refs[-1][...] = jnp.concatenate(rows, axis=0)


def assemble_kernel(spots, count, depth, *refs):
    keeps, gots, refs = split_refs(refs, len(spots), count, len(refs) - len(spots) - count)
    done, refs = refs[:2], refs[2:]
    grads = [ref[...] for ref in done] + whole_grads(spots, keeps, gots)
    g_q, g_k, g_v, g_o, g_up, g_down, *vectors, s_bu = refs
    own, cols = g_q.shape[1:]
    below = grads[2][own:]
    half = below.shape[0] // 2
    small = jnp.concatenate([below[:half], below[half:]], axis=1)
    model = small.shape[1]
    for layer in range(depth):
        up, down, one, two = grads[4 * layer : 4 * layer + 4]
        g_up[layer] = up
        g_down[layer] = down
        g_q[layer] = one[:own, :cols]
        g_k[layer] = one[:own, cols:]
        g_v[layer] = two[:, :cols]
        g_o[layer] = two[:, cols:].T
        rows = small[12 * layer : 12 * layer + 12]
        for item, ref in enumerate(vectors):
            ref[layer : layer + 1, :] = rows[item : item + 1, :]
        for item in range(4):
            s_bu[layer : layer + 1, item * model : (item + 1) * model] = rows[8 + item : 9 + item, :]


class Scalar:
    def __init__(self, array):
        self.array = array


class Far:
    def __init__(self, array):
        self.array = array


class Stay:
    def __init__(self, shape, kind):
        self.shape, self.kind = shape, kind


class View:
    def __init__(self, array, pieces=1):
        self.array, self.pieces = array, pieces


def call(kernel, name, ins, outs, vmem, scratch=()):
    arrays, specs, pieces = [], [], {}
    for spot, item in enumerate(ins):
        space = pltpu.VMEM
        if isinstance(item, Scalar):
            space = pltpu.SMEM
            arrays.append(item.array)
        elif isinstance(item, Far):
            space = pltpu.HBM
            arrays.append(pltpu.with_memory_space_constraint(item.array, pltpu.HBM))
        elif isinstance(item, View):
            arrays.append(pltpu.with_memory_space_constraint(item.array, pltpu.VMEM))
            pieces[spot] = item.pieces
        else:
            arrays.append(item)
        specs.append(pl.BlockSpec(memory_space=space))
    shapes = []
    for item in outs:
        if isinstance(item, Stay):
            shapes.append(pltpu.VMEM(item.shape, item.kind))
        else:
            shapes.append(jax.ShapeDtypeStruct(*item))

    def wrapped(*refs):
        kernel(*(Viewed(ref, pieces[spot]) if spot in pieces else ref for spot, ref in enumerate(refs)))

    return pl.pallas_call(
        wrapped,
        name=name,
        grid=(1,),
        out_shape=shapes,
        in_specs=specs,
        out_specs=[pl.BlockSpec(memory_space=pltpu.VMEM)] * len(shapes),
        scratch_shapes=scratch,
        compiler_params=pltpu.CompilerParams(vmem_limit_bytes=int(vmem * MIB)),
        cost_estimate=pl.CostEstimate(flops=int(GIGA.get(name, 0) * 1e9) + 1, bytes_accessed=1, transcendentals=0),
    )(*arrays)


def grad_outs(rows, cols, order, extra=0):
    pieces = 1 << len(order)
    if (rows // pieces) % 16:
        return [((rows, cols), bf16)]
    return [((rows // 2 + extra, cols), bf16)] * 2


def start_halving(parts, place, orders, small=()):
    half = len(parts) // 2
    extras = [2 * small[0].shape[0] if small else 0, 0]
    if half == 1:
        pairs = []
        for part, order, extra in zip(parts, orders, extras):
            pieces = 1 << len(order)
            whole = part.reshape(pieces, -1, part.shape[1])
            ranks = []
            for spot in range(pieces):
                ranks.append(
                    sum(((spot >> (len(order) - 1 - step)) & 1) << bit for step, bit in enumerate(order))
                )
            whole = jnp.take(whole, jnp.array(ranks, jnp.int32) ^ place, axis=0).reshape(part.shape)
            pair = (whole[: part.shape[0] // 2], whole[part.shape[0] // 2 :])
            if extra:
                below = fold_small(functools.reduce(jnp.add, small))
                pair = tuple(jnp.concatenate([item, below], axis=0) for item in pair)
            pairs.append(pair)
    else:
        pairs = (parts[:2], parts[2:])
    return Halving(*zip(*pairs), orders, extras)


def body(
    hidden_in, w_query, w_key, w_value, b_query, b_value, w_out, b_out, ln1_gain, ln1_bias,
    w_up, b_up, w_down, b_down, ln2_gain, ln2_bias, token_mask, query_order, key_order,
    out_cotangent,
):
    depth, model, cols = w_query.shape
    rows = hidden_in.shape[0]
    units = w_up.shape[2]
    pack = token_mask.shape[0]
    heads = query_order.shape[1]
    head = lax.axis_index("head").astype(jnp.int32)
    groups = lax.axis_size("head")
    place = lax.axis_index("dp").astype(jnp.int32)
    spot = Scalar(jnp.stack([head * rows, place, head]))
    bits = lax.axis_size("dp").bit_length() - 1
    order_one = tuple(range(bits))
    order_two = order_one[:2][::-1] + order_one[2:]
    orders = (order_one, order_two)
    w_query, w_key, w_value = (item.transpose(0, 2, 1) for item in (w_query, w_key, w_value))
    q_order, k_order = query_order.transpose(1, 0, 2), key_order.transpose(1, 0, 2)

    wide = (rows, model)
    dense = 2 * rows * model
    wide_low, wide_full = (wide, bf16), (wide, f32)

    low = hidden_in
    chip, core = swap(low, "head", 2), swap(low, "head", 1)
    around = token_mask.reshape(groups, rows)
    live = jnp.concatenate(
        [lax.dynamic_index_in_dim(around, head ^ item, 0, keepdims=False) for item in range(groups)]
    )
    live = live.astype(f32).reshape(pack, 1)

    entry = hidden_in
    kept = []
    pair = 2 * rows
    two = 2 * HEAD_DIM
    kept_rows = [Stay((heads, pair, pack), bf16), Stay((heads, pair, two), f32), Stay((pair, cols), bf16)]
    other_units = [swap(item, "head", 1) for item in (w_up, b_up, w_down)]
    for layer in range(depth):
        *marks, weights = call(
            functools.partial(cluster_kernel, layer), "clusters",
            [spot, q_order, k_order, live, Far(w_query), Far(w_key), Far(w_value)],
            [((heads, pack, two), bf16)] * 2 + [((heads, 2 * two, model), bf16)], vmem=7,
            scratch=[pltpu.VMEM((3, cols, model), bf16), pltpu.SemaphoreType.DMA((3,))],
        )
        if not layer:
            chip, other_units[1] = tie((chip, other_units[1]))
        chip = tie(chip, weights)
        cross = swap(chip, "head", 1)
        if not layer:
            cross, other_units[0], other_units[2] = tie((cross, other_units[0], other_units[2]))
            ups, biases, downs = zip((w_up, b_up, w_down), other_units)
        w_mine = tie(w_out[layer], chip)
        w_core, w_chip = swap(w_mine, "head", 1), swap(w_mine, "head", 2)
        q_all, kv_all, ob2, ob3, raised_far, out_far, ob_far, x_kept = call(
            functools.partial(attend_kernel, layer), "attend",
            [low, core, chip, cross, weights, b_query, b_value, *marks],
            [((heads, pack, two), bf16)] * 2 + [((rows, cols), bf16)] * 2 + kept_rows
            + [Stay((pack, model), bf16)], vmem=6,
        )
        got2, got3 = swap(ob2, "head", 2), swap(ob3, "head", 3)
        ob0, ob1, raised_near, out_near, ob_near, *q_kept, kv_kept = call(
            attend_near_kernel, "attend_near", [q_all, kv_all, marks[1]],
            [((rows, cols), bf16)] * 2 + kept_rows + [Stay((heads, pair, two), bf16)] * 2
            + [Stay((heads, pack, two), bf16)], vmem=4,
        )
        got1 = swap(ob1, "head", 1)
        got1, got2, got3, w_core, w_chip = tie((got1, got2, got3, w_core, w_chip))
        w_cross = swap(w_chip, "head", 1)
        outs = (w_mine, w_core, w_chip, w_cross)
        got = [ob0, got1, got2, got3]
        normed1, low1, normed1_kept, w_kept = call(
            functools.partial(mix_kernel, layer), "mix",
            [*got, *outs, entry, b_out, ln1_gain, ln1_bias, ln2_gain, ln2_bias],
            [wide_full, wide_low, Stay((rows, model + CLUSTER), f32), Stay((4, cols, model), bf16)], vmem=4,
        )

        def feed(block, kind):
            def kernel(x, up, up2, bias, bias2, down, down2, x_kept, act, act2, slope, out):
                feed_kernel(layer, x, (up, up2), (bias, bias2), (down, down2), x_kept, (act, act2), slope, out)

            return call(
                kernel, "feed", [block, *ups, *biases, *downs],
                [Stay(wide, bf16), Stay((rows, units), bf16), ((rows, units), bf16),
                 Stay((rows, 2 * units), bf16), (wide, kind)], vmem=5.5,
            )

        def turn_weights(up, up2, bias, bias2, down, down2, *outs):
            turn_weights_kernel(layer, (up, up2), (bias, bias2), (down, down2), outs[:2], outs[2:4], outs[4:6])
            for out in outs[6:]:
                out[...] = down2[...]

        def feed_turned(x, up, up2, bias, bias2, down, down2, x_kept, act, act2, slope, out):
            feed_turned_kernel(x, (up, up2), (bias, bias2), (down, down2), x_kept, (act, act2), slope, out)

        chip = swap(low1, "head", 2)
        turned = call(
            turn_weights, "turn_weights", [*tie([*ups, *biases, *downs], low1)],
            [((units, model), bf16)] * 2 + [((units, CLUSTER), f32)] * 2 + [((model, units), bf16)] * 2
            + [Stay(w_down.shape, bf16)] * (not layer), vmem=4 + 3 * (not layer),
        )
        if not layer:
            *turned, other_down = turned
            downs = (w_down, other_down)
        h_own, act_own, act_core, slope_own, own_term = feed(low1, f32)
        chip = tie(chip, own_term, turned)
        h_chip, act_chip, act_cross, slope_chip, far_term = call(
            feed_turned, "feed_turned", [chip, *turned],
            [Stay(wide, bf16), Stay((units, rows), bf16), ((units, rows), bf16), Stay((2 * units, rows), bf16),
             wide_low], vmem=5.5,
        )
        far = swap(far_term, "head", 2)
        away = [swap(item, "head", 1) for item in tie((h_own, act_core, h_chip, act_cross), far_term)]
        ends = [normed1, ln1_gain, ln1_bias, own_term, far, b_down, ln2_gain, ln2_bias]
        kept.append(
            (x_kept, (kv_kept, q_kept), ((out_near, raised_near), (out_far, raised_far)), (ob_near, ob_far),
             normed1_kept, w_kept, (slope_own, slope_chip))
        )
        if layer + 1 < depth:
            entry, low, normed2_kept = call(
                functools.partial(close_kernel, layer), "close", ends,
                [wide_full, wide_low, Stay((rows, model + CLUSTER), f32)], vmem=4,
            )
            kept[-1] += (normed2_kept,)
            low, away = tie((low, away))
            chip, core = swap(low, "head", 2), swap(low, "head", 1)
        else:
            result, low, sums2, d_second = call(
                functools.partial(turn_kernel, layer), "turn", ends + [out_cotangent],
                [wide_full, wide_low, ((8, model), f32), Stay(*wide_full)], vmem=4,
            )
            low, away = tie((low, away))
        h_core, act_core, h_cross, act_cross = away
        kept[-1] += ((h_own, h_core, h_chip, h_cross), (act_own, act_core, act_chip, act_cross))

    feed_sums = attend_sums = None
    grads, small = [None] * depth, [None] * depth
    pieces = heads
    for layer in reversed(range(depth)):
        x_kept, (kv_kept, q_kept), (near, far_rows), obs, normed1, w_kept, slopes, *_, h_kept, acts = kept[layer]
        above = feed_sums is not None

        def feed_back(grad, up, up2, down, down2, slope, pre, pre2, out):
            feed_back_kernel(layer, grad, (up, up2), (down, down2), slope, (pre, pre2), out)

        def feed_back_turned(grad, up, up2, down, down2, slope, pre, pre2, out):
            feed_back_turned_kernel(layer, grad, (up, up2), (down, down2), slope, (pre, pre2), out)

        chip, g_core = swap(low, "head", 2), swap(low, "head", 1)
        pre_own, pre_core, own_term = call(
            feed_back, "feed_back", [low, *ups, *downs, View(slopes[0])],
            [((rows, units), bf16)] * 2 + [wide_full], vmem=4,
        )
        chip, g_core = join((chip, g_core), [feed_sums, attend_sums] if above else [], own_term)
        g_cross = swap(chip, "head", 1)
        pre_chip, pre_cross, far_term = call(
            feed_back_turned, "feed_back_turned", [chip, *ups, *downs, View(slopes[1])],
            [((units, rows), bf16)] * 2 + [wide_low], vmem=5,
        )
        far_term, g_cross = tie((far_term, g_cross))
        far = swap(far_term, "head", 2)
        pre_core, pre_cross = [swap(item, "head", 1) for item in tie((pre_core, pre_cross), far_term)]
        g_blocks = (low, g_core, chip, g_cross)
        added = ()
        if above and attend_sums.more():
            added = advance([attend_sums], far_term)
        *parts, up_sums = call(
            functools.partial(feed_grad_kernel, orders), "feed_grad",
            [spot, *tie((pre_own, pre_core, pre_chip, pre_cross), added), *map(View, h_kept), *g_blocks,
             *map(View, acts)],
            grad_outs(model, units, order_one) + grad_outs(model, units, order_two) + [((8, units), f32)],
            vmem=9,
        )
        far = tie(far, parts)
        if above:
            parts = join(parts, [attend_sums])
        waiting = attend_sums
        feed_sums = start_halving(parts, place, orders)
        low, *d_obs, sums1, d_first = call(
            functools.partial(mix_back_kernel, layer), "mix_back",
            [View(d_second), View(normed1), View(w_kept, 4), own_term, far, ln1_gain],
            [wide_low] + [((rows, cols), bf16)] * 4 + [((8, model), f32), Stay(*wide_full)], vmem=4,
        )
        got = [d_obs[0]] + [swap(d_obs[item], "head", item) for item in (1, 2, 3)]

        def kept_part(part, start):
            out, raised = part
            raised = View(raised.reshape(heads * pair, pack), pieces)
            return [
                View(kv_kept, heads), View(out, heads), raised,
                View(q_kept[start // pair], heads),
            ]

        near_q, near_k, near_v = call(
            attend_back_near_kernel, "attend_back_near",
            kept_part(near, 0) + got[:2],
            [((pair, cols), bf16)] + [((cols, pack), f32)] * 2, vmem=4.5,
        )
        got = tie(got, near_q)
        others = [item for item in (feed_sums, waiting) if item]
        got = join(got, others)
        if any(item.more() for item in others):
            got = tie(got, advance(others))
        low = tie(low, got)
        chip, core = swap(low, "head", 2), swap(low, "head", 1)
        d_q, d_k, d_v, own_term, core_term, chip_term, cross_term, sums_qv = call(
            functools.partial(attend_back_kernel, layer), "attend_back",
            kept_part(far_rows, pair)
            + [got[2], got[3], near_q, near_k, near_v, w_query, w_key, w_value],
            [((pack, cols), bf16)] * 3 + [wide_full, wide_low, wide_full, wide_low]
            + [((8, 2 * cols), f32)], vmem=7.5,
        )
        others = [item for item in (feed_sums, waiting) if item]
        chip, core, core_term, cross_term = join((chip, core, core_term, cross_term), others)
        got_chip, got_core = swap(cross_term, "head", 1), swap(core_term, "head", 1)
        cross = swap(chip, "head", 1)
        small[layer] = [sums1, sums2, up_sums, sums_qv]
        last = ()
        if not layer:
            mine = call(
                collect_kernel, "collect", [spot] + [item for part in small for item in part],
                [((12 * depth, model), f32)], vmem=3,
            )[0]
            last = (mine, swap(mine, "head", 1))
        got_chip, got_core, last = tie((got_chip, got_core, last))
        merged = (chip_term + got_chip.astype(f32)).astype(bf16)
        if not layer:
            total = last[0] + last[1]
            last = (total, swap(total, "head", 2))
        a_blocks = (low, core, chip, cross)
        added = ()
        if any(item.more() for item in others):
            added = advance(others, merged, apart=bool(layer))
        ready = merged
        if not layer:
            ready, last = tie((merged, last))
        far = swap(ready, "head", 2)
        *parts, = call(
            functools.partial(attend_grad_kernel, orders), "attend_grad",
            [spot, View(x_kept), *tie((d_q, d_k, d_v), merged, added), *a_blocks, *map(View, obs)],
            grad_outs(model, 2 * cols, order_one) + grad_outs(model, 2 * cols, order_two), vmem=6,
        )
        if layer:
            far = land(far, [feed_sums.slots[0][0]], parts)
        if not layer and len(parts) == 4:
            longer = ((parts[0].shape[0] + 24 * depth, parts[0].shape[1]), bf16)
            parts[:2] = call(append_kernel, "append", [*parts[:2], *last], [longer] * 2, vmem=4)
        attend_sums = start_halving(parts, place, orders, last)
        grads[layer] = (feed_sums, attend_sums)
        if layer:
            low, sums2, d_second = call(
                functools.partial(open_back_kernel, layer - 1), "open_back",
                [View(kept[layer - 1][-3]), View(d_first), own_term, got_core, far, ln2_gain],
                [wide_low, ((8, model), f32), Stay(*wide_full)], vmem=4,
            )

    while feed_sums.more():
        advance([feed_sums])
    found = transfers_of([feed_sums])
    done = call(
        functools.partial(finish_kernel, spots_of([feed_sums]), len(found)), "finish",
        [*feed_sums.keeps, *(item.got for item in found)], [(keep.shape, f32) for keep in feed_sums.keeps], vmem=4,
    )
    done = join(done, [attend_sums])
    if attend_sums.more():
        advance([attend_sums], done)
    d_rows = call(close_back_kernel, "close_back", [View(d_first), own_term, got_core, far], [wide_full], vmem=4)[0]
    while attend_sums.more():
        advance([attend_sums], d_rows)
    items = [item for layer in grads for item in layer][1:]
    while any(item.more() for item in items):
        advance(items)
    ends = [keep for item in items for keep in item.keeps] + [item.got for item in transfers_of(items)] + list(done)
    own = done[0].shape[0]
    g_q, g_k, g_v, g_o, g_up, g_down, s_bq, s_bv, s_bo, s_g1, s_n1, s_bd, s_g2, s_n2, s_bu = call(
        functools.partial(assemble_kernel, spots_of(items), len(transfers_of(items)), depth), "assemble", ends,
        [((depth, own, cols), f32)] * 3 + [((depth, cols, own), f32)] + [((depth, own, units), f32)] * 2
        + [((depth, model), f32)] * 8 + [((depth, groups * units), f32)], vmem=8,
    )
    return (
        result, d_rows, g_q, g_k, g_v, s_bq, s_bv, g_o, s_bo, s_g1, s_n1, g_up,
        s_bu, g_down.transpose(0, 2, 1), s_bd, s_g2, s_n2,
    )


def solution(mesh):
    split = P(("dp", "head"), None)
    column, line = P(None, None, "head"), P(None, "head", None)
    placed = (
        split, column, column, column, P(None, "head"), P(None, "head"), line, P(), P(), P(),
        column, P(None, "head"), line, P(), P(), P(),
        P("dp"), P(None, "head", "dp"), P(None, "head", "dp"), split,
    )
    by_rows, by_cols = P(None, "dp", "head"), P(None, "head", "dp")
    results = (
        split, split, by_rows, by_rows, by_rows, P(), P(), by_cols, P(), P(), P(), by_rows, P(),
        by_cols, P(), P(), P(),
    )
    return jax.shard_map(body, mesh=mesh, in_specs=placed, out_specs=results, check_vma=False)
```

```python
import functools
import math

import jax
import jax.numpy as jnp
from jax import lax
from jax.experimental import pallas as pl
from jax.experimental.pallas import tpu as pltpu
from jax.sharding import PartitionSpec as P

CLUSTER = 128
HEAD_DIM = 64
EPS = 1e-12
NEG = -1e30
MIB = 1024 * 1024
GIGA = {"attend_back_near": 3, "finish": 3}

f32 = jnp.float32
bf16 = jnp.bfloat16


def swap(array, axis, bit):
    size = lax.axis_size(axis)
    return lax.ppermute(array, axis, [(item, item ^ bit) for item in range(size)])


def tie(value, *earlier):
    return lax.optimization_barrier((value, earlier))[0]


class Transfer:
    def __init__(self, send, bit):
        self.got = swap(send, "dp", 1 << bit)


class Halving:
    def __init__(self, keeps, sends, orders, extras):
        self.keeps, self.orders, self.extras = list(keeps), [list(order) for order in orders], extras
        self.slots = [(Transfer(send, order.pop(0)), 0) for send, order in zip(sends, self.orders)]

    def more(self):
        return bool(self.orders[0])


def transfers_of(items):
    found = []
    for item in items:
        for transfer, _ in item.slots:
            if transfer not in found:
                found.append(transfer)
    return found


def spots_of(items):
    found = transfers_of(items)
    return [
        (found.index(transfer), start, keep.shape[0], extra)
        for item in items
        for keep, (transfer, start), extra in zip(item.keeps, item.slots, item.extras)
    ]


def join(value, items, *earlier):
    return land(value, transfers_of(items), *earlier)


def land(value, found, *earlier):
    value, gots, _ = lax.optimization_barrier((value, [item.got for item in found], earlier))
    for item, got in zip(found, gots):
        item.got = got
    return value


def advance(items, *earlier, apart=False):
    items = [item for item in items if item.more()]
    found = transfers_of(items)
    keeps = [keep for item in items for keep in item.keeps]
    keeps, gots = tie((keeps, [item.got for item in found]), *earlier)
    extras = [extra for item in items for extra in item.extras]
    outs = [(((keep.shape[0] - extra) // 2 + extra, keep.shape[1]), bf16) for keep, extra in zip(keeps, extras)]
    groups = {}
    bits = [order.pop(0) for item in items for order in item.orders]
    for spot, (bit, out) in enumerate(zip(bits, outs)):
        groups.setdefault((bit, out[0][1], spot if apart else 0), []).append(spot)
    sends = []
    for (_, cols, _), group in groups.items():
        sends.append(((sum(outs[spot][0][0] for spot in group), cols), bf16))
    parts = call(
        functools.partial(halve_kernel, spots_of(items), list(groups.values()), len(gots)), "halve",
        [*keeps, *gots], outs + sends, vmem=8,
    )
    slots = [None] * len(keeps)
    for (bit, *_), group, send in zip(groups, groups.values(), parts[len(keeps) :]):
        transfer, start = Transfer(send, bit), 0
        for spot in group:
            slots[spot] = (transfer, start)
            start += outs[spot][0][0]
    start = 0
    for item in items:
        stop = start + len(item.keeps)
        item.keeps, item.slots = parts[start:stop], slots[start:stop]
        start = stop
    return parts


def dot(left, right):
    return jnp.dot(left, right, preferred_element_type=f32)


def dot_nt(left, right):
    return lax.dot_general(left, right, (((1,), (1,)), ((), ())), preferred_element_type=f32)


def dot_tn(left, right):
    return lax.dot_general(left, right, (((0,), (0,)), ((), ())), preferred_element_type=f32)


def row(ref, layer):
    return ref[layer : layer + 1, :]


def normalise(rows):
    centre = rows - jnp.mean(rows, axis=-1, keepdims=True)
    spread = jnp.mean(centre * centre, axis=-1, keepdims=True)
    scale = lax.rsqrt(spread + EPS)
    return centre * scale, scale


def normalise_back(grad, gain, normed, scale):
    part = grad * gain
    mean_one = jnp.mean(part, axis=-1, keepdims=True)
    mean_two = jnp.mean(part * normed, axis=-1, keepdims=True)
    return (part - mean_one - normed * mean_two) * scale


def store_sums(ref, *arrays):
    rows = [jnp.sum(item, axis=0, keepdims=True) for item in arrays]
    rows.append(jnp.zeros((ref.shape[0] - len(rows), ref.shape[1]), f32))
    ref[...] = jnp.concatenate(rows, axis=0)


def gelu_pair(values):
    bell = jnp.exp(values * values * -0.5)
    t = 1.0 / (1.0 + (0.3275911 * math.sqrt(0.5)) * jnp.abs(values))
    poly = 0.5 * 1.061405429
    for factor in (-1.453152027, 1.421413741, -0.284496736, 0.254829592):
        poly = poly * t + 0.5 * factor
    tail = poly * t * bell
    cdf = jnp.where(values >= 0.0, 1.0 - tail, tail)
    return values * cdf, cdf + values * bell * (1.0 / math.sqrt(2.0 * math.pi))


def stack_rows(refs):
    return jnp.concatenate([ref[...] for ref in refs], axis=0)


def head_cols(array, head):
    return array[:, head * HEAD_DIM : (head + 1) * HEAD_DIM]


def lanes_of(rows):
    return lax.broadcasted_iota(jnp.int32, (rows, 2 * HEAD_DIM), 1)


class Viewed:
    def __init__(self, source, pieces):
        self.source, self.shape, self.size = source, source.shape, source.shape[0] // pieces

    def piece(self, item):
        return self.source[item * self.size : (item + 1) * self.size]

    def __getitem__(self, index):
        return self.source[index]


def cluster_kernel(layer, spot, q_order, k_order, live, wq, wk, wv, q_marks, k_marks, weights, held, sems):
    heads, length, width = q_marks.shape
    copies = [
        pltpu.make_async_copy(source.at[layer], held.at[item], sems.at[item])
        for item, source in enumerate((wq, wk, wv))
    ]
    for copy in copies:
        copy.start()
    count = length // CLUSTER
    lines = lax.broadcasted_iota(jnp.int32, (length, length), 0)
    spread_line = lax.broadcasted_iota(jnp.int32, (length, width), 0) // CLUSTER + HEAD_DIM
    lanes = lanes_of(length)
    spread = jnp.where(spread_line == lanes, 1.0, 0.0).astype(bf16)
    in_use = jnp.logical_and(lanes >= HEAD_DIM, lanes < HEAD_DIM + count)
    for head in range(heads):
        order = q_order[head, layer : layer + 1, :] ^ spot[0]
        hot = jnp.where(order == lines, 1.0, 0.0).astype(bf16)
        q_marks[head] = dot(hot, spread).astype(bf16)
        order = k_order[head, layer : layer + 1, :] ^ spot[0]
        hot = jnp.where(order == lines, 1.0, 0.0).astype(bf16)
        inside = dot(hot, spread) * live[...]
        outside = jnp.where(in_use, jnp.where(inside > 0.5, 0.0, NEG), 0.0)
        k_marks[head] = outside.astype(bf16)
    for copy in copies:
        copy.wait()
    blank = jnp.zeros((HEAD_DIM, held.shape[2]), bf16)
    for head in range(heads):
        part = slice(head * HEAD_DIM, (head + 1) * HEAD_DIM)
        weights[head] = jnp.concatenate([held[0, part], blank, held[1, part], held[2, part]], axis=0)


def attend_rows(first, rows, q_ref, kv_ref, k_marks, raised_kept, out_kept):
    heads, length, width = kv_ref.shape
    chunk = rows
    left = lanes_of(length) < HEAD_DIM
    mixed = []
    for head in range(heads):
        keys = kv_ref[head].astype(f32)
        marked = jnp.where(left, keys, k_marks[head].astype(f32)).astype(bf16)
        values = jnp.where(left, 1.0, keys).astype(bf16)
        outs = []
        for start in range(0, rows, chunk):
            scores = dot_nt(q_ref[head, first + start : first + start + chunk], marked)
            raised = jnp.exp(scores - jnp.max(scores, axis=1, keepdims=True)).astype(bf16)
            raised_kept[head, pl.ds(start, chunk)] = raised
            total = dot(raised, values)
            share = 1.0 / total
            outs.append(jnp.where(left[:chunk], share, total * pltpu.roll(share, HEAD_DIM, 1)))
        outs = jnp.concatenate(outs, axis=0)
        out_kept[head] = outs
        mixed.append(outs[:, HEAD_DIM:])
    return jnp.concatenate(mixed, axis=1).astype(bf16)


def project(layer, x, weights, bq, bv, marks):
    blank = jnp.zeros((1, HEAD_DIM), f32)
    bias_q, bias_v = row(bq, layer), row(bv, layer)
    queries, pairs = [], []
    for head in range(weights.shape[0]):
        part = slice(head * HEAD_DIM, (head + 1) * HEAD_DIM)
        bias = jnp.concatenate([bias_q[:, part], blank, blank, bias_v[:, part]], axis=1)
        qkv = (dot_nt(x, weights[head]) + bias).astype(bf16)
        query = qkv[:, : 2 * HEAD_DIM].astype(f32) * (1.0 / math.sqrt(HEAD_DIM))
        queries.append((query + marks[head].astype(f32)).astype(bf16))
        pairs.append(qkv[:, 2 * HEAD_DIM :])
    return queries, pairs


def project_kernel(layer, x0, x1, weights, bq, bv, q_marks, q_out, kv_out):
    rows = q_out.shape[1]
    marks = [q_marks[head][:rows] for head in range(q_marks.shape[0])]
    queries, pairs = project(layer, stack_rows((x0, x1)), weights, bq, bv, marks)
    for head in range(len(queries)):
        q_out[head] = queries[head]
        kv_out[head] = pairs[head]


def attend_kernel(
    layer, x0, x1, x2, x3, weights, bq, bv, q_marks, k_marks, kv_near,
    q_far, kv_out, ob2, ob3, raised_kept, out_kept, ob_kept, x_kept,
):
    size = ob2.shape[0]
    rows = 2 * size
    for item, ref in enumerate((x0, x1, x2, x3)):
        x_kept[pl.ds(item * size, size)] = ref[...]
    marks = [q_marks[head][rows:] for head in range(q_marks.shape[0])]
    queries, pairs = project(layer, stack_rows((x2, x3)), weights, bq, bv, marks)
    for head in range(len(queries)):
        q_far[head] = queries[head]
        kv_out[head, :rows] = kv_near[head]
        kv_out[head, rows:] = pairs[head]
    mixed = attend_rows(0, rows, q_far, kv_out, k_marks, raised_kept, out_kept)
    ob_kept[...] = mixed
    ob2[...] = mixed[:size]
    ob3[...] = mixed[size:]


def attend_near_kernel(
    q_in, kv_in, k_marks, ob0, ob1, raised_kept, out_kept, ob_kept, kv_kept
):
    size = ob0.shape[0]
    kv_kept[...] = kv_in[...]
    mixed = attend_rows(0, 2 * size, q_in, kv_in, k_marks, raised_kept, out_kept)
    ob_kept[...] = mixed
    ob0[...] = mixed[:size]
    ob1[...] = mixed[size:]


def entry_rows(layer, x, gain, shift):
    rows = x[...].astype(f32)
    if layer:
        rows = rows * row(gain, layer - 1) + row(shift, layer - 1)
    return rows


def with_scale(unit, scale):
    return jnp.concatenate([unit, jnp.broadcast_to(scale, (unit.shape[0], CLUSTER))], axis=1)


def mix_kernel(
    layer, ob0, ob1, ob2, ob3, w0, w1, w2, w3, x, b_out, gain1, shift1, gain2, shift2,
    normed, low, normed_kept, w_kept,
):
    total = entry_rows(layer, x, gain2, shift2) + row(b_out, layer)
    for item, (left, right) in enumerate(((ob0, w0), (ob1, w1), (ob2, w2), (ob3, w3))):
        w_kept[item] = right[...]
        total = total + dot(left[...], right[...])
    unit, root = normalise(total)
    normed[...] = unit
    normed_kept[...] = with_scale(unit, root)
    low[...] = (unit * row(gain1, layer) + row(shift1, layer)).astype(bf16)


def store_rows(value, refs):
    start = 0
    for ref in refs:
        ref[...] = value[start : start + ref.shape[0]].astype(ref.dtype)
        start += ref.shape[0]


def feed_kernel(layer, x, ups, biases, downs, x_kept, acts, slope, out):
    rows = x[...]
    x_kept[...] = rows
    total = 0.0
    units = acts[0].shape[1]
    for item in range(2):
        act, der = gelu_pair(dot(rows, ups[item][layer]) + row(biases[item], layer))
        act = act.astype(bf16)
        acts[item][...] = act
        slope[:, item * units : (item + 1) * units] = der.astype(bf16)
        total = total + dot(act, downs[item][layer])
    out[...] = total.astype(out.dtype)


def turn_weights_kernel(layer, ups, biases, downs, ups_t, biases_t, downs_t):
    for item in range(2):
        ups_t[item][...] = ups[item][layer].T
        downs_t[item][...] = downs[item][layer].T
        bias = row(biases[item], layer)
        biases_t[item][...] = jnp.broadcast_to(bias, (CLUSTER, bias.shape[1])).T


def feed_turned_kernel(x, ups_t, biases_t, downs_t, x_kept, acts, slope, out):
    rows = x[...]
    x_kept[...] = rows
    total = 0.0
    units, count = acts[0].shape
    for item in range(2):
        bias = jnp.concatenate([biases_t[item][...]] * (count // CLUSTER), axis=1)
        act, der = gelu_pair(dot_nt(ups_t[item][...], rows) + bias)
        act = act.astype(bf16)
        acts[item][...] = act
        slope[item * units : (item + 1) * units, :] = der.astype(bf16)
        total = total + dot(downs_t[item][...], act)
    out[...] = total.T.astype(out.dtype)


def second_rows(layer, normed1, gain1, shift1, own, far, b_down):
    rows = normed1[...] * row(gain1, layer) + row(shift1, layer)
    return rows + own[...] + far[...].astype(f32) + row(b_down, layer)


def close_kernel(
    layer, normed1, gain1, shift1, own, far, b_down, gain2, shift2, normed, low, normed_kept
):
    unit, root = normalise(
        second_rows(layer, normed1, gain1, shift1, own, far, b_down)
    )
    normed[...] = unit
    normed_kept[...] = with_scale(unit, root)
    low[...] = (unit * row(gain2, layer) + row(shift2, layer)).astype(bf16)


def turn_kernel(
    layer, normed1, gain1, shift1, own, far, b_down, gain2, shift2, grad,
    result, low, sums, d_second,
):
    unit, root = normalise(
        second_rows(layer, normed1, gain1, shift1, own, far, b_down)
    )
    gain = row(gain2, layer)
    result[...] = unit * gain + row(shift2, layer)
    back = normalise_back(grad[...], gain, unit, root)
    d_second[...] = back
    low[...] = back.astype(bf16)
    store_sums(sums, back, grad[...] * unit, grad[...])


def unit_and_scale(kept, width):
    both = kept[...]
    return both[:, :width], both[:, width : width + 1]


def open_back_kernel(layer, normed2, base, own, core, far, gain2, low, sums, d_second):
    rest = own[...] + core[...].astype(f32) + far[...].astype(f32)
    grad = base[...] + rest
    unit, root = unit_and_scale(normed2, grad.shape[1])
    back = normalise_back(grad, row(gain2, layer), unit, root)
    d_second[...] = back
    low[...] = back.astype(bf16)
    store_sums(sums, back, grad * unit, grad)


def feed_back_kernel(layer, grad, ups, downs, slope, pres, out):
    rows = grad[...]
    total = 0.0
    units = pres[0].shape[1]
    for item in range(2):
        der = slope[:, item * units : (item + 1) * units].astype(f32)
        pre = (dot_nt(rows, downs[item][layer]) * der).astype(bf16)
        pres[item][...] = pre
        total = total + dot_nt(pre, ups[item][layer])
    out[...] = total.astype(out.dtype)


def feed_back_turned_kernel(layer, grad, ups, downs, slope, pres, out):
    rows = grad[...]
    total = 0.0
    units = pres[0].shape[0]
    for item in range(2):
        der = slope[item * units : (item + 1) * units, :].astype(f32)
        pre = (dot_nt(downs[item][layer], rows) * der).astype(bf16)
        pres[item][...] = pre
        total = total + dot(ups[item][layer], pre)
    out[...] = total.T.astype(out.dtype)


def mix_back_kernel(
    layer, base, normed1, weights, own, far, gain1, low, d0, d1, d2, d3, sums, d_first
):
    grad = base[...] + own[...] + far[...].astype(f32)
    unit, root = unit_and_scale(normed1, grad.shape[1])
    back = normalise_back(grad, row(gain1, layer), unit, root)
    d_first[...] = back
    small = back.astype(bf16)
    low[...] = small
    for item, out in enumerate((d0, d1, d2, d3)):
        out[...] = dot_nt(small, weights.piece(item)[0]).astype(bf16)
    store_sums(sums, back, grad * unit, grad)


def close_back_kernel(base, own, core, far, out):
    out[...] = base[...] + own[...] + core[...].astype(f32) + far[...].astype(f32)


def attend_back_rows(refs, q_kept, kv_kept, out_kept, raised_kept):
    d_mixed = stack_rows(refs)
    rows = d_mixed.shape[0]
    heads, length, width = kv_kept.shape
    chunk = rows
    steps = rows // chunk
    key_lanes, lanes = lanes_of(length), lanes_of(rows)[:, :HEAD_DIM]
    d_q, d_k, d_v = [], [], []
    for head in range(heads):
        part = slice(head * HEAD_DIM, (head + 1) * HEAD_DIM)
        keys = kv_kept.piece(head)[0]
        both = out_kept.piece(head)[0]
        share, out = both[:, :HEAD_DIM], both[:, HEAD_DIM:]
        grad = (d_mixed[:, part].astype(f32) * share).astype(bf16).astype(f32)
        inner = jnp.sum(grad * out, axis=1, keepdims=True)
        high = inner.astype(bf16).astype(f32)
        middle = (inner - high).astype(bf16).astype(f32)
        low = inner - high - middle
        terms = jnp.where(
            lanes == 0, -high, jnp.where(lanes == 1, -middle, jnp.where(lanes == 2, -low, 0.0))
        )
        grad = jnp.concatenate([terms, grad], axis=1).astype(bf16)
        values = jnp.where(
            key_lanes < 3, 1.0, jnp.where(key_lanes < HEAD_DIM, 0.0, keys.astype(f32))
        ).astype(bf16)
        d_score, raised = [], []
        for item in range(steps):
            d_prob = dot_nt(grad[item * chunk : (item + 1) * chunk], values)
            raised.append(raised_kept.piece(head * steps + item))
            d_score.append((raised[-1].astype(f32) * d_prob).astype(bf16))
        d_score = jnp.concatenate(d_score, axis=0)
        raised = jnp.concatenate(raised, axis=0)
        query = q_kept.piece(head)[0]
        d_q.append(dot(d_score, keys)[:, :HEAD_DIM] * (1.0 / math.sqrt(HEAD_DIM)))
        d_k.append(dot(query.T[:HEAD_DIM], d_score))
        d_v.append(dot(grad.T[HEAD_DIM:], raised))
    return (
        jnp.concatenate(d_q, axis=1).astype(bf16),
        jnp.concatenate(d_k, axis=0),
        jnp.concatenate(d_v, axis=0),
    )


def attend_back_near_kernel(kv_kept, out_kept, raised_kept, q_kept, d0, d1, d_query, d_k, d_v):
    d_query[...], d_k[...], d_v[...] = attend_back_rows((d0, d1), q_kept, kv_kept, out_kept, raised_kept)


def attend_back_kernel(
    layer, kv_kept, out_kept, raised_kept, q_kept, d2, d3, near_q, near_k, near_v, wq, wk, wv,
    d_query, d_key, d_value, own, core, chip, cross, sums,
):
    d_q, d_k, d_v = attend_back_rows((d2, d3), q_kept, kv_kept, out_kept, raised_kept)
    d_q = jnp.concatenate([near_q[...], d_q], axis=0)
    d_k, d_v = ((item + near[...]).T.astype(bf16) for item, near in ((d_k, near_k), (d_v, near_v)))
    d_query[...] = d_q
    d_key[...] = d_k
    d_value[...] = d_v
    store_sums(sums, jnp.concatenate([d_q.astype(f32), d_v.astype(f32)], axis=1))
    store_rows(dot(d_q, wq[layer]) + dot(d_k, wk[layer]) + dot(d_v, wv[layer]), (own, core, chip, cross))


def store_pieces(place, grad, outs, order):
    if len(outs) == 1:
        outs[0][...] = grad.astype(bf16)
        return
    keep, send = outs
    bits = len(order)
    pieces = 1 << bits
    size = grad.shape[0] // pieces
    for piece in range(pieces):
        rel = place ^ piece
        index = 0
        for step, bit in enumerate(order[1:]):
            index = index + (((rel >> bit) & 1) << (bits - 2 - step))
        value = grad[piece * size : (piece + 1) * size].astype(bf16)
        leaves = (rel >> order[0]) & 1

        @pl.when(leaves == 0)
        def _(value=value, index=index, keep=keep):
            keep[pl.ds(pl.multiple_of(index * size, size), size)] = value

        @pl.when(leaves == 1)
        def _(value=value, index=index, send=send):
            send[pl.ds(pl.multiple_of(index * size, size), size)] = value


def split_refs(refs, *counts):
    parts = []
    for count in counts:
        parts.append(refs[:count])
        refs = refs[count:]
    return parts


def dot_tt(left, right):
    return lax.dot_general(left, right, (((0,), (1,)), ((), ())), preferred_element_type=f32)


def stack_cols(refs):
    return jnp.concatenate([ref[...] for ref in refs], axis=1)


def feed_grad_kernel(orders, spot, *refs):
    size = (len(refs) - 17) // 2
    pre, x, grad, act, one, two, (sums,) = split_refs(refs, 4, 4, 4, 4, size, size, 1)
    pre_near, pre_far = stack_rows(pre[:2]), stack_cols(pre[2:])
    up = dot_tn(stack_rows(x[:2]), pre_near) + dot_tt(stack_rows(x[2:]), pre_far)
    store_pieces(spot[1], up, one, orders[0])
    down = dot_tn(stack_rows(grad[:2]), stack_rows(act[:2])) + dot_tt(stack_rows(grad[2:]), stack_cols(act[2:]))
    store_pieces(spot[1], down, two, orders[1])
    ones = jnp.ones((sums.shape[0], pre_near.shape[0]), bf16)
    sums[...] = dot(ones, pre_near) + dot_nt(ones, pre_far)


def fold_small(rows):
    half = rows.shape[1] // 2
    return jnp.concatenate([rows[:, :half], rows[:, half:]], axis=0).astype(bf16)


def append_kernel(keep, send, small, got, keep_out, send_out):
    below = fold_small(small[...] + got[...])
    keep_out[...] = jnp.concatenate([keep[...], below], axis=0)
    send_out[...] = jnp.concatenate([send[...], below], axis=0)


def finish_kernel(spots, count, *refs):
    keeps, gots, outs = split_refs(refs, len(spots), count, 2)
    for spot, item in enumerate(whole_grads(spots, keeps, gots)):
        outs[spot % 2][spot // 2] = item


def attend_grad_kernel(orders, spot, *refs):
    size = (len(refs) - 10) // 2
    x, (dq, dk, dv), grad, mixed, one, two = split_refs(refs, 1, 3, 4, 2, size, size)
    x = x[0][...]
    right = jnp.concatenate([dq[...], dk[...]], axis=1)
    store_pieces(spot[1], dot_tn(x, right), one, orders[0])
    out = dot_tn(stack_rows(grad), stack_rows(mixed))
    store_pieces(spot[1], jnp.concatenate([dot_tn(x, dv[...]), out], axis=1), two, orders[1])


def whole_grads(spots, keeps, gots):
    return [
        keep[...].astype(f32) + gots[spot][start : start + rows].astype(f32)
        for keep, (spot, start, rows, _) in zip(keeps, spots)
    ]


def halve_kernel(spots, groups, count, *refs):
    keeps, gots, rest = split_refs(refs, len(spots), count, len(refs) - len(spots) - count)
    leaving = []
    for item, ref, (*_, rows, extra) in zip(whole_grads(spots, keeps, gots), rest, spots):
        item = item.astype(bf16)
        half, body = (rows - extra) // 2, rows - extra
        stays, leaves = item[:half], item[half:body]
        if extra:
            stays, leaves = (jnp.concatenate([part, item[body:]], axis=0) for part in (stays, leaves))
        ref[...] = stays
        leaving.append(leaves)
    for group, ref in zip(groups, rest[len(spots) :]):
        ref[...] = jnp.concatenate([leaving[spot] for spot in group], axis=0)


def place_rows(head, piece, groups=4):
    return jnp.concatenate([jnp.where(head == item, piece, 0.0) for item in range(groups)], axis=1)


def collect_kernel(spot, *refs):
    rows = []
    for layer in range(len(refs) // 4):
        mix, feed, up, qv = refs[4 * layer : 4 * layer + 4]
        cols = qv.shape[1] // 2
        rows += [place_rows(spot[2], qv[:1, :cols]), place_rows(spot[2], qv[:1, cols:])]
        rows += [mix[:3, :], feed[:3, :]]
        rows += [jnp.where(spot[2] == item, up[:1, :], 0.0) for item in range(4)]
    refs[-1][...] = jnp.concatenate(rows, axis=0)


def assemble_kernel(spots, count, depth, *refs):
    keeps, gots, refs = split_refs(refs, len(spots), count, len(refs) - len(spots) - count)
    grads = whole_grads(spots, keeps, gots)
    g_q, g_k, g_v, g_o, *vectors, s_bu = refs
    own, cols = g_q.shape[1:]
    below = grads[0][own:]
    half = below.shape[0] // 2
    small = jnp.concatenate([below[:half], below[half:]], axis=1)
    model = small.shape[1]
    for layer in range(depth):
        one, two = grads[2 * layer : 2 * layer + 2]
        g_q[layer] = one[:own, :cols]
        g_k[layer] = one[:own, cols:]
        g_v[layer] = two[:, :cols]
        g_o[layer] = two[:, cols:].T
        rows = small[12 * layer : 12 * layer + 12]
        for item, ref in enumerate(vectors):
            ref[layer : layer + 1, :] = rows[item : item + 1, :]
        for item in range(4):
            s_bu[layer : layer + 1, item * model : (item + 1) * model] = rows[8 + item : 9 + item, :]


class Scalar:
    def __init__(self, array):
        self.array = array


class Far:
    def __init__(self, array):
        self.array = array


class Stay:
    def __init__(self, shape, kind):
        self.shape, self.kind = shape, kind


class View:
    def __init__(self, array, pieces=1):
        self.array, self.pieces = array, pieces


def call(kernel, name, ins, outs, vmem, scratch=()):
    arrays, specs, pieces = [], [], {}
    for spot, item in enumerate(ins):
        space = pltpu.VMEM
        if isinstance(item, Scalar):
            space = pltpu.SMEM
            arrays.append(item.array)
        elif isinstance(item, Far):
            space = pltpu.HBM
            arrays.append(pltpu.with_memory_space_constraint(item.array, pltpu.HBM))
        elif isinstance(item, View):
            arrays.append(pltpu.with_memory_space_constraint(item.array, pltpu.VMEM))
            pieces[spot] = item.pieces
        else:
            arrays.append(item)
        specs.append(pl.BlockSpec(memory_space=space))
    shapes = []
    for item in outs:
        if isinstance(item, Stay):
            shapes.append(pltpu.VMEM(item.shape, item.kind))
        else:
            shapes.append(jax.ShapeDtypeStruct(*item))

    def wrapped(*refs):
        kernel(*(Viewed(ref, pieces[spot]) if spot in pieces else ref for spot, ref in enumerate(refs)))

    return pl.pallas_call(
        wrapped,
        name=name,
        grid=(1,),
        out_shape=shapes,
        in_specs=specs,
        out_specs=[pl.BlockSpec(memory_space=pltpu.VMEM)] * len(shapes),
        scratch_shapes=scratch,
        compiler_params=pltpu.CompilerParams(vmem_limit_bytes=int(vmem * MIB)),
        cost_estimate=pl.CostEstimate(flops=int(GIGA.get(name, 0) * 1e9) + 1, bytes_accessed=1, transcendentals=0),
    )(*arrays)


def grad_outs(rows, cols, order, extra=0):
    pieces = 1 << len(order)
    if (rows // pieces) % 16:
        return [((rows, cols), bf16)]
    return [((rows // 2 + extra, cols), bf16)] * 2


def start_halving(parts, place, orders, small=()):
    half = len(parts) // 2
    extras = [2 * small[0].shape[0] if small else 0, 0]
    if half == 1:
        pairs = []
        for part, order, extra in zip(parts, orders, extras):
            pieces = 1 << len(order)
            whole = part.reshape(pieces, -1, part.shape[1])
            ranks = []
            for spot in range(pieces):
                ranks.append(
                    sum(((spot >> (len(order) - 1 - step)) & 1) << bit for step, bit in enumerate(order))
                )
            whole = jnp.take(whole, jnp.array(ranks, jnp.int32) ^ place, axis=0).reshape(part.shape)
            pair = (whole[: part.shape[0] // 2], whole[part.shape[0] // 2 :])
            if extra:
                below = fold_small(functools.reduce(jnp.add, small))
                pair = tuple(jnp.concatenate([item, below], axis=0) for item in pair)
            pairs.append(pair)
    else:
        pairs = (parts[:2], parts[2:])
    return Halving(*zip(*pairs), orders, extras)


def body(
    hidden_in, w_query, w_key, w_value, b_query, b_value, w_out, b_out, ln1_gain, ln1_bias,
    w_up, b_up, w_down, b_down, ln2_gain, ln2_bias, token_mask, query_order, key_order,
    out_cotangent,
):
    depth, model, cols = w_query.shape
    rows = hidden_in.shape[0]
    units = w_up.shape[2]
    pack = token_mask.shape[0]
    heads = query_order.shape[1]
    head = lax.axis_index("head").astype(jnp.int32)
    groups = lax.axis_size("head")
    place = lax.axis_index("dp").astype(jnp.int32)
    spot = Scalar(jnp.stack([head * rows, place, head]))
    bits = lax.axis_size("dp").bit_length() - 1
    order_one = tuple(range(bits))
    order_two = order_one[:2][::-1] + order_one[2:]
    orders = (order_one, order_two)
    w_query, w_key, w_value = (item.transpose(0, 2, 1) for item in (w_query, w_key, w_value))
    q_order, k_order = query_order.transpose(1, 0, 2), key_order.transpose(1, 0, 2)

    wide = (rows, model)
    dense = 2 * rows * model
    wide_low, wide_full = (wide, bf16), (wide, f32)

    low = hidden_in
    chip, core = swap(low, "head", 2), swap(low, "head", 1)
    around = token_mask.reshape(groups, rows)
    live = jnp.concatenate(
        [lax.dynamic_index_in_dim(around, head ^ item, 0, keepdims=False) for item in range(groups)]
    )
    live = live.astype(f32).reshape(pack, 1)

    entry = hidden_in
    kept = []
    pair = 2 * rows
    two = 2 * HEAD_DIM
    kept_rows = [Stay((heads, pair, pack), bf16), Stay((heads, pair, two), f32), Stay((pair, cols), bf16)]
    other_units = [swap(item, "head", 1) for item in (w_up, b_up, w_down)]
    for layer in range(depth):
        *marks, weights = call(
            functools.partial(cluster_kernel, layer), "clusters",
            [spot, q_order, k_order, live, Far(w_query), Far(w_key), Far(w_value)],
            [((heads, pack, two), bf16)] * 2 + [((heads, 2 * two, model), bf16)], vmem=7,
            scratch=[pltpu.VMEM((3, cols, model), bf16), pltpu.SemaphoreType.DMA((3,))],
        )
        if not layer:
            chip, other_units[1] = tie((chip, other_units[1]))
        q_near, kv_near = call(
            functools.partial(project_kernel, layer), "project", [low, core, weights, b_query, b_value, marks[0]],
            [Stay((heads, pair, two), bf16), ((heads, pair, two), bf16)], vmem=5,
        )
        chip = tie(chip, kv_near)
        cross = swap(chip, "head", 1)
        if not layer:
            cross, other_units[0], other_units[2] = tie((cross, other_units[0], other_units[2]))
            ups, biases, downs = zip((w_up, b_up, w_down), other_units)
        w_mine = tie(w_out[layer], chip)
        w_core, w_chip = swap(w_mine, "head", 1), swap(w_mine, "head", 2)
        q_far, kv_all, ob2, ob3, raised_far, out_far, ob_far, x_kept = call(
            functools.partial(attend_kernel, layer), "attend",
            [low, core, chip, cross, weights, b_query, b_value, *marks, kv_near],
            [Stay((heads, pair, two), bf16), ((heads, pack, two), bf16)] + [((rows, cols), bf16)] * 2 + kept_rows
            + [Stay((pack, model), bf16)], vmem=6,
        )
        got2, got3 = swap(ob2, "head", 2), swap(ob3, "head", 3)
        q_kept = (q_near, q_far)
        ob0, ob1, raised_near, out_near, ob_near, kv_kept = call(
            attend_near_kernel, "attend_near", [q_near, kv_all, marks[1]],
            [((rows, cols), bf16)] * 2 + kept_rows + [Stay((heads, pack, two), bf16)], vmem=4,
        )
        got1 = swap(ob1, "head", 1)
        got1, got2, got3, w_core, w_chip = tie((got1, got2, got3, w_core, w_chip))
        w_cross = swap(w_chip, "head", 1)
        outs = (w_mine, w_core, w_chip, w_cross)
        got = [ob0, got1, got2, got3]
        normed1, low1, normed1_kept, w_kept = call(
            functools.partial(mix_kernel, layer), "mix",
            [*got, *outs, entry, b_out, ln1_gain, ln1_bias, ln2_gain, ln2_bias],
            [wide_full, wide_low, Stay((rows, model + CLUSTER), f32), Stay((4, cols, model), bf16)], vmem=4,
        )

        def feed(block, kind):
            def kernel(x, up, up2, bias, bias2, down, down2, x_kept, act, act2, slope, out):
                feed_kernel(layer, x, (up, up2), (bias, bias2), (down, down2), x_kept, (act, act2), slope, out)

            return call(
                kernel, "feed", [block, *ups, *biases, *downs],
                [Stay(wide, bf16), Stay((rows, units), bf16), ((rows, units), bf16),
                 Stay((rows, 2 * units), bf16), (wide, kind)], vmem=5.5,
            )

        def turn_weights(up, up2, bias, bias2, down, down2, *outs):
            turn_weights_kernel(layer, (up, up2), (bias, bias2), (down, down2), outs[:2], outs[2:4], outs[4:6])
            for out in outs[6:]:
                out[...] = down2[...]

        def feed_turned(x, up, up2, bias, bias2, down, down2, x_kept, act, act2, slope, out):
            feed_turned_kernel(x, (up, up2), (bias, bias2), (down, down2), x_kept, (act, act2), slope, out)

        chip = swap(low1, "head", 2)
        turned = call(
            turn_weights, "turn_weights", [*tie([*ups, *biases, *downs], low1)],
            [((units, model), bf16)] * 2 + [((units, CLUSTER), f32)] * 2 + [((model, units), bf16)] * 2
            + [Stay(w_down.shape, bf16)] * (not layer), vmem=4 + 3 * (not layer),
        )
        if not layer:
            *turned, other_down = turned
            downs = (w_down, other_down)
        h_own, act_own, act_core, slope_own, own_term = feed(low1, f32)
        chip = tie(chip, own_term, turned)
        h_chip, act_chip, act_cross, slope_chip, far_term = call(
            feed_turned, "feed_turned", [chip, *turned],
            [Stay(wide, bf16), Stay((units, rows), bf16), ((units, rows), bf16), Stay((2 * units, rows), bf16),
             wide_low], vmem=5.5,
        )
        far = swap(far_term, "head", 2)
        away = [swap(item, "head", 1) for item in tie((h_own, act_core, h_chip, act_cross), far_term)]
        ends = [normed1, ln1_gain, ln1_bias, own_term, far, b_down, ln2_gain, ln2_bias]
        kept.append(
            (x_kept, (kv_kept, q_kept), ((out_near, raised_near), (out_far, raised_far)), (ob_near, ob_far),
             normed1_kept, w_kept, (slope_own, slope_chip))
        )
        if layer + 1 < depth:
            entry, low, normed2_kept = call(
                functools.partial(close_kernel, layer), "close", ends,
                [wide_full, wide_low, Stay((rows, model + CLUSTER), f32)], vmem=4,
            )
            kept[-1] += (normed2_kept,)
            low, away = tie((low, away))
            chip, core = swap(low, "head", 2), swap(low, "head", 1)
        else:
            result, low, sums2, d_second = call(
                functools.partial(turn_kernel, layer), "turn", ends + [out_cotangent],
                [wide_full, wide_low, ((8, model), f32), Stay(*wide_full)], vmem=4,
            )
            low, away = tie((low, away))
        h_core, act_core, h_cross, act_cross = away
        kept[-1] += ((h_own, h_core, h_chip, h_cross), (act_own, act_core, act_chip, act_cross))

    feed_sums = attend_sums = None
    grads, small = [None] * depth, [None] * depth
    pieces = heads
    for layer in reversed(range(depth)):
        x_kept, (kv_kept, q_kept), (near, far_rows), obs, normed1, w_kept, slopes, *_, h_kept, acts = kept[layer]
        above = feed_sums is not None

        def feed_back(grad, up, up2, down, down2, slope, pre, pre2, out):
            feed_back_kernel(layer, grad, (up, up2), (down, down2), slope, (pre, pre2), out)

        def feed_back_turned(grad, up, up2, down, down2, slope, pre, pre2, out):
            feed_back_turned_kernel(layer, grad, (up, up2), (down, down2), slope, (pre, pre2), out)

        chip, g_core = swap(low, "head", 2), swap(low, "head", 1)
        pre_own, pre_core, own_term = call(
            feed_back, "feed_back", [low, *ups, *downs, View(slopes[0])],
            [((rows, units), bf16)] * 2 + [wide_full], vmem=4,
        )
        chip, g_core = join((chip, g_core), [feed_sums, attend_sums] if above else [], own_term)
        g_cross = swap(chip, "head", 1)
        pre_chip, pre_cross, far_term = call(
            feed_back_turned, "feed_back_turned", [chip, *ups, *downs, View(slopes[1])],
            [((units, rows), bf16)] * 2 + [wide_low], vmem=5,
        )
        far_term, g_cross = tie((far_term, g_cross))
        far = swap(far_term, "head", 2)
        pre_core, pre_cross = [swap(item, "head", 1) for item in tie((pre_core, pre_cross), far_term)]
        g_blocks = (low, g_core, chip, g_cross)
        added = ()
        if above and attend_sums.more():
            added = advance([attend_sums], far_term)
        *parts, up_sums = call(
            functools.partial(feed_grad_kernel, orders), "feed_grad",
            [spot, *tie((pre_own, pre_core, pre_chip, pre_cross), added), *map(View, h_kept), *g_blocks,
             *map(View, acts)],
            grad_outs(model, units, order_one) + grad_outs(model, units, order_two) + [((8, units), f32)],
            vmem=9,
        )
        far = tie(far, parts)
        if above:
            parts = join(parts, [attend_sums])
        waiting = attend_sums
        feed_sums = start_halving(parts, place, orders)
        low, *d_obs, sums1, d_first = call(
            functools.partial(mix_back_kernel, layer), "mix_back",
            [View(d_second), View(normed1), View(w_kept, 4), own_term, far, ln1_gain],
            [wide_low] + [((rows, cols), bf16)] * 4 + [((8, model), f32), Stay(*wide_full)], vmem=4,
        )
        got = [d_obs[0]] + [swap(d_obs[item], "head", item) for item in (1, 2, 3)]

        def kept_part(part, start):
            out, raised = part
            raised = View(raised.reshape(heads * pair, pack), pieces)
            return [
                View(kv_kept, heads), View(out, heads), raised,
                View(q_kept[start // pair], heads),
            ]

        near_q, near_k, near_v = call(
            attend_back_near_kernel, "attend_back_near",
            kept_part(near, 0) + got[:2],
            [((pair, cols), bf16)] + [((cols, pack), f32)] * 2, vmem=4.5,
        )
        got = tie(got, near_q)
        others = [item for item in (feed_sums, waiting) if item]
        got = join(got, others)
        if any(item.more() for item in others):
            got = tie(got, advance(others))
        low = tie(low, got)
        chip, core = swap(low, "head", 2), swap(low, "head", 1)
        d_q, d_k, d_v, own_term, core_term, chip_term, cross_term, sums_qv = call(
            functools.partial(attend_back_kernel, layer), "attend_back",
            kept_part(far_rows, pair)
            + [got[2], got[3], near_q, near_k, near_v, w_query, w_key, w_value],
            [((pack, cols), bf16)] * 3 + [wide_full, wide_low, wide_full, wide_low]
            + [((8, 2 * cols), f32)], vmem=7.5,
        )
        others = [item for item in (feed_sums, waiting) if item]
        chip, core, core_term, cross_term = join((chip, core, core_term, cross_term), others)
        got_chip, got_core = swap(cross_term, "head", 1), swap(core_term, "head", 1)
        cross = swap(chip, "head", 1)
        small[layer] = [sums1, sums2, up_sums, sums_qv]
        last = ()
        if not layer:
            mine = call(
                collect_kernel, "collect", [spot] + [item for part in small for item in part],
                [((12 * depth, model), f32)], vmem=3,
            )[0]
            last = (mine, swap(mine, "head", 1))
        got_chip, got_core, last = tie((got_chip, got_core, last))
        merged = (chip_term + got_chip.astype(f32)).astype(bf16)
        if not layer:
            total = last[0] + last[1]
            last = (total, swap(total, "head", 2))
        a_blocks = (low, core, chip, cross)
        added = ()
        if any(item.more() for item in others):
            added = advance(others, merged, apart=bool(layer))
        ready = merged
        if not layer:
            ready, last = tie((merged, last))
        far = swap(ready, "head", 2)
        *parts, = call(
            functools.partial(attend_grad_kernel, orders), "attend_grad",
            [spot, View(x_kept), *tie((d_q, d_k, d_v), merged, added), *a_blocks, *map(View, obs)],
            grad_outs(model, 2 * cols, order_one) + grad_outs(model, 2 * cols, order_two), vmem=6,
        )
        if layer:
            far = land(far, [feed_sums.slots[0][0]], parts)
        if not layer and len(parts) == 4:
            longer = ((parts[0].shape[0] + 24 * depth, parts[0].shape[1]), bf16)
            parts[:2] = call(append_kernel, "append", [*parts[:2], *last], [longer] * 2, vmem=4)
        attend_sums = start_halving(parts, place, orders, last)
        grads[layer] = (feed_sums, attend_sums)
        if layer:
            low, sums2, d_second = call(
                functools.partial(open_back_kernel, layer - 1), "open_back",
                [View(kept[layer - 1][-3]), View(d_first), own_term, got_core, far, ln2_gain],
                [wide_low, ((8, model), f32), Stay(*wide_full)], vmem=4,
            )

    items = [layer[0] for layer in grads]
    while any(item.more() for item in items):
        advance(items)
    found = transfers_of(items)
    own = feed_sums.keeps[0].shape[0]
    g_up, g_down = call(
        functools.partial(finish_kernel, spots_of(items), len(found)), "finish",
        [keep for item in items for keep in item.keeps] + [item.got for item in found],
        [((depth, own, units), f32)] * 2, vmem=5,
    )
    done = join((g_up, g_down), [attend_sums])
    if attend_sums.more():
        advance([attend_sums], done)
    d_rows = call(close_back_kernel, "close_back", [View(d_first), own_term, got_core, far], [wide_full], vmem=4)[0]
    while attend_sums.more():
        advance([attend_sums], d_rows)
    items = [layer[1] for layer in grads]
    while any(item.more() for item in items):
        advance(items)
    ends = [keep for item in items for keep in item.keeps] + [item.got for item in transfers_of(items)]
    g_q, g_k, g_v, g_o, s_bq, s_bv, s_bo, s_g1, s_n1, s_bd, s_g2, s_n2, s_bu = call(
        functools.partial(assemble_kernel, spots_of(items), len(transfers_of(items)), depth), "assemble", ends,
        [((depth, own, cols), f32)] * 3 + [((depth, cols, own), f32)]
        + [((depth, model), f32)] * 8 + [((depth, groups * units), f32)], vmem=8,
    )
    return (
        result, d_rows, g_q, g_k, g_v, s_bq, s_bv, g_o, s_bo, s_g1, s_n1, g_up,
        s_bu, g_down.transpose(0, 2, 1), s_bd, s_g2, s_n2,
    )


def solution(mesh):
    split = P(("dp", "head"), None)
    column, line = P(None, None, "head"), P(None, "head", None)
    placed = (
        split, column, column, column, P(None, "head"), P(None, "head"), line, P(), P(), P(),
        column, P(None, "head"), line, P(), P(), P(),
        P("dp"), P(None, "head", "dp"), P(None, "head", "dp"), split,
    )
    by_rows, by_cols = P(None, "dp", "head"), P(None, "head", "dp")
    results = (
        split, split, by_rows, by_rows, by_rows, P(), P(), by_cols, P(), P(), P(), by_rows, P(),
        by_cols, P(), P(), P(),
    )
    return jax.shard_map(body, mesh=mesh, in_specs=placed, out_specs=results, check_vma=False)
```
